32 devices in a mesh: groups: 2 (over x), hid: 16 (over z, y, core).
Axes of the slice: x: 2, y: 2, z: 4, core: 2. Of those that a mesh axis runs over, the one named last changes fastest.
Arguments:
- tokens: bfloat16 [256, 8192], P(('groups', 'hid')), parts along dimension 0, may hold values from -6 to 6
- norm_gain: float32 [8192], replicated, may hold values from 0.1 to 1.9
- gate_weight: bfloat16 [8192, 16384], P(None, 'hid'), may hold values from -0.0625 to 0.0625
- up_weight: bfloat16 [8192, 16384], P(None, 'hid'), may hold values from -0.0625 to 0.0625
- down_weight: bfloat16 [16384, 8192], P('hid'), may hold values from -0.046875 to 0.046875
- clip_scale: float32 [16384], P('hid'), may hold values from 0.002 to 0.02
Outputs:
- mixed: bfloat16 [256, 8192], P(('groups', 'hid')), parts along dimension 0
The draws below stay inside these ranges and needn't reach their ends.
There are 2 independent parts, one for each index of `groups`. The reference program is written for one: setup_inputs(seed, part) draws one part's arguments, and reference() takes and returns one part's arrays. A program takes and returns all parts, laid end to end along the dimension named above; an argument that names none is the same for every part. Nothing has to cross between parts.
All inputs are finite; a program needn't handle non-finite values.
Results may differ from the reference program's by a relative error of at most 0.006.
Values may be sent and summed in bfloat16 or wider, within the bound.
No kernel may reach another device: no remote copies, remote signals or barrier semaphores. Data moves between devices by JAX's collectives and lax.ppermute only.
A program may use at most 128 MiB of HBM per device.

```python
import math
import jax
import jax.numpy as jnp
from jax import lax

D = 8192
FF = 16384
BLOCK = 256
TOKENS = 128


def block_scale(own_key, extent, split, smallest, top_value):
    level = 1.0
    for axis_at, blocks in split:
        draws = jax.random.uniform(jax.random.fold_in(jax.random.fold_in(own_key, 6), axis_at), (blocks,), jnp.float32, smallest / len(split), top_value / len(split))
        level = level * jnp.repeat(jnp.exp(draws), extent[axis_at] // blocks).reshape((-1,) + (1,) * (len(extent) - 1 - axis_at))
    return level


def scatter_about(rng, shape, width, reach, split=(), kind=jnp.bfloat16):
    array = jax.random.normal(rng, shape, jnp.float32) * width
    if len(split) > 0:
        array = block_scale(rng, shape, split, -0.22, 0.18) * array
    return jnp.clip(array, min=-reach, max=reach).astype(kind)


def setup_inputs(seed: int = 0, part: int = 0) -> dict:
    streams_of = jax.random.split(jax.random.key(seed), 7)
    part_splits = jax.random.split(jax.random.fold_in(streams_of[6], part), 7)
    tokens = scatter_about(part_splits[0], (TOKENS, D), 1.0, 6.0, ((0, 16),))
    norm_gain = jnp.clip(1.0 + 0.18 * jax.random.normal(streams_of[1], (D,), jnp.float32), 0.1, 1.9)
    gate_weight = scatter_about(streams_of[2], (D, FF), D ** -0.5, 0.0625, ((1, 16),))
    up_weight = scatter_about(streams_of[3], (D, FF), D ** -0.5, 0.0625, ((1, 16),))
    down_weight = scatter_about(streams_of[4], (FF, D), FF ** -0.5, 0.046875, ((0, 16),))
    clip_scale = jnp.clip(jnp.exp(math.log(0.02) - 2.30258502 * jax.random.uniform(streams_of[5], (FF,), jnp.float32) ** block_scale(streams_of[5], (FF,), ((0, 16),), -0.2, 0.2)), 0.002, 0.02)
    return dict(tokens=tokens, norm_gain=norm_gain, gate_weight=gate_weight, up_weight=up_weight, down_weight=down_weight, clip_scale=clip_scale)


def hadamard(count):
    rows = jnp.arange(count, dtype=jnp.int32)[:, None]
    cols = jnp.arange(count, dtype=jnp.int32)[None, :]
    both = rows & cols
    parity = jnp.zeros((count, count), jnp.int32)
    for place in range(max(count.bit_length(), 1)):
        parity = parity + (both >> place & 1)
    return jnp.where(parity % 2 == 0, 1.0, -1.0).astype(jnp.float32)

def reference(tokens, norm_gain, gate_weight, up_weight, down_weight, clip_scale):
    values = tokens.astype(jnp.float32)
    inverse = lax.rsqrt(lax.optimization_barrier(jnp.mean(values * values, axis=-1, keepdims=True)) + 1e-05)
    normed = (values * inverse * norm_gain).astype(jnp.bfloat16)
    gate = jnp.dot(normed, gate_weight, preferred_element_type=jnp.float32)
    up = jnp.dot(normed, up_weight, preferred_element_type=jnp.float32)
    hidden = jax.nn.silu(gate) * up
    blocks = FF // BLOCK
    shaped = hidden.reshape(TOKENS, blocks, BLOCK)
    shaped = jnp.einsum('tbc,cd->tbd', shaped, hadamard(BLOCK), precision=lax.Precision.HIGHEST)
    shaped = jnp.einsum('tbc,be->tec', shaped, hadamard(blocks), precision=lax.Precision.HIGHEST)
    rotated = shaped.reshape(TOKENS, FF) / jnp.sqrt(jnp.float32(FF))
    limit = 127.0 * clip_scale
    clipped = jnp.clip(rotated, -limit, limit).astype(jnp.bfloat16)
    result = values + jnp.dot(clipped, down_weight, preferred_element_type=jnp.float32)
    return result.astype(jnp.bfloat16)
```

```python
import functools

import jax
import jax.numpy as jnp
from jax import lax
from jax.experimental import pallas as pl
from jax.experimental.pallas import tpu as pltpu
from jax.sharding import PartitionSpec as P

BLOCK = 256
MIB = 1 << 20


def hadamard(count):
    rows = lax.broadcasted_iota(jnp.int32, (count, count), 0)
    cols = lax.broadcasted_iota(jnp.int32, (count, count), 1)
    both = rows & cols
    parity = jnp.zeros((count, count), jnp.int32)
    for place in range(max(count.bit_length(), 1)):
        parity = parity + (both >> place & 1)
    return jnp.where(parity % 2 == 0, 1.0, -1.0).astype(jnp.bfloat16)


def normalize(rows_in, norm_gain):
    values = rows_in.astype(jnp.float32)
    inverse = lax.rsqrt(jnp.mean(values * values, axis=-1, keepdims=True) + 1e-05)
    return (values * inverse * norm_gain).astype(jnp.bfloat16)


def ring_of(chips):
    return list(range(0, chips, 2)) + list(range(chips - 1, 0, -2))


def up_kernel(count, blocks, place_ref, *refs):
    parts, (gate_ref, up_ref, out_a, out_b, rows_ref, hidden_ref) = refs[:count], refs[count:]
    own = parts[0].shape[0]
    for pair in range(count // 2):
        both = [parts[2 * pair + k][...].astype(jnp.float32) for k in range(2)]
        rows_ref[2 * own * pair : 2 * own * (pair + 1), :] = jnp.concatenate(both, axis=0).astype(jnp.bfloat16)
    rows = rows_ref.shape[0]
    depth = rows_ref.shape[1]
    step = min(1024, depth)
    turn = hadamard(BLOCK)
    outs = []
    for block in range(blocks):
        lanes = slice(block * BLOCK, (block + 1) * BLOCK)

        def add(at, sums):
            along = pl.ds(pl.multiple_of(at * step, step), step)
            values = rows_ref[:, along]
            gate = sums[0] + jnp.dot(values, gate_ref[along, lanes], preferred_element_type=jnp.float32)
            up = sums[1] + jnp.dot(values, up_ref[along, lanes], preferred_element_type=jnp.float32)
            return gate, up

        zero = jnp.zeros((rows, BLOCK), jnp.float32)
        gate, up = lax.fori_loop(0, depth // step, add, (zero, zero))
        hidden = gate / (1.0 + jnp.exp(-gate)) * up
        high = hidden.astype(jnp.bfloat16)
        low = (hidden - high.astype(jnp.float32)).astype(jnp.bfloat16)
        turned = jnp.dot(high, turn, preferred_element_type=jnp.float32) + jnp.dot(
            low, turn, preferred_element_type=jnp.float32
        )
        for part in range(count):
            spot = pl.multiple_of(place_ref[part] * own, own)
            hidden_ref[pl.ds(spot, own), lanes] = turned[part * own : (part + 1) * own]
    half = out_a.shape[1]
    out_a[...] = hidden_ref[:, :half].astype(jnp.bfloat16)
    out_b[...] = hidden_ref[:, half:].astype(jnp.bfloat16)


def up_project(place, parts, gate_weight, up_weight):
    count, own = len(parts), parts[0].shape[0]
    depth, width = gate_weight.shape
    rows = count * own
    half = jax.ShapeDtypeStruct((rows, width // 2), jnp.bfloat16)
    vmem = pl.BlockSpec(memory_space=pltpu.VMEM)
    return pl.pallas_call(
        functools.partial(up_kernel, count, width // BLOCK),
        out_shape=(half, half),
        in_specs=[pl.BlockSpec(memory_space=pltpu.SMEM)] + [vmem] * (count + 2),
        out_specs=(vmem, vmem),
        scratch_shapes=[pltpu.VMEM((rows, depth), jnp.bfloat16), pltpu.VMEM((rows, width), jnp.float32)],
        compiler_params=pltpu.CompilerParams(vmem_limit_bytes=20 * MIB),
        cost_estimate=pl.CostEstimate(
            flops=4 * rows * depth * width, bytes_accessed=4 * depth * width, transcendentals=rows * width
        ),
        name="up_project",
    )(place, *parts, gate_weight, up_weight)


def down_kernel(blocks, chips, scale, place_ref, first_ref, a_ref, b_ref, clip_ref, weight_ref, out_ref, rows_ref, mixed_ref):
    half = a_ref.shape[1]
    rows_ref[:, :half] = a_ref[...].astype(jnp.float32)
    rows_ref[:, half:] = b_ref[...].astype(jnp.float32)
    parts = [rows_ref[:, b * BLOCK : (b + 1) * BLOCK] for b in range(blocks)]
    span = 1
    while span < blocks:
        parts = [
            parts[b] + parts[b ^ span] if b & span == 0 else parts[b ^ span] - parts[b] for b in range(blocks)
        ]
        span *= 2
    for b in range(blocks):
        lanes = slice(b * BLOCK, (b + 1) * BLOCK)
        limit = 127.0 * clip_ref[:, lanes]
        rows_ref[:, lanes] = jnp.clip(parts[b] * scale, -limit, limit)
    rows = rows_ref.shape[0]
    each = rows // chips
    for chip in range(chips):
        spot = pl.multiple_of(place_ref[chip] * each, each)
        mixed_ref[chip * each : (chip + 1) * each, :] = rows_ref[pl.ds(spot, each), :].astype(jnp.bfloat16)
    wide = out_ref.shape[1]
    step = min(512, wide)

    def column(at, carry):
        lanes = pl.ds(pl.multiple_of(first_ref[0] * wide + at * step, step), step)
        product = jnp.dot(mixed_ref[...], weight_ref[:, lanes], preferred_element_type=jnp.float32)
        out_ref[:, pl.ds(pl.multiple_of(at * step, step), step)] = product.astype(jnp.bfloat16)
        return carry

    lax.fori_loop(0, wide // step, column, 0)


def down_project(place, first, a, b, clip_scale, weight, chips, total):
    rows = a.shape[0]
    width, depth = weight.shape
    vmem = pl.BlockSpec(memory_space=pltpu.VMEM)
    smem = pl.BlockSpec(memory_space=pltpu.SMEM)
    return pl.pallas_call(
        functools.partial(down_kernel, width // BLOCK, chips, total**-0.5),
        out_shape=jax.ShapeDtypeStruct((rows, depth // 2), jnp.bfloat16),
        in_specs=[smem, smem, vmem, vmem, vmem, vmem],
        out_specs=vmem,
        scratch_shapes=[pltpu.VMEM((rows, width), jnp.float32), pltpu.VMEM((rows, width), jnp.bfloat16)],
        compiler_params=pltpu.CompilerParams(vmem_limit_bytes=12 * MIB),
        cost_estimate=pl.CostEstimate(flops=rows * depth * width, bytes_accessed=depth * width, transcendentals=0),
        name="down_project",
    )(place, first, a, b, clip_scale, weight)


def shards(count, tokens, norm_gain, gate_weight, up_weight, down_weight, clip_scale):
    chips = count // 2
    order = ring_of(chips)
    me = lax.axis_index("hid")
    chip, core = me // 2, me % 2
    ring = jnp.array(order, jnp.int32)
    position = jnp.array([order.index(c) for c in range(chips)], jnp.int32)[chip]
    steps = chips // 2

    def hop(value, shift_even, shift_odd):
        pairs = []
        for at, c in enumerate(order):
            pairs.append((2 * c, 2 * order[(at + shift_even) % chips]))
            pairs.append((2 * c + 1, 2 * order[(at + shift_odd) % chips] + 1))
        return lax.ppermute(value, "hid", pairs)

    def right(value):
        return hop(value, 1, 1)

    def left(value):
        return hop(value, -1, -1)

    def cross(value, mask=1):
        return lax.ppermute(value, "hid", [(d, d ^ mask) for d in range(count)])

    normed = normalize(tokens, norm_gain)
    mine, shifts = [normed], [0]
    ahead = behind = normed
    for step in range(1, steps):
        ahead, behind = right(ahead), left(behind)
        mine += [ahead, behind]
        shifts += [-step, step]
    mine.append(hop(jnp.where(core == 0, ahead, behind), 1, -1))
    shifts.append(steps)
    parts = [block for own in mine for block in (own, cross(own))]
    chip_at = ring[(position + jnp.array(shifts, jnp.int32)) % chips]
    place = jnp.stack([2 * chip_at + core, 2 * chip_at + 1 - core], axis=1).reshape(-1).astype(jnp.int32)

    half_a, half_b = up_project(place, parts, gate_weight, up_weight)

    def butterfly(value, mask):
        sign = jnp.where(me & mask == 0, 1.0, -1.0).astype(jnp.float32)
        other = cross(value, mask)
        return (other.astype(jnp.float32) + sign * value.astype(jnp.float32)).astype(jnp.bfloat16)

    masks = [1 << bit for bit in range(count.bit_length() - 1)]
    orders = [masks[-1:] + masks[:-1], masks]
    for stage in range(len(masks)):
        half_a = butterfly(half_a, orders[0][stage])
        half_b = butterfly(half_b, orders[1][stage])

    turn = list(range(chips))
    places = ring[(position + jnp.array(turn, jnp.int32)) % chips]
    total = count * gate_weight.shape[1]
    limits = clip_scale.reshape(1, -1)
    theirs = down_project(places, (1 - core).reshape(1), half_a, half_b, limits, down_weight, chips, total)
    own = down_project(places, core.reshape(1), half_a, half_b, limits, down_weight, chips, total)
    arrived = cross(theirs)
    rows = own.shape[0] // chips

    def chunk(away):
        at = away % chips
        return own[at * rows : (at + 1) * rows].astype(jnp.float32) + arrived[at * rows : (at + 1) * rows].astype(
            jnp.float32
        )

    far = hop(chunk(steps).astype(jnp.bfloat16), 1, -1).astype(jnp.float32)
    zero = jnp.zeros_like(far)
    ahead = jnp.where(core == 0, far, zero)
    behind = jnp.where(core == 0, zero, far)
    for away in range(steps - 1, 0, -1):
        ahead = right((ahead + chunk(away)).astype(jnp.bfloat16)).astype(jnp.float32)
        behind = left((behind + chunk(-away)).astype(jnp.bfloat16)).astype(jnp.float32)
    summed = ahead + behind + chunk(0)
    part = rows // 2
    keep = lax.dynamic_slice_in_dim(summed, core * part, part, 0)
    give = lax.dynamic_slice_in_dim(summed, (1 - core) * part, part, 0)
    take = cross(give.astype(jnp.bfloat16)).astype(jnp.float32)
    low = jnp.where(core == 0, keep, take)
    high = jnp.where(core == 0, take, keep)
    return (tokens.astype(jnp.float32) + jnp.concatenate([low, high], axis=1)).astype(jnp.bfloat16)


def solution(mesh):
    in_specs = (
        P(("groups", "hid"), None),
        P(),
        P(None, "hid"),
        P(None, "hid"),
        P("hid", None),
        P("hid"),
    )
    out_specs = P(("groups", "hid"), None)
    body = functools.partial(shards, mesh.shape["hid"])
    return jax.shard_map(body, mesh=mesh, in_specs=in_specs, out_specs=out_specs, check_vma=False)
```

```python
import functools

import jax
import jax.numpy as jnp
from jax import lax
from jax.experimental import pallas as pl
from jax.experimental.pallas import tpu as pltpu
from jax.sharding import PartitionSpec as P

BLOCK = 256
MIB = 1 << 20


def hadamard(count):
    rows = lax.broadcasted_iota(jnp.int32, (count, count), 0)
    cols = lax.broadcasted_iota(jnp.int32, (count, count), 1)
    both = rows & cols
    parity = jnp.zeros((count, count), jnp.int32)
    for place in range(max(count.bit_length(), 1)):
        parity = parity + (both >> place & 1)
    return jnp.where(parity % 2 == 0, 1.0, -1.0).astype(jnp.bfloat16)


def normalize_kernel(rows_ref, gain_ref, out_ref):
    values = rows_ref[...].astype(jnp.float32)
    inverse = lax.rsqrt(jnp.mean(values * values, axis=-1, keepdims=True) + 1e-05)
    out_ref[...] = (values * inverse * gain_ref[...]).astype(jnp.bfloat16)


def normalize(rows_in, norm_gain):
    vmem = pl.BlockSpec(memory_space=pltpu.VMEM)
    return pl.pallas_call(
        normalize_kernel,
        out_shape=jax.ShapeDtypeStruct(rows_in.shape, jnp.bfloat16),
        in_specs=[vmem, vmem],
        out_specs=vmem,
        compiler_params=pltpu.CompilerParams(vmem_limit_bytes=4 * MIB),
        cost_estimate=pl.CostEstimate(flops=8 * rows_in.size, bytes_accessed=4 * rows_in.size, transcendentals=0),
        name="normalize",
    )(rows_in, norm_gain.reshape(1, -1))


def ring_of(chips):
    return list(range(0, chips, 2)) + list(range(chips - 1, 0, -2))


def ring_place(chip, shift, chips):
    spot = jnp.where(chip % 2 == 0, chip // 2, chips - 1 - (chip - 1) // 2)
    spot = (spot + shift) % chips
    return jnp.where(spot < (chips + 1) // 2, 2 * spot, 2 * (chips - spot) - 1)


def load_kernel(flip, splits, me_ref, weight_ref, after_ref, out_ref, sems):
    rows, cols = out_ref.shape
    wide = weight_ref.shape[1]
    start = splits[1] * cols
    if flip is not None:
        side = me_ref[0] % 2
        side = 1 - side if flip else side
        start = start + side * (wide // 2)
        start = pl.multiple_of(start, cols)
    each = rows // splits[0]
    copies = [
        pltpu.make_async_copy(
            weight_ref.at[pl.ds(part * each, each), pl.ds(start, cols)],
            out_ref.at[pl.ds(part * each, each), :],
            sems.at[part],
        )
        for part in range(splits[0])
    ]
    for copy in copies:
        copy.start()
    for copy in copies:
        copy.wait()


def load(me, weight, after, cols, at, flip=None):
    rows = weight.shape[0]
    hbm = pl.BlockSpec(memory_space=pltpu.HBM)
    return pl.pallas_call(
        functools.partial(load_kernel, flip, (8, at)),
        out_shape=jax.ShapeDtypeStruct((rows, cols), weight.dtype),
        in_specs=[pl.BlockSpec(memory_space=pltpu.SMEM), hbm, hbm],
        out_specs=pl.BlockSpec(memory_space=pltpu.VMEM),
        scratch_shapes=[pltpu.SemaphoreType.DMA((8,))],
        compiler_params=pltpu.CompilerParams(vmem_limit_bytes=1 * MIB),
        cost_estimate=pl.CostEstimate(flops=0, bytes_accessed=4 * rows * cols, transcendentals=0),
        name="load",
    )(me, pltpu.with_memory_space_constraint(weight, pltpu.HBM), after)


def up_kernel(count, shifts, me_ref, *refs):
    chip, core = me_ref[0] // 2, me_ref[0] % 2
    spots = []
    for shift in shifts:
        there = 2 * ring_place(chip, shift, count // 2)
        spots += [there + core, there + 1 - core]
    parts, (out_a, out_b, rows_ref, hidden_ref) = refs[:count], refs[-4:]
    gates, ups = refs[count:-4:2], refs[count + 1 : -4 : 2]
    own = parts[0].shape[0]
    for pair in range(count // 2):
        both = [parts[2 * pair + k][...].astype(jnp.float32) for k in range(2)]
        rows_ref[2 * own * pair : 2 * own * (pair + 1), :] = jnp.concatenate(both, axis=0).astype(jnp.bfloat16)
    turn = hadamard(BLOCK)
    values = rows_ref[...]
    for block in range(len(gates)):
        gate = jnp.dot(values, gates[block][...], preferred_element_type=jnp.float32)
        up = jnp.dot(values, ups[block][...], preferred_element_type=jnp.float32)
        hidden = gate / (1.0 + jnp.exp(-gate)) * up
        high = hidden.astype(jnp.bfloat16)
        low = (hidden - high.astype(jnp.float32)).astype(jnp.bfloat16)
        turned = jnp.dot(high, turn, preferred_element_type=jnp.float32) + jnp.dot(
            low, turn, preferred_element_type=jnp.float32
        )
        lanes = slice(block * BLOCK, (block + 1) * BLOCK)
        for part in range(count):
            spot = pl.multiple_of(spots[part] * own, own)
            hidden_ref[pl.ds(spot, own), lanes] = turned[part * own : (part + 1) * own]
    half = out_a.shape[1]
    out_a[...] = hidden_ref[:, :half].astype(jnp.bfloat16)
    out_b[...] = hidden_ref[:, half:].astype(jnp.bfloat16)


def up_project(me, shifts, parts, weights):
    count, own = len(parts), parts[0].shape[0]
    depth = weights[0].shape[0]
    width = BLOCK * len(weights) // 2
    rows = count * own
    half = jax.ShapeDtypeStruct((rows, width // 2), jnp.bfloat16)
    vmem = pl.BlockSpec(memory_space=pltpu.VMEM)
    return pl.pallas_call(
        functools.partial(up_kernel, count, shifts),
        out_shape=(half, half),
        in_specs=[pl.BlockSpec(memory_space=pltpu.SMEM)] + [vmem] * (count + len(weights)),
        out_specs=(vmem, vmem),
        scratch_shapes=[pltpu.VMEM((rows, depth), jnp.bfloat16), pltpu.VMEM((rows, width), jnp.float32)],
        compiler_params=pltpu.CompilerParams(vmem_limit_bytes=12 * MIB),
        cost_estimate=pl.CostEstimate(flops=4 * rows * depth * width, bytes_accessed=0, transcendentals=rows * width),
        name="up_project",
    )(me, *parts, *weights)


def down_kernel(blocks, chips, scale, me_ref, a_ref, b_ref, clip_ref, *refs):
    weights, (out_ref, rows_ref, mixed_ref) = refs[:-3], refs[-3:]
    half = a_ref.shape[1]
    rows_ref[:, :half] = a_ref[...].astype(jnp.float32)
    rows_ref[:, half:] = b_ref[...].astype(jnp.float32)
    parts = [rows_ref[:, b * BLOCK : (b + 1) * BLOCK] for b in range(blocks)]
    span = 1
    while span < blocks:
        parts = [
            parts[b] + parts[b ^ span] if b & span == 0 else parts[b ^ span] - parts[b] for b in range(blocks)
        ]
        span *= 2
    for b in range(blocks):
        lanes = slice(b * BLOCK, (b + 1) * BLOCK)
        limit = 127.0 * clip_ref[:, lanes]
        rows_ref[:, lanes] = jnp.clip(parts[b] * scale, -limit, limit)
    rows = rows_ref.shape[0]
    each = rows // chips
    for chip in range(chips):
        spot = pl.multiple_of(ring_place(me_ref[0] // 2, chip, chips) * each, each)
        mixed_ref[chip * each : (chip + 1) * each, :] = rows_ref[pl.ds(spot, each), :].astype(jnp.bfloat16)
    step = weights[0].shape[1]
    for at, weight_ref in enumerate(weights):
        product = jnp.dot(mixed_ref[...], weight_ref[...], preferred_element_type=jnp.float32)
        out_ref[:, at * step : (at + 1) * step] = product.astype(jnp.bfloat16)


def down_project(me, a, b, clip_scale, weights, chips, total):
    rows = a.shape[0]
    width = 2 * a.shape[1]
    depth = len(weights) * weights[0].shape[1]
    vmem = pl.BlockSpec(memory_space=pltpu.VMEM)
    smem = pl.BlockSpec(memory_space=pltpu.SMEM)
    return pl.pallas_call(
        functools.partial(down_kernel, width // BLOCK, chips, total**-0.5),
        out_shape=jax.ShapeDtypeStruct((rows, depth), jnp.bfloat16),
        in_specs=[smem, vmem, vmem, vmem] + [vmem] * len(weights),
        out_specs=vmem,
        scratch_shapes=[pltpu.VMEM((rows, width), jnp.float32), pltpu.VMEM((rows, width), jnp.bfloat16)],
        compiler_params=pltpu.CompilerParams(vmem_limit_bytes=8 * MIB),
        cost_estimate=pl.CostEstimate(flops=2 * rows * depth * width, bytes_accessed=0, transcendentals=0),
        name="down_project",
    )(me, a, b, clip_scale, *weights)


def shards(count, tokens, norm_gain, gate_weight, up_weight, down_weight, clip_scale):
    chips = count // 2
    order = ring_of(chips)
    me = lax.axis_index("hid")
    core = me & 1
    where = me.astype(jnp.int32).reshape(1)
    steps = chips // 2

    def hop(value, shift_even, shift_odd):
        pairs = []
        for at, c in enumerate(order):
            pairs.append((2 * c, 2 * order[(at + shift_even) % chips]))
            pairs.append((2 * c + 1, 2 * order[(at + shift_odd) % chips] + 1))
        return lax.ppermute(value, "hid", pairs)

    def right(value):
        return hop(value, 1, 1)

    def left(value):
        return hop(value, -1, -1)

    def cross(value, mask=1):
        return lax.ppermute(value, "hid", [(d, d ^ mask) for d in range(count)])

    normed = normalize(tokens, norm_gain)
    mine, shifts = [normed], [0]
    ahead = behind = normed
    for step in range(1, steps):
        ahead, behind = right(ahead), left(behind)
        mine += [ahead, behind]
        shifts += [-step, step]
    mine.append(hop(jnp.where(core == 0, ahead, behind), 1, -1))
    shifts.append(steps)
    parts = [block for own in mine for block in (own, cross(own))]
    blocks = gate_weight.shape[1] // BLOCK
    weights = []
    for block in range(blocks):
        for weight in (gate_weight, up_weight):
            weights.append(load(where, weight, normed, BLOCK, block))
    half_a, half_b = up_project(where, shifts, parts, weights)
    wide = down_weight.shape[1] // 4
    theirs_weight, own_weight = [
        [load(where, down_weight, half_a, wide, at, flip) for at in range(2)] for flip in (True, False)
    ]

    def butterfly(value, mask):
        sign = jnp.where(me & mask == 0, 1.0, -1.0).astype(jnp.float32)
        other = cross(value, mask)
        return (other.astype(jnp.float32) + sign * value.astype(jnp.float32)).astype(jnp.bfloat16)

    masks = [1 << bit for bit in range(count.bit_length() - 1)]
    orders = [masks[-1:] + masks[:-1], masks]
    for stage in range(len(masks)):
        half_a = butterfly(half_a, orders[0][stage])
        half_b = butterfly(half_b, orders[1][stage])

    total = count * gate_weight.shape[1]
    limits = clip_scale.reshape(1, -1)
    theirs = down_project(where, half_a, half_b, limits, theirs_weight, chips, total)
    own = down_project(where, half_a, half_b, limits, own_weight, chips, total)
    arrived = cross(theirs)
    rows = own.shape[0] // chips

    def chunk(away):
        at = away % chips
        return own[at * rows : (at + 1) * rows].astype(jnp.float32) + arrived[at * rows : (at + 1) * rows].astype(
            jnp.float32
        )

    far = hop(chunk(steps).astype(jnp.bfloat16), 1, -1).astype(jnp.float32)
    zero = jnp.zeros_like(far)
    ahead = jnp.where(core == 0, far, zero)
    behind = jnp.where(core == 0, zero, far)
    for away in range(steps - 1, 0, -1):
        ahead = right((ahead + chunk(away)).astype(jnp.bfloat16)).astype(jnp.float32)
        behind = left((behind + chunk(-away)).astype(jnp.bfloat16)).astype(jnp.float32)
    summed = ahead + behind + chunk(0)
    part = rows // 2
    keep = lax.dynamic_slice_in_dim(summed, core * part, part, 0)
    give = lax.dynamic_slice_in_dim(summed, (1 - core) * part, part, 0)
    take = cross(give.astype(jnp.bfloat16)).astype(jnp.float32)
    low = jnp.where(core == 0, keep, take)
    high = jnp.where(core == 0, take, keep)
    return (tokens.astype(jnp.float32) + jnp.concatenate([low, high], axis=1)).astype(jnp.bfloat16)


def solution(mesh):
    in_specs = (
        P(("groups", "hid"), None),
        P(),
        P(None, "hid"),
        P(None, "hid"),
        P("hid", None),
        P("hid"),
    )
    out_specs = P(("groups", "hid"), None)
    body = functools.partial(shards, mesh.shape["hid"])
    return jax.shard_map(body, mesh=mesh, in_specs=in_specs, out_specs=out_specs, check_vma=False)
```

```python
import functools

import jax
import jax.numpy as jnp
from jax import lax
from jax.experimental import pallas as pl
from jax.experimental.pallas import tpu as pltpu
from jax.sharding import PartitionSpec as P

BLOCK = 256
MIB = 1 << 20


def hadamard(count):
    rows = lax.broadcasted_iota(jnp.int32, (count, count), 0)
    cols = lax.broadcasted_iota(jnp.int32, (count, count), 1)
    both = rows & cols
    parity = jnp.zeros((count, count), jnp.int32)
    for place in range(max(count.bit_length(), 1)):
        parity = parity + (both >> place & 1)
    return jnp.where(parity % 2 == 0, 1.0, -1.0).astype(jnp.bfloat16)


def normalize_kernel(rows_ref, gain_ref, out_ref):
    values = rows_ref[...].astype(jnp.float32)
    inverse = lax.rsqrt(jnp.mean(values * values, axis=-1, keepdims=True) + 1e-05)
    out_ref[...] = (values * inverse * gain_ref[...]).astype(jnp.bfloat16)


def normalize(rows_in, norm_gain):
    vmem = pl.BlockSpec(memory_space=pltpu.VMEM)
    return pl.pallas_call(
        normalize_kernel,
        out_shape=jax.ShapeDtypeStruct(rows_in.shape, jnp.bfloat16),
        in_specs=[vmem, vmem],
        out_specs=vmem,
        compiler_params=pltpu.CompilerParams(vmem_limit_bytes=4 * MIB),
        cost_estimate=pl.CostEstimate(flops=8 * rows_in.size, bytes_accessed=4 * rows_in.size, transcendentals=0),
        name="normalize",
    )(rows_in, norm_gain.reshape(1, -1))


def ring_of(chips):
    return list(range(0, chips, 2)) + list(range(chips - 1, 0, -2))


def ring_place(chip, shift, chips):
    spot = jnp.where(chip % 2 == 0, chip // 2, chips - 1 - (chip - 1) // 2)
    spot = (spot + shift) % chips
    return jnp.where(spot < (chips + 1) // 2, 2 * spot, 2 * (chips - spot) - 1)


def load_kernel(flip, at, weight_ref, after_ref, out_ref, sem):
    cols = out_ref.shape[1]
    wide = weight_ref.shape[1]
    start = at * cols
    if flip is not None:
        side = lax.axis_index("hid") % 2
        side = 1 - side if flip else side
        start = start + side * (wide // 2)
        start = pl.multiple_of(start, cols)
    copy = pltpu.make_async_copy(weight_ref.at[:, pl.ds(start, cols)], out_ref, sem)
    copy.start()
    copy.wait()


def load(weight, after, cols, at, flip=None):
    rows = weight.shape[0]
    hbm = pl.BlockSpec(memory_space=pltpu.HBM)
    return pl.pallas_call(
        functools.partial(load_kernel, flip, at),
        out_shape=jax.ShapeDtypeStruct((rows, cols), weight.dtype),
        in_specs=[hbm, hbm],
        out_specs=pl.BlockSpec(memory_space=pltpu.VMEM),
        scratch_shapes=[pltpu.SemaphoreType.DMA],
        compiler_params=pltpu.CompilerParams(vmem_limit_bytes=1 * MIB),
        cost_estimate=pl.CostEstimate(flops=0, bytes_accessed=2 * rows * cols, transcendentals=0),
        name="load",
    )(pltpu.with_memory_space_constraint(weight, pltpu.HBM), after)


def up_kernel(count, shifts, *refs):
    me = lax.axis_index("hid")
    chip, core = me // 2, me % 2
    spots = []
    for shift in shifts:
        there = 2 * ring_place(chip, shift, count // 2)
        spots += [there + core, there + 1 - core]
    parts, (out_a, out_b, rows_ref, hidden_ref) = refs[:count], refs[-4:]
    gates, ups = refs[count:-4:2], refs[count + 1 : -4 : 2]
    own = parts[0].shape[0]
    for pair in range(count // 2):
        both = [parts[2 * pair + k][...].astype(jnp.float32) for k in range(2)]
        rows_ref[2 * own * pair : 2 * own * (pair + 1), :] = jnp.concatenate(both, axis=0).astype(jnp.bfloat16)
    turn = hadamard(BLOCK)
    values = rows_ref[...]
    wide = gates[0].shape[1]
    for at in range(len(gates)):
        gate = jnp.dot(values, gates[at][...], preferred_element_type=jnp.float32)
        up = jnp.dot(values, ups[at][...], preferred_element_type=jnp.float32)
        hidden = gate / (1.0 + jnp.exp(-gate)) * up
        high = hidden.astype(jnp.bfloat16)
        low = (hidden - high.astype(jnp.float32)).astype(jnp.bfloat16)
        for block in range(wide // BLOCK):
            inner = slice(block * BLOCK, (block + 1) * BLOCK)
            outer = slice(at * wide + block * BLOCK, at * wide + (block + 1) * BLOCK)
            turned = jnp.dot(high[:, inner], turn, preferred_element_type=jnp.float32) + jnp.dot(
                low[:, inner], turn, preferred_element_type=jnp.float32
            )
            for part in range(count):
                spot = pl.multiple_of(spots[part] * own, own)
                hidden_ref[pl.ds(spot, own), outer] = turned[part * own : (part + 1) * own]
    half = out_a.shape[1]
    out_a[...] = hidden_ref[:, :half].astype(jnp.bfloat16)
    out_b[...] = hidden_ref[:, half:].astype(jnp.bfloat16)


def up_project(shifts, parts, weights):
    count, own = len(parts), parts[0].shape[0]
    depth = weights[0].shape[0]
    width = weights[0].shape[1] * len(weights) // 2
    rows = count * own
    half = jax.ShapeDtypeStruct((rows, width // 2), jnp.bfloat16)
    vmem = pl.BlockSpec(memory_space=pltpu.VMEM)
    return pl.pallas_call(
        functools.partial(up_kernel, count, shifts),
        out_shape=(half, half),
        in_specs=[vmem] * (count + len(weights)),
        out_specs=(vmem, vmem),
        scratch_shapes=[pltpu.VMEM((rows, depth), jnp.bfloat16), pltpu.VMEM((rows, width), jnp.float32)],
        compiler_params=pltpu.CompilerParams(vmem_limit_bytes=12 * MIB),
        cost_estimate=pl.CostEstimate(flops=4 * rows * depth * width, bytes_accessed=0, transcendentals=rows * width),
        name="up_project",
    )(*parts, *weights)


def down_kernel(blocks, chips, scale, a_ref, b_ref, clip_ref, *refs):
    weights, (out_ref, rows_ref, mixed_ref) = refs[:-3], refs[-3:]
    half = a_ref.shape[1]
    rows_ref[:, :half] = a_ref[...].astype(jnp.float32)
    rows_ref[:, half:] = b_ref[...].astype(jnp.float32)
    parts = [rows_ref[:, b * BLOCK : (b + 1) * BLOCK] for b in range(blocks)]
    span = 1
    while span < blocks:
        parts = [
            parts[b] + parts[b ^ span] if b & span == 0 else parts[b ^ span] - parts[b] for b in range(blocks)
        ]
        span *= 2
    for b in range(blocks):
        lanes = slice(b * BLOCK, (b + 1) * BLOCK)
        limit = 127.0 * clip_ref[:, lanes]
        rows_ref[:, lanes] = jnp.clip(parts[b] * scale, -limit, limit)
    rows = rows_ref.shape[0]
    each = rows // chips
    me = lax.axis_index("hid")
    for chip in range(chips):
        spot = pl.multiple_of(ring_place(me // 2, chip, chips) * each, each)
        mixed_ref[chip * each : (chip + 1) * each, :] = rows_ref[pl.ds(spot, each), :].astype(jnp.bfloat16)
    step = weights[0].shape[1]
    for at, weight_ref in enumerate(weights):
        product = jnp.dot(mixed_ref[...], weight_ref[...], preferred_element_type=jnp.float32)
        out_ref[:, at * step : (at + 1) * step] = product.astype(jnp.bfloat16)


def down_project(a, b, clip_scale, weights, chips, total):
    rows = a.shape[0]
    width = 2 * a.shape[1]
    depth = len(weights) * weights[0].shape[1]
    vmem = pl.BlockSpec(memory_space=pltpu.VMEM)
    return pl.pallas_call(
        functools.partial(down_kernel, width // BLOCK, chips, total**-0.5),
        out_shape=jax.ShapeDtypeStruct((rows, depth), jnp.bfloat16),
        in_specs=[vmem, vmem, vmem] + [vmem] * len(weights),
        out_specs=vmem,
        scratch_shapes=[pltpu.VMEM((rows, width), jnp.float32), pltpu.VMEM((rows, width), jnp.bfloat16)],
        compiler_params=pltpu.CompilerParams(vmem_limit_bytes=8 * MIB),
        cost_estimate=pl.CostEstimate(flops=2 * rows * depth * width, bytes_accessed=0, transcendentals=0),
        name="down_project",
    )(a, b, clip_scale, *weights)


def pick_kernel(even_ref, odd_ref, out_ref):
    core = lax.axis_index("hid") % 2

    @pl.when(core == 0)
    def _():
        out_ref[...] = even_ref[...]

    @pl.when(core != 0)
    def _():
        out_ref[...] = odd_ref[...]


def turn_kernel(mask, value_ref, other_ref, out_ref):
    sign = jnp.where(lax.axis_index("hid") & mask == 0, 1.0, -1.0).astype(jnp.float32)
    out_ref[...] = (other_ref[...].astype(jnp.float32) + sign * value_ref[...].astype(jnp.float32)).astype(jnp.bfloat16)


def both(body, first, second, name):
    vmem = pl.BlockSpec(memory_space=pltpu.VMEM)
    return pl.pallas_call(
        body,
        out_shape=jax.ShapeDtypeStruct(first.shape, first.dtype),
        in_specs=[vmem, vmem],
        out_specs=vmem,
        compiler_params=pltpu.CompilerParams(vmem_limit_bytes=2 * MIB),
        cost_estimate=pl.CostEstimate(flops=2 * first.size, bytes_accessed=0, transcendentals=0),
        name=name,
    )(first, second)


def chunk(away, chips, own_ref, arrived_ref):
    rows = own_ref.shape[0] // chips
    at = slice(away % chips * rows, (away % chips + 1) * rows)
    return own_ref[at, :].astype(jnp.float32) + arrived_ref[at, :].astype(jnp.float32)


def far_kernel(away, chips, own_ref, arrived_ref, out_ref):
    out_ref[...] = chunk(away, chips, own_ref, arrived_ref).astype(jnp.bfloat16)


def split_kernel(away, chips, far_ref, own_ref, arrived_ref, ahead_ref, behind_ref):
    ahead = chunk(away, chips, own_ref, arrived_ref)
    behind = chunk(-away, chips, own_ref, arrived_ref)
    core = lax.axis_index("hid") % 2
    far = far_ref[...].astype(jnp.float32)
    ahead_ref[...] = (ahead + jnp.where(core == 0, far, 0.0)).astype(jnp.bfloat16)
    behind_ref[...] = (behind + jnp.where(core == 0, 0.0, far)).astype(jnp.bfloat16)


def relay_kernel(away, chips, ahead_in, behind_in, own_ref, arrived_ref, ahead_ref, behind_ref):
    ahead = chunk(away, chips, own_ref, arrived_ref) + ahead_in[...].astype(jnp.float32)
    behind = chunk(-away, chips, own_ref, arrived_ref) + behind_in[...].astype(jnp.float32)
    ahead_ref[...] = ahead.astype(jnp.bfloat16)
    behind_ref[...] = behind.astype(jnp.bfloat16)


def last_kernel(chips, ahead_in, behind_in, own_ref, arrived_ref, keep_ref, give_ref, sum_ref):
    part = keep_ref.shape[0]
    core = lax.axis_index("hid") % 2
    sum_ref[...] = (
        chunk(0, chips, own_ref, arrived_ref) + ahead_in[...].astype(jnp.float32) + behind_in[...].astype(jnp.float32)
    )
    keep_ref[...] = sum_ref[pl.ds(pl.multiple_of(core * part, part), part), :]
    give_ref[...] = sum_ref[pl.ds(pl.multiple_of((1 - core) * part, part), part), :].astype(jnp.bfloat16)


def mix_kernel(tokens_ref, keep_ref, take_ref, out_ref):
    wide = keep_ref.shape[1]
    keep, take = keep_ref[...], take_ref[...].astype(jnp.float32)
    first = lax.axis_index("hid") % 2 == 0
    low, high = jnp.where(first, keep, take), jnp.where(first, take, keep)
    out_ref[:, :wide] = (tokens_ref[:, :wide].astype(jnp.float32) + low).astype(jnp.bfloat16)
    out_ref[:, wide:] = (tokens_ref[:, wide:].astype(jnp.float32) + high).astype(jnp.bfloat16)


def small(body, outs, operands, name, scratch=()):
    vmem = pl.BlockSpec(memory_space=pltpu.VMEM)
    return pl.pallas_call(
        body,
        out_shape=outs,
        in_specs=[vmem] * len(operands),
        out_specs=jax.tree.map(lambda _: vmem, outs),
        scratch_shapes=scratch,
        compiler_params=pltpu.CompilerParams(vmem_limit_bytes=4 * MIB),
        cost_estimate=pl.CostEstimate(flops=2 * operands[0].size, bytes_accessed=0, transcendentals=0),
        name=name,
    )(*operands)


def shards(count, tokens, norm_gain, gate_weight, up_weight, down_weight, clip_scale):
    chips = count // 2
    order = ring_of(chips)
    steps = chips // 2

    def hop(value, shift_even, shift_odd):
        pairs = []
        for at, c in enumerate(order):
            pairs.append((2 * c, 2 * order[(at + shift_even) % chips]))
            pairs.append((2 * c + 1, 2 * order[(at + shift_odd) % chips] + 1))
        return lax.ppermute(value, "hid", pairs)

    def right(value):
        return hop(value, 1, 1)

    def left(value):
        return hop(value, -1, -1)

    def cross(value, mask=1):
        return lax.ppermute(value, "hid", [(d, d ^ mask) for d in range(count)])

    normed = normalize(tokens, norm_gain)
    width = gate_weight.shape[1]
    wide = max(BLOCK, width // 2)
    wanted = [(weight, at) for at in range(width // wide) for weight in (gate_weight, up_weight)]
    weights = []

    def beside(after, *arrived):
        if len(weights) == len(wanted):
            return arrived
        weight, at = wanted[len(weights)]
        arrived = lax.optimization_barrier((load(weight, after, wide, at), *arrived))
        weights.append(arrived[0])
        return arrived[1:]

    mine, shifts = [normed], [0]
    ahead = behind = normed
    for step in range(1, steps):
        ahead, behind = beside(ahead, right(ahead), left(behind))
        mine += [ahead, behind]
        shifts += [-step, step]
    (far,) = beside(ahead, hop(both(pick_kernel, ahead, behind, "pick"), 1, -1))
    mine.append(far)
    shifts.append(steps)
    while len(weights) < len(wanted):
        (normed,) = beside(normed, normed)
    parts = [block for own in mine for block in (own, cross(own))]
    half_a, half_b = up_project(shifts, parts, weights)
    wide = down_weight.shape[1] // 2
    def butterfly(value, mask):
        return both(functools.partial(turn_kernel, mask), value, cross(value, mask), "turn")

    masks = [1 << bit for bit in range(count.bit_length() - 1)]
    orders = [masks[-1:] + masks[:-1], masks]
    down_weights = []
    for stage in range(len(masks)):
        before = half_a
        half_a = butterfly(half_a, orders[0][stage])
        half_b = butterfly(half_b, orders[1][stage])
        if stage < 2:
            columns = load(down_weight, before, wide, 0, stage == 0)
            columns, half_a, half_b = lax.optimization_barrier((columns, half_a, half_b))
            down_weights.append(columns)
    total = count * gate_weight.shape[1]
    limits = clip_scale.reshape(1, -1)
    theirs = down_project(half_a, half_b, limits, down_weights[:1], chips, total)
    own = down_project(half_a, half_b, limits, down_weights[1:], chips, total)
    arrived = cross(theirs)
    rows, wide = own.shape[0] // chips, own.shape[1]
    part = jax.ShapeDtypeStruct((rows, wide), jnp.bfloat16)

    far = hop(small(functools.partial(far_kernel, steps, chips), part, (own, arrived), "far"), 1, -1)
    for away in range(steps - 1, 0, -1):
        if away == steps - 1:
            body, operands = split_kernel, (far, own, arrived)
        else:
            body, operands = relay_kernel, (ahead, behind, own, arrived)
        ahead, behind = small(functools.partial(body, away, chips), (part, part), operands, "relay")
        ahead, behind = right(ahead), left(behind)
    half = jax.ShapeDtypeStruct((rows // 2, wide), jnp.bfloat16)
    kept = jax.ShapeDtypeStruct((rows // 2, wide), jnp.float32)
    keep, give = small(
        functools.partial(last_kernel, chips),
        (kept, half),
        (ahead, behind, own, arrived),
        "last",
        [pltpu.VMEM((rows, wide), jnp.float32)],
    )
    mixed = jax.ShapeDtypeStruct(tokens.shape, tokens.dtype)
    return small(mix_kernel, mixed, (tokens, keep, cross(give)), "mix")


def solution(mesh):
    in_specs = (
        P(("groups", "hid"), None),
        P(),
        P(None, "hid"),
        P(None, "hid"),
        P("hid", None),
        P("hid"),
    )
    out_specs = P(("groups", "hid"), None)
    body = functools.partial(shards, mesh.shape["hid"])
    return jax.shard_map(body, mesh=mesh, in_specs=in_specs, out_specs=out_specs, check_vma=False)
```

```python
import functools

import jax
import jax.numpy as jnp
from jax import lax
from jax.experimental import pallas as pl
from jax.experimental.pallas import tpu as pltpu
from jax.sharding import PartitionSpec as P

BLOCK = 256
MIB = 1 << 20


def hadamard(count):
    rows = lax.broadcasted_iota(jnp.int32, (count, count), 0)
    cols = lax.broadcasted_iota(jnp.int32, (count, count), 1)
    both = rows & cols
    parity = jnp.zeros((count, count), jnp.int32)
    for place in range(max(count.bit_length(), 1)):
        parity = parity + (both >> place & 1)
    return jnp.where(parity % 2 == 0, 1.0, -1.0).astype(jnp.bfloat16)


def normalize_kernel(rows_hbm, gain_hbm, out_ref, rows_ref, gain_ref, sems):
    copies = [
        pltpu.make_async_copy(rows_hbm, rows_ref, sems.at[0]),
        pltpu.make_async_copy(gain_hbm, gain_ref, sems.at[1]),
    ]
    for copy in copies:
        copy.start()
    for copy in copies:
        copy.wait()
    values = rows_ref[...].astype(jnp.float32)
    inverse = lax.rsqrt(jnp.mean(values * values, axis=-1, keepdims=True) + 1e-05)
    out_ref[...] = (values * inverse * gain_ref[...]).astype(jnp.bfloat16)


def in_hbm(value):
    return pltpu.with_memory_space_constraint(value, pltpu.HBM)


def normalize(rows_in, norm_gain):
    hbm = pl.BlockSpec(memory_space=pltpu.HBM)
    gain = norm_gain.reshape(1, -1)
    return pl.pallas_call(
        normalize_kernel,
        out_shape=jax.ShapeDtypeStruct(rows_in.shape, jnp.bfloat16),
        in_specs=[hbm, hbm],
        out_specs=pl.BlockSpec(memory_space=pltpu.VMEM),
        scratch_shapes=[
            pltpu.VMEM(rows_in.shape, rows_in.dtype),
            pltpu.VMEM(gain.shape, gain.dtype),
            pltpu.SemaphoreType.DMA((2,)),
        ],
        compiler_params=pltpu.CompilerParams(vmem_limit_bytes=4 * MIB),
        cost_estimate=pl.CostEstimate(flops=8 * rows_in.size, bytes_accessed=4 * rows_in.size, transcendentals=0),
        name="normalize",
    )(in_hbm(rows_in), in_hbm(gain))


def ring_of(chips):
    return list(range(0, chips, 2)) + list(range(chips - 1, 0, -2))


def ring_place(chip, shift, chips):
    spot = jnp.where(chip % 2 == 0, chip // 2, chips - 1 - (chip - 1) // 2)
    spot = (spot + shift) % chips
    return jnp.where(spot < (chips + 1) // 2, 2 * spot, 2 * (chips - spot) - 1)


def once(value, *others):
    return lax.optimization_barrier((value, *others))[0]


def load_kernel(at, weight_ref, after_ref, out_ref, sem):
    cols = out_ref.shape[1]
    at = lax.axis_index("hid") % 2 if at is None else at
    start = pl.multiple_of(at * cols, cols)
    copy = pltpu.make_async_copy(weight_ref.at[:, pl.ds(start, cols)], out_ref, sem)
    copy.start()
    copy.wait()


def load(weight, after, cols, at):
    rows = weight.shape[0]
    hbm = pl.BlockSpec(memory_space=pltpu.HBM)
    return pl.pallas_call(
        functools.partial(load_kernel, at),
        out_shape=jax.ShapeDtypeStruct((rows, cols), weight.dtype),
        in_specs=[hbm, hbm],
        out_specs=pl.BlockSpec(memory_space=pltpu.VMEM),
        scratch_shapes=[pltpu.SemaphoreType.DMA],
        compiler_params=pltpu.CompilerParams(vmem_limit_bytes=1 * MIB),
        cost_estimate=pl.CostEstimate(flops=0, bytes_accessed=2 * rows * cols, transcendentals=0),
        name="load",
    )(in_hbm(weight), after)


def up_kernel(count, shifts, *refs):
    me = lax.axis_index("hid")
    chip, core = me // 2, me % 2
    spots = []
    for shift in shifts:
        there = 2 * ring_place(chip, shift, count // 2)
        spots += [there + core, there + 1 - core]
    parts, (down_hbm, out_a, out_b, down_ref, rows_ref, hidden_ref, sem) = refs[:count], refs[-7:]
    gates, ups = refs[count:-7:2], refs[count + 1 : -7 : 2]
    cols = down_ref.shape[1]
    start = pl.multiple_of((1 - core) * cols, cols)
    fetch = pltpu.make_async_copy(down_hbm.at[:, pl.ds(start, cols)], down_ref, sem)
    fetch.start()
    own = parts[0].shape[0]
    for pair in range(count // 2):
        both = [parts[2 * pair + k][...].astype(jnp.float32) for k in range(2)]
        rows_ref[2 * own * pair : 2 * own * (pair + 1), :] = jnp.concatenate(both, axis=0).astype(jnp.bfloat16)
    turn = hadamard(BLOCK)
    values = rows_ref[...]
    wide = gates[0].shape[1]
    for at in range(len(gates)):
        gate = jnp.dot(values, gates[at][...], preferred_element_type=jnp.float32)
        up = jnp.dot(values, ups[at][...], preferred_element_type=jnp.float32)
        hidden = gate / (1.0 + jnp.exp(-gate)) * up
        high = hidden.astype(jnp.bfloat16)
        low = (hidden - high.astype(jnp.float32)).astype(jnp.bfloat16)
        for block in range(wide // BLOCK):
            inner = slice(block * BLOCK, (block + 1) * BLOCK)
            outer = slice(at * wide + block * BLOCK, at * wide + (block + 1) * BLOCK)
            turned = jnp.dot(high[:, inner], turn, preferred_element_type=jnp.float32) + jnp.dot(
                low[:, inner], turn, preferred_element_type=jnp.float32
            )
            for part in range(count):
                spot = pl.multiple_of(spots[part] * own, own)
                hidden_ref[pl.ds(spot, own), outer] = turned[part * own : (part + 1) * own]
    half = out_a.shape[1]
    out_a[...] = hidden_ref[:, :half].astype(jnp.bfloat16)
    out_b[...] = hidden_ref[:, half:].astype(jnp.bfloat16)
    fetch.wait()


def up_project(shifts, parts, weights, down_weight):
    count, own = len(parts), parts[0].shape[0]
    depth = weights[0].shape[0]
    width = weights[0].shape[1] * len(weights) // 2
    rows = count * own
    half = jax.ShapeDtypeStruct((rows, width // 2), jnp.bfloat16)
    down = jax.ShapeDtypeStruct((down_weight.shape[0], down_weight.shape[1] // 2), down_weight.dtype)
    vmem = pl.BlockSpec(memory_space=pltpu.VMEM)
    return pl.pallas_call(
        functools.partial(up_kernel, count, shifts),
        out_shape=[half, half] + [down],
        in_specs=[vmem] * (count + len(weights)) + [pl.BlockSpec(memory_space=pltpu.HBM)],
        out_specs=[vmem] * 3,
        scratch_shapes=[
            pltpu.VMEM((rows, depth), jnp.bfloat16),
            pltpu.VMEM((rows, width), jnp.float32),
            pltpu.SemaphoreType.DMA,
        ],
        compiler_params=pltpu.CompilerParams(vmem_limit_bytes=6 * MIB),
        cost_estimate=pl.CostEstimate(flops=4 * rows * depth * width, bytes_accessed=0, transcendentals=rows * width),
        name="up_project",
    )(*parts, *weights, in_hbm(down_weight))


def down_kernel(blocks, chips, scale, a_ref, b_ref, clip_ref, weight_ref, *refs):
    outs, (rows_ref, mixed_ref) = refs[:-2], refs[-2:]
    half = a_ref.shape[1]
    rows_ref[:, :half] = a_ref[...].astype(jnp.float32)
    rows_ref[:, half:] = b_ref[...].astype(jnp.float32)
    parts = [rows_ref[:, b * BLOCK : (b + 1) * BLOCK] for b in range(blocks)]
    span = 1
    while span < blocks:
        parts = [
            parts[b] + parts[b ^ span] if b & span == 0 else parts[b ^ span] - parts[b] for b in range(blocks)
        ]
        span *= 2
    for b in range(blocks):
        lanes = slice(b * BLOCK, (b + 1) * BLOCK)
        limit = 127.0 * clip_ref[:, lanes]
        rows_ref[:, lanes] = jnp.clip(parts[b] * scale, -limit, limit)
    rows = rows_ref.shape[0]
    each = rows // chips
    me = lax.axis_index("hid")
    for chip in range(chips):
        spot = pl.multiple_of(ring_place(me // 2, chip + chips // 2, chips) * each, each)
        mixed_ref[chip * each : (chip + 1) * each, :] = rows_ref[pl.ds(spot, each), :].astype(jnp.bfloat16)
    product = jnp.dot(mixed_ref[...], weight_ref[...], preferred_element_type=jnp.float32)
    first = 0
    for out_ref in outs:
        out_ref[...] = product[first : first + out_ref.shape[0]].astype(jnp.bfloat16)
        first += out_ref.shape[0]


def down_project(a, b, clip_scale, weight, chips, total):
    rows = a.shape[0]
    width, depth = weight.shape
    vmem = pl.BlockSpec(memory_space=pltpu.VMEM)
    outs = [
        jax.ShapeDtypeStruct((count, depth), jnp.bfloat16) for count in (rows // chips, rows - rows // chips)
    ]
    return pl.pallas_call(
        functools.partial(down_kernel, width // BLOCK, chips, total**-0.5),
        out_shape=outs,
        in_specs=[vmem] * 4,
        out_specs=[vmem] * 2,
        scratch_shapes=[pltpu.VMEM((rows, width), jnp.float32), pltpu.VMEM((rows, width), jnp.bfloat16)],
        compiler_params=pltpu.CompilerParams(vmem_limit_bytes=8 * MIB),
        cost_estimate=pl.CostEstimate(flops=2 * rows * depth * width, bytes_accessed=0, transcendentals=0),
        name="down_project",
    )(a, b, clip_scale, weight)


def pick_kernel(even_ref, odd_ref, out_ref):
    core = lax.axis_index("hid") % 2

    @pl.when(core == 0)
    def _():
        out_ref[...] = even_ref[...]

    @pl.when(core != 0)
    def _():
        out_ref[...] = odd_ref[...]


def turn_kernel(mask, value_ref, other_ref, out_ref):
    sign = jnp.where(lax.axis_index("hid") & mask == 0, 1.0, -1.0).astype(jnp.float32)
    out_ref[...] = (other_ref[...].astype(jnp.float32) + sign * value_ref[...].astype(jnp.float32)).astype(jnp.bfloat16)


def both(body, first, second, name):
    vmem = pl.BlockSpec(memory_space=pltpu.VMEM)
    return pl.pallas_call(
        body,
        out_shape=jax.ShapeDtypeStruct(first.shape, first.dtype),
        in_specs=[vmem, vmem],
        out_specs=vmem,
        compiler_params=pltpu.CompilerParams(vmem_limit_bytes=2 * MIB),
        cost_estimate=pl.CostEstimate(flops=2 * first.size, bytes_accessed=0, transcendentals=0),
        name=name,
    )(first, second)


def chunk(away, chips, own_ref, arrived_ref):
    rows = own_ref.shape[0] // (chips - 1)
    spot = (away + chips // 2 - 1) % chips
    at = slice(spot * rows, (spot + 1) * rows)
    return own_ref[at, :].astype(jnp.float32) + arrived_ref[at, :].astype(jnp.float32)


def sum_kernel(one_ref, two_ref, out_ref):
    out_ref[...] = (one_ref[...].astype(jnp.float32) + two_ref[...].astype(jnp.float32)).astype(jnp.bfloat16)


def relay_kernel(away, chips, core, arrived_in, own_ref, arrived_ref, out_ref):
    value = arrived_in[...].astype(jnp.float32)
    if core is not None:
        value = jnp.where(lax.axis_index("hid") % 2 == core, value, 0.0)
    out_ref[...] = (chunk(away, chips, own_ref, arrived_ref) + value).astype(jnp.bfloat16)


def last_kernel(chips, ahead_in, behind_in, own_ref, arrived_ref, keep_ref, give_ref, sum_ref):
    part = keep_ref.shape[0]
    core = lax.axis_index("hid") % 2
    sum_ref[...] = (
        chunk(0, chips, own_ref, arrived_ref) + ahead_in[...].astype(jnp.float32) + behind_in[...].astype(jnp.float32)
    )
    keep_ref[...] = sum_ref[pl.ds(pl.multiple_of(core * part, part), part), :]
    give_ref[...] = sum_ref[pl.ds(pl.multiple_of((1 - core) * part, part), part), :].astype(jnp.bfloat16)


def mix_kernel(tokens_ref, keep_ref, take_ref, out_ref):
    wide = keep_ref.shape[1]
    keep, take = keep_ref[...], take_ref[...].astype(jnp.float32)
    first = lax.axis_index("hid") % 2 == 0
    low, high = jnp.where(first, keep, take), jnp.where(first, take, keep)
    out_ref[:, :wide] = (tokens_ref[:, :wide].astype(jnp.float32) + low).astype(jnp.bfloat16)
    out_ref[:, wide:] = (tokens_ref[:, wide:].astype(jnp.float32) + high).astype(jnp.bfloat16)


def small(body, outs, operands, name, scratch=()):
    vmem = pl.BlockSpec(memory_space=pltpu.VMEM)
    return pl.pallas_call(
        body,
        out_shape=outs,
        in_specs=[vmem] * len(operands),
        out_specs=jax.tree.map(lambda _: vmem, outs),
        scratch_shapes=scratch,
        compiler_params=pltpu.CompilerParams(vmem_limit_bytes=4 * MIB),
        cost_estimate=pl.CostEstimate(flops=2 * operands[0].size, bytes_accessed=0, transcendentals=0),
        name=name,
    )(*operands)


def shards(count, tokens, norm_gain, gate_weight, up_weight, down_weight, clip_scale):
    chips = count // 2
    order = ring_of(chips)
    steps = chips // 2

    def hop(value, shift_even, shift_odd):
        pairs = []
        for at, c in enumerate(order):
            pairs.append((2 * c, 2 * order[(at + shift_even) % chips]))
            pairs.append((2 * c + 1, 2 * order[(at + shift_odd) % chips] + 1))
        return lax.ppermute(value, "hid", pairs)

    def right(value):
        return hop(value, 1, 1)

    def left(value):
        return hop(value, -1, -1)

    def cross(value, mask=1):
        return lax.ppermute(value, "hid", [(d, d ^ mask) for d in range(count)])

    normed = normalize(tokens, norm_gain)
    width = gate_weight.shape[1]
    wide = max(BLOCK, width // 2)
    wanted = [(weight, at) for at in range(width // wide) for weight in (gate_weight, up_weight)]
    weights = []

    def beside(after, arrived, *others):
        if len(weights) < len(wanted):
            weight, at = wanted[len(weights)]
            weights.append(load(weight, after, wide, at))
            others = (weights[-1], *others)
        return once(arrived, *others) if others else arrived

    parts, shifts = [normed, cross(normed)], [0]
    ahead = behind = normed
    for step in range(1, steps):
        after, done = behind, parts[-1:] if step == 1 else parts[-3::2]
        ahead, behind = right(ahead), left(behind)
        behind = beside(after, behind, *done)
        parts += [ahead, cross(ahead), behind, cross(behind)]
        shifts += [-step, step]
    far = beside(ahead, hop(both(pick_kernel, ahead, behind, "pick"), 1, -1), *parts[-3::2])
    parts += [far, cross(far)]
    shifts.append(steps)
    while len(weights) < len(wanted):
        parts[0] = beside(parts[0], parts[0])

    half_a, half_b, down_theirs = up_project(shifts, parts, weights, down_weight)

    def turn(value, mask, *others):
        return both(functools.partial(turn_kernel, mask), value, once(cross(value, mask), *others), "turn")

    masks = [1 << bit for bit in range(count.bit_length() - 1)]
    for stage in range(len(masks)):
        first, second = masks[stage - 1], masks[stage]
        if stage == 0:
            half_b = turn(half_b, second)
            down_own = load(down_weight, half_b, down_weight.shape[1] // 2, None)
            half_a = turn(half_a, first, half_b, down_own)
        elif stage < len(masks) - 1:
            half_b = turn(half_b, second, half_a)
            half_a = turn(half_a, first, half_b)
        else:
            half_a = turn(half_a, first, half_b)
            half_b = turn(half_b, second, half_a)

    total = count * width
    limits = clip_scale.reshape(1, -1)
    theirs_far, theirs = down_project(half_a, half_b, limits, down_theirs, chips, total)
    arrived_far = cross(theirs_far)
    own_far, own = down_project(half_a, half_b, limits, down_own, chips, total)
    arrived = cross(once(theirs, own, arrived_far))
    rows, wide = own_far.shape
    part = jax.ShapeDtypeStruct((rows, wide), jnp.bfloat16)

    ahead = behind = hop(small(sum_kernel, part, (own_far, arrived_far), "far"), 1, -1)
    for away in range(steps - 1, 0, -1):
        cores = (0, 1) if away == steps - 1 else (None, None)
        ahead = small(
            functools.partial(relay_kernel, away, chips, cores[0]), part, (ahead, own, arrived), "relay"
        )
        behind = small(
            functools.partial(relay_kernel, -away, chips, cores[1]), part, (behind, own, arrived), "relay"
        )
        ahead, behind = right(ahead), left(behind)
    half = jax.ShapeDtypeStruct((rows // 2, wide), jnp.bfloat16)
    kept = jax.ShapeDtypeStruct((rows // 2, wide), jnp.float32)
    keep, give = small(
        functools.partial(last_kernel, chips),
        (kept, half),
        (ahead, behind, own, arrived),
        "last",
        [pltpu.VMEM((rows, wide), jnp.float32)],
    )
    mixed = jax.ShapeDtypeStruct(tokens.shape, tokens.dtype)
    return small(mix_kernel, mixed, (tokens, keep, cross(give)), "mix")


def solution(mesh):
    in_specs = (
        P(("groups", "hid"), None),
        P(),
        P(None, "hid"),
        P(None, "hid"),
        P("hid", None),
        P("hid"),
    )
    out_specs = P(("groups", "hid"), None)
    body = functools.partial(shards, mesh.shape["hid"])
    return jax.shard_map(body, mesh=mesh, in_specs=in_specs, out_specs=out_specs, check_vma=False)
```

```python
import functools

import jax
import jax.numpy as jnp
from jax import lax
from jax.experimental import pallas as pl
from jax.experimental.pallas import tpu as pltpu
from jax.sharding import PartitionSpec as P

BLOCK = 256
MIB = 1 << 20


def hadamard(count):
    rows = lax.broadcasted_iota(jnp.int32, (count, count), 0)
    cols = lax.broadcasted_iota(jnp.int32, (count, count), 1)
    both = rows & cols
    parity = jnp.zeros((count, count), jnp.int32)
    for place in range(max(count.bit_length(), 1)):
        parity = parity + (both >> place & 1)
    return jnp.where(parity % 2 == 0, 1.0, -1.0).astype(jnp.bfloat16)


def normalize_kernel(rows_hbm, gain_hbm, out_ref, rows_ref, gain_ref, sems):
    copies = [
        pltpu.make_async_copy(rows_hbm, rows_ref, sems.at[0]),
        pltpu.make_async_copy(gain_hbm, gain_ref, sems.at[1]),
    ]
    for copy in copies:
        copy.start()
    for copy in copies:
        copy.wait()
    values = rows_ref[...].astype(jnp.float32)
    inverse = lax.rsqrt(jnp.mean(values * values, axis=-1, keepdims=True) + 1e-05)
    out_ref[...] = (values * inverse * gain_ref[...]).astype(jnp.bfloat16)


def in_hbm(value):
    return pltpu.with_memory_space_constraint(value, pltpu.HBM)


def normalize(rows_in, norm_gain):
    hbm = pl.BlockSpec(memory_space=pltpu.HBM)
    gain = norm_gain.reshape(1, -1)
    return pl.pallas_call(
        normalize_kernel,
        out_shape=jax.ShapeDtypeStruct(rows_in.shape, jnp.bfloat16),
        in_specs=[hbm, hbm],
        out_specs=pl.BlockSpec(memory_space=pltpu.VMEM),
        scratch_shapes=[
            pltpu.VMEM(rows_in.shape, rows_in.dtype),
            pltpu.VMEM(gain.shape, gain.dtype),
            pltpu.SemaphoreType.DMA((2,)),
        ],
        compiler_params=pltpu.CompilerParams(vmem_limit_bytes=4 * MIB),
        cost_estimate=pl.CostEstimate(flops=8 * rows_in.size, bytes_accessed=4 * rows_in.size, transcendentals=0),
        name="normalize",
    )(in_hbm(rows_in), in_hbm(gain))


def ring_of(chips):
    return list(range(0, chips, 2)) + list(range(chips - 1, 0, -2))


def ring_place(chip, shift, chips):
    spot = jnp.where(chip % 2 == 0, chip // 2, chips - 1 - (chip - 1) // 2)
    spot = (spot + shift) % chips
    return jnp.where(spot < (chips + 1) // 2, 2 * spot, 2 * (chips - spot) - 1)


def once(value, *others):
    return lax.optimization_barrier((value, *others))[0]


def load_kernel(places, after_ref, *refs):
    count = len(places)
    weights, outs, sems = refs[:count], refs[count:-1], refs[-1]
    core = lax.axis_index("hid") % 2
    copies = []
    for piece, (own, pieces, at) in enumerate(places):
        cols = outs[piece].shape[1]
        side = 0 if own is None else core if own else 1 - core
        start = pl.multiple_of((side * pieces + at) * cols, cols)
        copies.append(
            pltpu.make_async_copy(weights[piece].at[:, pl.ds(start, cols)], outs[piece], sems.at[piece])
        )
    for copy in copies:
        copy.start()
    for copy in copies:
        copy.wait()


def load(after, *wanted):
    hbm = pl.BlockSpec(memory_space=pltpu.HBM)
    shapes = []
    for weight, own, pieces, _ in wanted:
        cols = weight.shape[1] // (pieces if own is None else 2 * pieces)
        shapes.append(jax.ShapeDtypeStruct((weight.shape[0], cols), weight.dtype))
    return pl.pallas_call(
        functools.partial(load_kernel, [place[1:] for place in wanted]),
        out_shape=shapes,
        in_specs=[hbm] * (1 + len(wanted)),
        out_specs=[pl.BlockSpec(memory_space=pltpu.VMEM)] * len(wanted),
        scratch_shapes=[pltpu.SemaphoreType.DMA((len(wanted),))],
        compiler_params=pltpu.CompilerParams(vmem_limit_bytes=1 * MIB),
        cost_estimate=pl.CostEstimate(flops=0, bytes_accessed=2 * sum(s.size for s in shapes), transcendentals=0),
        name="load",
    )(after, *[in_hbm(place[0]) for place in wanted])


def join_rows(parts, out_ref):
    own = parts[0].shape[0]
    for pair in range(len(parts) // 2):
        both = [parts[2 * pair + k][...].astype(jnp.float32) for k in range(2)]
        out_ref[2 * own * pair : 2 * own * (pair + 1), :] = jnp.concatenate(both, axis=0).astype(jnp.bfloat16)


def up_kernel(shifts, first, *refs):
    count = 2 * len(shifts)
    if first:
        gate_ref, up_ref, out_ref, rows_ref, hidden_ref = refs[count:]
        join_rows(refs[:count], rows_ref)
    else:
        rows_ref, gate_ref, up_ref, out_ref, hidden_ref = refs
    me = lax.axis_index("hid")
    chip, core = me // 2, me % 2
    own = rows_ref.shape[0] // count
    turn = hadamard(BLOCK)
    values = rows_ref[...]
    gate = jnp.dot(values, gate_ref[...], preferred_element_type=jnp.float32)
    up = jnp.dot(values, up_ref[...], preferred_element_type=jnp.float32)
    hidden = gate / (1.0 + jnp.exp(-gate)) * up
    high = hidden.astype(jnp.bfloat16)
    low = (hidden - high.astype(jnp.float32)).astype(jnp.bfloat16)
    for block in range(gate.shape[1] // BLOCK):
        lanes = slice(block * BLOCK, (block + 1) * BLOCK)
        turned = jnp.dot(high[:, lanes], turn, preferred_element_type=jnp.float32) + jnp.dot(
            low[:, lanes], turn, preferred_element_type=jnp.float32
        )
        for part in range(count):
            there = 2 * ring_place(chip, shifts[part // 2], count // 2)
            there = there + core if part % 2 == 0 else there + 1 - core
            spot = pl.multiple_of(there * own, own)
            hidden_ref[pl.ds(spot, own), lanes] = turned[part * own : (part + 1) * own]
    out_ref[...] = hidden_ref[...].astype(jnp.bfloat16)


def up_project(shifts, parts, gate_weight, up_weight):
    first = len(parts) > 1
    depth, width = gate_weight.shape
    rows = sum(part.shape[0] for part in parts)
    vmem = pl.BlockSpec(memory_space=pltpu.VMEM)
    outs = [jax.ShapeDtypeStruct((rows, width), jnp.bfloat16)]
    if first:
        outs.append(jax.ShapeDtypeStruct((rows, depth), jnp.bfloat16))
    return pl.pallas_call(
        functools.partial(up_kernel, shifts, first),
        out_shape=outs,
        in_specs=[vmem] * (len(parts) + 2),
        out_specs=[vmem] * len(outs),
        scratch_shapes=[pltpu.VMEM((rows, width), jnp.float32)],
        compiler_params=pltpu.CompilerParams(vmem_limit_bytes=4 * MIB + 2 * rows * depth),
        cost_estimate=pl.CostEstimate(flops=4 * rows * depth * width, bytes_accessed=0, transcendentals=rows * width),
        name="up_project",
    )(*parts, gate_weight, up_weight)


def down_kernel(blocks, chips, scale, a_ref, b_ref, clip_ref, *refs):
    weights, outs, (rows_ref, mixed_ref) = refs[:-4], refs[-4:-2], refs[-2:]
    half = a_ref.shape[1]
    rows_ref[:, :half] = a_ref[...].astype(jnp.float32)
    rows_ref[:, half:] = b_ref[...].astype(jnp.float32)
    parts = [rows_ref[:, b * BLOCK : (b + 1) * BLOCK] for b in range(blocks)]
    span = 1
    while span < blocks:
        parts = [
            parts[b] + parts[b ^ span] if b & span == 0 else parts[b ^ span] - parts[b] for b in range(blocks)
        ]
        span *= 2
    for b in range(blocks):
        lanes = slice(b * BLOCK, (b + 1) * BLOCK)
        limit = 127.0 * clip_ref[:, lanes]
        rows_ref[:, lanes] = jnp.clip(parts[b] * scale, -limit, limit)
    rows = rows_ref.shape[0]
    each = rows // chips
    me = lax.axis_index("hid")
    for chip in range(chips):
        spot = pl.multiple_of(ring_place(me // 2, chip + chips // 2, chips) * each, each)
        mixed_ref[chip * each : (chip + 1) * each, :] = rows_ref[pl.ds(spot, each), :].astype(jnp.bfloat16)
    wide = weights[0].shape[1]
    for at, weight_ref in enumerate(weights):
        product = jnp.dot(mixed_ref[...], weight_ref[...], preferred_element_type=jnp.float32)
        first = 0
        for out_ref in outs:
            out_ref[:, at * wide : (at + 1) * wide] = product[first : first + out_ref.shape[0]].astype(jnp.bfloat16)
            first += out_ref.shape[0]


def down_project(a, b, clip_scale, weights, chips, total):
    rows = a.shape[0]
    width, depth = weights[0].shape[0], weights[0].shape[1] * len(weights)
    vmem = pl.BlockSpec(memory_space=pltpu.VMEM)
    outs = [
        jax.ShapeDtypeStruct((count, depth), jnp.bfloat16) for count in (rows // chips, rows - rows // chips)
    ]
    return pl.pallas_call(
        functools.partial(down_kernel, width // BLOCK, chips, total**-0.5),
        out_shape=outs,
        in_specs=[vmem] * (3 + len(weights)),
        out_specs=[vmem] * 2,
        scratch_shapes=[pltpu.VMEM((rows, width), jnp.float32), pltpu.VMEM((rows, width), jnp.bfloat16)],
        compiler_params=pltpu.CompilerParams(vmem_limit_bytes=8 * MIB),
        cost_estimate=pl.CostEstimate(flops=2 * rows * depth * width, bytes_accessed=0, transcendentals=0),
        name="down_project",
    )(a, b, clip_scale, *weights)


def pick_kernel(even_ref, odd_ref, out_ref):
    core = lax.axis_index("hid") % 2

    @pl.when(core == 0)
    def _():
        out_ref[...] = even_ref[...]

    @pl.when(core != 0)
    def _():
        out_ref[...] = odd_ref[...]


def turn_kernel(mask, value_ref, other_ref, out_ref):
    sign = jnp.where(lax.axis_index("hid") & mask == 0, 1.0, -1.0).astype(jnp.float32)
    out_ref[...] = (other_ref[...].astype(jnp.float32) + sign * value_ref[...].astype(jnp.float32)).astype(jnp.bfloat16)


def both(body, first, second, name):
    vmem = pl.BlockSpec(memory_space=pltpu.VMEM)
    return pl.pallas_call(
        body,
        out_shape=jax.ShapeDtypeStruct(first.shape, first.dtype),
        in_specs=[vmem, vmem],
        out_specs=vmem,
        compiler_params=pltpu.CompilerParams(vmem_limit_bytes=2 * MIB),
        cost_estimate=pl.CostEstimate(flops=2 * first.size, bytes_accessed=0, transcendentals=0),
        name=name,
    )(first, second)


def chunk(away, chips, own_ref, arrived_ref):
    rows = own_ref.shape[0] // (chips - 1)
    spot = (away + chips // 2 - 1) % chips
    at = slice(spot * rows, (spot + 1) * rows)
    return own_ref[at, :].astype(jnp.float32) + arrived_ref[at, :].astype(jnp.float32)


def sum_kernel(one_ref, two_ref, out_ref):
    out_ref[...] = (one_ref[...].astype(jnp.float32) + two_ref[...].astype(jnp.float32)).astype(jnp.bfloat16)


def relay_kernel(away, chips, core, arrived_in, own_ref, arrived_ref, out_ref):
    value = arrived_in[...].astype(jnp.float32)
    if core is not None:
        value = jnp.where(lax.axis_index("hid") % 2 == core, value, 0.0)
    out_ref[...] = (chunk(away, chips, own_ref, arrived_ref) + value).astype(jnp.bfloat16)


def last_kernel(chips, ahead_in, behind_in, own_ref, arrived_ref, keep_ref, give_ref, sum_ref):
    part = keep_ref.shape[0]
    core = lax.axis_index("hid") % 2
    sum_ref[...] = (
        chunk(0, chips, own_ref, arrived_ref) + ahead_in[...].astype(jnp.float32) + behind_in[...].astype(jnp.float32)
    )
    keep_ref[...] = sum_ref[pl.ds(pl.multiple_of(core * part, part), part), :]
    give_ref[...] = sum_ref[pl.ds(pl.multiple_of((1 - core) * part, part), part), :].astype(jnp.bfloat16)


def mix_kernel(tokens_ref, keep_ref, take_ref, out_ref):
    wide = keep_ref.shape[1]
    keep, take = keep_ref[...], take_ref[...].astype(jnp.float32)
    first = lax.axis_index("hid") % 2 == 0
    low, high = jnp.where(first, keep, take), jnp.where(first, take, keep)
    out_ref[:, :wide] = (tokens_ref[:, :wide].astype(jnp.float32) + low).astype(jnp.bfloat16)
    out_ref[:, wide:] = (tokens_ref[:, wide:].astype(jnp.float32) + high).astype(jnp.bfloat16)


def small(body, outs, operands, name, scratch=()):
    vmem = pl.BlockSpec(memory_space=pltpu.VMEM)
    return pl.pallas_call(
        body,
        out_shape=outs,
        in_specs=[vmem] * len(operands),
        out_specs=jax.tree.map(lambda _: vmem, outs),
        scratch_shapes=scratch,
        compiler_params=pltpu.CompilerParams(vmem_limit_bytes=4 * MIB),
        cost_estimate=pl.CostEstimate(flops=2 * operands[0].size, bytes_accessed=0, transcendentals=0),
        name=name,
    )(*operands)


def shards(count, tokens, norm_gain, gate_weight, up_weight, down_weight, clip_scale):
    chips = count // 2
    order = ring_of(chips)
    steps = chips // 2

    def hop(value, shift_even, shift_odd):
        pairs = []
        for at, c in enumerate(order):
            pairs.append((2 * c, 2 * order[(at + shift_even) % chips]))
            pairs.append((2 * c + 1, 2 * order[(at + shift_odd) % chips] + 1))
        return lax.ppermute(value, "hid", pairs)

    def right(value):
        return hop(value, 1, 1)

    def left(value):
        return hop(value, -1, -1)

    def cross(value, mask=1):
        return lax.ppermute(value, "hid", [(d, d ^ mask) for d in range(count)])

    normed = normalize(tokens, norm_gain)
    width = gate_weight.shape[1]
    pieces = width // max(BLOCK, width // 2)
    wanted = [(weight, None, pieces, at) for at in range(pieces) for weight in (gate_weight, up_weight)]
    weights, down_theirs = [], []

    def beside(after, arrived):
        if len(weights) < len(wanted):
            at = len(weights)
            columns, below = load(after, wanted[at], (down_weight, False, len(wanted), at))
            weights.append(columns)
            down_theirs.append(below)
            arrived = once(arrived, columns, below)
        return arrived

    mine, shifts = [normed], [0]
    ahead = behind = normed
    for step in range(1, steps):
        after = behind
        ahead, behind = right(ahead), left(behind)
        behind = beside(after, behind)
        mine += [ahead, behind]
        shifts += [-step, step]
    mine.append(beside(ahead, hop(both(pick_kernel, ahead, behind, "pick"), 1, -1)))
    shifts.append(steps)
    while len(weights) < len(wanted):
        mine[0] = beside(mine[0], mine[0])
    parts = [block for own in mine for block in (own, cross(own))]

    half_b, joined = up_project(shifts, parts, *weights[-2:])
    if pieces == 1:
        half_a, half_b = jnp.split(half_b, 2, axis=1)
    else:
        (half_a,) = up_project(shifts, [joined], *weights[:2])

    def turn(value, mask, *others):
        return both(functools.partial(turn_kernel, mask), value, once(cross(value, mask), *others), "turn")

    masks = [1 << bit for bit in range(count.bit_length() - 1)]
    for stage in range(len(masks)):
        first, second = masks[stage - 1], masks[stage]
        if stage == 0:
            half_b = turn(half_b, second)
            (down_own,) = load(half_b, (down_weight, True, 1, 0))
            early = turn(half_b, masks[1], down_own)
            half_a = turn(half_a, first, half_b, down_own)
        elif stage == 1:
            half_b = early
            half_a = turn(half_a, first, early)
        elif stage < len(masks) - 1:
            half_b = turn(half_b, second, half_a)
            half_a = turn(half_a, first, half_b)
        else:
            half_a = turn(half_a, first, half_b)
            half_b = turn(half_b, second, half_a)

    total = count * width
    limits = clip_scale.reshape(1, -1)
    theirs_far, theirs = down_project(half_a, half_b, limits, down_theirs, chips, total)
    arrived_far = cross(theirs_far)
    own_far, own = down_project(half_a, half_b, limits, [down_own], chips, total)
    arrived = cross(once(theirs, own, arrived_far))
    rows, wide = own_far.shape
    part = jax.ShapeDtypeStruct((rows, wide), jnp.bfloat16)

    ahead = behind = hop(small(sum_kernel, part, (own_far, arrived_far), "far"), 1, -1)
    for away in range(steps - 1, 0, -1):
        cores = (0, 1) if away == steps - 1 else (None, None)
        ahead = small(
            functools.partial(relay_kernel, away, chips, cores[0]), part, (ahead, own, arrived), "relay"
        )
        behind = small(
            functools.partial(relay_kernel, -away, chips, cores[1]), part, (behind, own, arrived), "relay"
        )
        ahead, behind = right(ahead), left(behind)
    half = jax.ShapeDtypeStruct((rows // 2, wide), jnp.bfloat16)
    kept = jax.ShapeDtypeStruct((rows // 2, wide), jnp.float32)
    keep, give = small(
        functools.partial(last_kernel, chips),
        (kept, half),
        (ahead, behind, own, arrived),
        "last",
        [pltpu.VMEM((rows, wide), jnp.float32)],
    )
    mixed = jax.ShapeDtypeStruct(tokens.shape, tokens.dtype)
    return small(mix_kernel, mixed, (tokens, keep, cross(give)), "mix")


def solution(mesh):
    in_specs = (
        P(("groups", "hid"), None),
        P(),
        P(None, "hid"),
        P(None, "hid"),
        P("hid", None),
        P("hid"),
    )
    out_specs = P(("groups", "hid"), None)
    body = functools.partial(shards, mesh.shape["hid"])
    return jax.shard_map(body, mesh=mesh, in_specs=in_specs, out_specs=out_specs, check_vma=False)
```

```python
import functools

import jax
import jax.numpy as jnp
from jax import lax
from jax.experimental import pallas as pl
from jax.experimental.pallas import tpu as pltpu
from jax.sharding import PartitionSpec as P

BLOCK = 256
MIB = 1 << 20
TURN = 2_000_000_000
COST = 20_000_000_000


def hadamard(count):
    rows = lax.broadcasted_iota(jnp.int32, (count, count), 0)
    cols = lax.broadcasted_iota(jnp.int32, (count, count), 1)
    both = rows & cols
    parity = jnp.zeros((count, count), jnp.int32)
    for place in range(max(count.bit_length(), 1)):
        parity = parity + (both >> place & 1)
    return jnp.where(parity % 2 == 0, 1.0, -1.0).astype(jnp.bfloat16)


def normalize_kernel(rows_hbm, gain_hbm, out_ref, rows_ref, gain_ref, sems):
    copies = [
        pltpu.make_async_copy(rows_hbm, rows_ref, sems.at[0]),
        pltpu.make_async_copy(gain_hbm, gain_ref, sems.at[1]),
    ]
    for copy in copies:
        copy.start()
    for copy in copies:
        copy.wait()
    values = rows_ref[...].astype(jnp.float32)
    inverse = lax.rsqrt(jnp.mean(values * values, axis=-1, keepdims=True) + 1e-05)
    out_ref[...] = (values * inverse * gain_ref[...]).astype(jnp.bfloat16)


def in_hbm(value):
    return pltpu.with_memory_space_constraint(value, pltpu.HBM)


def normalize(rows_in, norm_gain):
    hbm = pl.BlockSpec(memory_space=pltpu.HBM)
    gain = norm_gain.reshape(1, -1)
    return pl.pallas_call(
        normalize_kernel,
        out_shape=jax.ShapeDtypeStruct(rows_in.shape, jnp.bfloat16),
        in_specs=[hbm, hbm],
        out_specs=pl.BlockSpec(memory_space=pltpu.VMEM),
        scratch_shapes=[
            pltpu.VMEM(rows_in.shape, rows_in.dtype),
            pltpu.VMEM(gain.shape, gain.dtype),
            pltpu.SemaphoreType.DMA((2,)),
        ],
        compiler_params=pltpu.CompilerParams(vmem_limit_bytes=4 * MIB),
        cost_estimate=pl.CostEstimate(flops=COST, bytes_accessed=4 * rows_in.size, transcendentals=0),
        name="normalize",
    )(in_hbm(rows_in), in_hbm(gain))


def ring_of(chips):
    return list(range(0, chips, 2)) + list(range(chips - 1, 0, -2))


def ring_place(chip, shift, chips):
    spot = jnp.where(chip % 2 == 0, chip // 2, chips - 1 - (chip - 1) // 2)
    spot = (spot + shift) % chips
    return jnp.where(spot < (chips + 1) // 2, 2 * spot, 2 * (chips - spot) - 1)


def once(value, *others):
    return lax.optimization_barrier((value, *others))[0]


def join_rows(parts, out_ref):
    own = parts[0].shape[0]
    for pair in range(len(parts) // 2):
        both = [parts[2 * pair + k][...].astype(jnp.float32) for k in range(2)]
        out_ref[2 * own * pair : 2 * own * (pair + 1), :] = jnp.concatenate(both, axis=0).astype(jnp.bfloat16)


def up_kernel(shifts, first, lanes_of, *refs):
    count = 2 * len(shifts)
    if first:
        gate_ref, up_ref, out_ref, rows_ref, hidden_ref = refs[count:]
        join_rows(refs[:count], rows_ref)
    else:
        rows_ref, gate_ref, up_ref, out_ref, hidden_ref = refs
    me = lax.axis_index("hid")
    chip, core = me // 2, me % 2
    own = rows_ref.shape[0] // count
    turn = hadamard(BLOCK)
    values = rows_ref[...]
    gate = jnp.dot(values, gate_ref[:, lanes_of], preferred_element_type=jnp.float32)
    up = jnp.dot(values, up_ref[:, lanes_of], preferred_element_type=jnp.float32)
    hidden = gate / (1.0 + jnp.exp(-gate)) * up
    high = hidden.astype(jnp.bfloat16)
    low = (hidden - high.astype(jnp.float32)).astype(jnp.bfloat16)
    for block in range(gate.shape[1] // BLOCK):
        lanes = slice(block * BLOCK, (block + 1) * BLOCK)
        turned = jnp.dot(high[:, lanes], turn, preferred_element_type=jnp.float32) + jnp.dot(
            low[:, lanes], turn, preferred_element_type=jnp.float32
        )
        for part in range(count):
            there = 2 * ring_place(chip, shifts[part // 2], count // 2)
            there = there + core if part % 2 == 0 else there + 1 - core
            spot = pl.multiple_of(there * own, own)
            hidden_ref[pl.ds(spot, own), lanes] = turned[part * own : (part + 1) * own]
    out_ref[...] = hidden_ref[...].astype(jnp.bfloat16)


def up_project(shifts, parts, gate_weight, up_weight, at, pieces):
    first = len(parts) > 1
    depth, width = gate_weight.shape
    width = width // pieces
    rows = sum(part.shape[0] for part in parts)
    vmem = pl.BlockSpec(memory_space=pltpu.VMEM)
    outs = [jax.ShapeDtypeStruct((rows, width), jnp.bfloat16)]
    if first:
        outs.append(jax.ShapeDtypeStruct((rows, depth), jnp.bfloat16))
    return pl.pallas_call(
        functools.partial(up_kernel, shifts, first, slice(at * width, (at + 1) * width)),
        out_shape=outs,
        in_specs=[vmem] * (len(parts) + 2),
        out_specs=[vmem] * len(outs),
        scratch_shapes=[pltpu.VMEM((rows, width), jnp.float32)],
        compiler_params=pltpu.CompilerParams(vmem_limit_bytes=4 * MIB + 2 * rows * depth),
        cost_estimate=pl.CostEstimate(flops=4 * rows * depth * width, bytes_accessed=0, transcendentals=rows * width),
        name="up_project",
    )(*parts, gate_weight, up_weight)


def down_kernel(blocks, chips, scale, flip, a_ref, b_ref, clip_ref, weight_ref, *refs):
    outs, (rows_ref, mixed_ref) = refs[:-2], refs[-2:]
    half = a_ref.shape[1]
    rows_ref[:, :half] = a_ref[...].astype(jnp.float32)
    rows_ref[:, half:] = b_ref[...].astype(jnp.float32)
    parts = [rows_ref[:, b * BLOCK : (b + 1) * BLOCK] for b in range(blocks)]
    span = 1
    while span < blocks:
        parts = [
            parts[b] + parts[b ^ span] if b & span == 0 else parts[b ^ span] - parts[b] for b in range(blocks)
        ]
        span *= 2
    for b in range(blocks):
        lanes = slice(b * BLOCK, (b + 1) * BLOCK)
        limit = 127.0 * clip_ref[:, lanes]
        rows_ref[:, lanes] = jnp.clip(parts[b] * scale, -limit, limit)
    rows = rows_ref.shape[0]
    each = rows // chips
    me = lax.axis_index("hid")
    for chip in range(chips):
        spot = pl.multiple_of(ring_place(me // 2, chip + chips // 2, chips) * each, each)
        mixed_ref[chip * each : (chip + 1) * each, :] = rows_ref[pl.ds(spot, each), :].astype(jnp.bfloat16)
    wide = weight_ref.shape[1] // 2
    side = 1 - me % 2 if flip else me % 2
    lanes = pl.ds(pl.multiple_of(side * wide, wide), wide)
    product = jnp.dot(mixed_ref[...], weight_ref[:, lanes], preferred_element_type=jnp.float32)
    first = 0
    for out_ref in outs:
        out_ref[...] = product[first : first + out_ref.shape[0]].astype(jnp.bfloat16)
        first += out_ref.shape[0]


def down_project(a, b, clip_scale, weight, flip, chips, total):
    rows = a.shape[0]
    width, depth = weight.shape[0], weight.shape[1] // 2
    vmem = pl.BlockSpec(memory_space=pltpu.VMEM)
    outs = [
        jax.ShapeDtypeStruct((count, depth), jnp.bfloat16) for count in (rows // chips, rows - rows // chips)
    ]
    return pl.pallas_call(
        functools.partial(down_kernel, width // BLOCK, chips, total**-0.5, flip),
        out_shape=outs,
        in_specs=[vmem] * 4,
        out_specs=[vmem] * 2,
        scratch_shapes=[pltpu.VMEM((rows, width), jnp.float32), pltpu.VMEM((rows, width), jnp.bfloat16)],
        compiler_params=pltpu.CompilerParams(vmem_limit_bytes=8 * MIB),
        cost_estimate=pl.CostEstimate(flops=2 * rows * depth * width, bytes_accessed=0, transcendentals=0),
        name="down_project",
    )(a, b, clip_scale, weight)


def pick_kernel(even_ref, odd_ref, out_ref):
    core = lax.axis_index("hid") % 2

    @pl.when(core == 0)
    def _():
        out_ref[...] = even_ref[...]

    @pl.when(core != 0)
    def _():
        out_ref[...] = odd_ref[...]


def turn_kernel(mask, value_ref, other_ref, out_ref):
    sign = jnp.where(lax.axis_index("hid") & mask == 0, 1.0, -1.0).astype(jnp.float32)
    out_ref[...] = (other_ref[...].astype(jnp.float32) + sign * value_ref[...].astype(jnp.float32)).astype(jnp.bfloat16)


def both(body, first, second, name):
    vmem = pl.BlockSpec(memory_space=pltpu.VMEM)
    return pl.pallas_call(
        body,
        out_shape=jax.ShapeDtypeStruct(first.shape, first.dtype),
        in_specs=[vmem, vmem],
        out_specs=vmem,
        compiler_params=pltpu.CompilerParams(vmem_limit_bytes=2 * MIB),
        cost_estimate=pl.CostEstimate(flops=TURN, bytes_accessed=0, transcendentals=0),
        name=name,
    )(first, second)


def chunk(away, chips, own_ref, arrived_ref):
    rows = own_ref.shape[0] // (chips - 1)
    spot = (away + chips // 2 - 1) % chips
    at = slice(spot * rows, (spot + 1) * rows)
    return own_ref[at, :].astype(jnp.float32) + arrived_ref[at, :].astype(jnp.float32)


def sum_kernel(one_ref, two_ref, out_ref):
    out_ref[...] = (one_ref[...].astype(jnp.float32) + two_ref[...].astype(jnp.float32)).astype(jnp.bfloat16)


def relay_kernel(away, chips, core, arrived_in, own_ref, arrived_ref, out_ref):
    value = arrived_in[...].astype(jnp.float32)
    if core is not None:
        value = jnp.where(lax.axis_index("hid") % 2 == core, value, 0.0)
    out_ref[...] = (chunk(away, chips, own_ref, arrived_ref) + value).astype(jnp.bfloat16)


def last_kernel(chips, ahead_in, behind_in, own_ref, arrived_ref, keep_ref, give_ref, sum_ref):
    part = keep_ref.shape[0]
    core = lax.axis_index("hid") % 2
    sum_ref[...] = (
        chunk(0, chips, own_ref, arrived_ref) + ahead_in[...].astype(jnp.float32) + behind_in[...].astype(jnp.float32)
    )
    keep_ref[...] = sum_ref[pl.ds(pl.multiple_of(core * part, part), part), :]
    give_ref[...] = sum_ref[pl.ds(pl.multiple_of((1 - core) * part, part), part), :].astype(jnp.bfloat16)


def mix_kernel(tokens_ref, keep_ref, take_ref, out_ref):
    wide = keep_ref.shape[1]
    keep, take = keep_ref[...], take_ref[...].astype(jnp.float32)
    first = lax.axis_index("hid") % 2 == 0
    low, high = jnp.where(first, keep, take), jnp.where(first, take, keep)
    out_ref[:, :wide] = (tokens_ref[:, :wide].astype(jnp.float32) + low).astype(jnp.bfloat16)
    out_ref[:, wide:] = (tokens_ref[:, wide:].astype(jnp.float32) + high).astype(jnp.bfloat16)


def small(body, outs, operands, name, scratch=()):
    vmem = pl.BlockSpec(memory_space=pltpu.VMEM)
    return pl.pallas_call(
        body,
        out_shape=outs,
        in_specs=[vmem] * len(operands),
        out_specs=jax.tree.map(lambda _: vmem, outs),
        scratch_shapes=scratch,
        compiler_params=pltpu.CompilerParams(vmem_limit_bytes=4 * MIB),
        cost_estimate=pl.CostEstimate(flops=2 * operands[0].size, bytes_accessed=0, transcendentals=0),
        name=name,
    )(*operands)


def shards(count, tokens, norm_gain, gate_weight, up_weight, down_weight, clip_scale):
    chips = count // 2
    order = ring_of(chips)
    steps = chips // 2

    def hop(value, shift_even, shift_odd):
        pairs = []
        for at, c in enumerate(order):
            pairs.append((2 * c, 2 * order[(at + shift_even) % chips]))
            pairs.append((2 * c + 1, 2 * order[(at + shift_odd) % chips] + 1))
        return lax.ppermute(value, "hid", pairs)

    def right(value):
        return hop(value, 1, 1)

    def left(value):
        return hop(value, -1, -1)

    def cross(value, mask=1):
        return lax.ppermute(value, "hid", [(d, d ^ mask) for d in range(count)])

    normed = normalize(tokens, norm_gain)
    width = gate_weight.shape[1]
    pieces = width // max(BLOCK, width // 2)
    mine, shifts = [normed], [0]
    ahead = behind = normed
    for step in range(1, steps):
        ahead, behind = right(ahead), left(behind)
        mine += [ahead, behind]
        shifts += [-step, step]
    mine.append(hop(both(pick_kernel, ahead, behind, "pick"), 1, -1))
    shifts.append(steps)
    parts = [block for own in mine for block in (own, cross(own))]

    half_b, joined = up_project(shifts, parts, gate_weight, up_weight, pieces - 1, pieces)
    if pieces == 1:
        half_a, half_b = jnp.split(half_b, 2, axis=1)
    else:
        (half_a,) = up_project(shifts, [joined], gate_weight, up_weight, 0, pieces)

    def turn(value, mask, *others):
        return both(functools.partial(turn_kernel, mask), value, once(cross(value, mask), *others), "turn")

    masks = [1 << bit for bit in range(count.bit_length() - 1)]
    for stage in range(len(masks)):
        first, second = masks[stage - 1], masks[stage]
        if stage == 0:
            half_b = turn(half_b, second)
            early = turn(half_b, masks[1])
            half_a = turn(half_a, first, half_b)
        elif stage == 1:
            half_b = early
            half_a = turn(half_a, first, early)
        elif stage < len(masks) - 1:
            half_b = turn(half_b, second, half_a)
            half_a = turn(half_a, first, half_b)
        else:
            half_a = turn(half_a, first, half_b)
            half_b = turn(half_b, second, half_a)

    total = count * width
    limits = clip_scale.reshape(1, -1)
    theirs_far, theirs = down_project(half_a, half_b, limits, down_weight, True, chips, total)
    arrived_far = cross(theirs_far)
    own_far, own = down_project(half_a, half_b, limits, down_weight, False, chips, total)
    arrived = cross(once(theirs, own, arrived_far))
    rows, wide = own_far.shape
    part = jax.ShapeDtypeStruct((rows, wide), jnp.bfloat16)

    ahead = behind = hop(small(sum_kernel, part, (own_far, arrived_far), "far"), 1, -1)
    for away in range(steps - 1, 0, -1):
        cores = (0, 1) if away == steps - 1 else (None, None)
        ahead = small(
            functools.partial(relay_kernel, away, chips, cores[0]), part, (ahead, own, arrived), "relay"
        )
        behind = small(
            functools.partial(relay_kernel, -away, chips, cores[1]), part, (behind, own, arrived), "relay"
        )
        ahead, behind = right(ahead), left(behind)
    half = jax.ShapeDtypeStruct((rows // 2, wide), jnp.bfloat16)
    kept = jax.ShapeDtypeStruct((rows // 2, wide), jnp.float32)
    keep, give = small(
        functools.partial(last_kernel, chips),
        (kept, half),
        (ahead, behind, own, arrived),
        "last",
        [pltpu.VMEM((rows, wide), jnp.float32)],
    )
    mixed = jax.ShapeDtypeStruct(tokens.shape, tokens.dtype)
    return small(mix_kernel, mixed, (tokens, keep, cross(give)), "mix")


def solution(mesh):
    in_specs = (
        P(("groups", "hid"), None),
        P(),
        P(None, "hid"),
        P(None, "hid"),
        P("hid", None),
        P("hid"),
    )
    out_specs = P(("groups", "hid"), None)
    body = functools.partial(shards, mesh.shape["hid"])
    return jax.shard_map(body, mesh=mesh, in_specs=in_specs, out_specs=out_specs, check_vma=False)
```

```python
import functools

import jax
import jax.numpy as jnp
from jax import lax
from jax.experimental import pallas as pl
from jax.experimental.pallas import tpu as pltpu
from jax.sharding import PartitionSpec as P

BLOCK = 256
MIB = 1 << 20
TURN = 2_000_000_000
COST = 20_000_000_000


def hadamard(count):
    rows = lax.broadcasted_iota(jnp.int32, (count, count), 0)
    cols = lax.broadcasted_iota(jnp.int32, (count, count), 1)
    both = rows & cols
    parity = jnp.zeros((count, count), jnp.int32)
    for place in range(max(count.bit_length(), 1)):
        parity = parity + (both >> place & 1)
    return jnp.where(parity % 2 == 0, 1.0, -1.0).astype(jnp.bfloat16)


def normalize_kernel(rows_hbm, gain_hbm, out_ref, rows_ref, gain_ref, sems):
    copies = [
        pltpu.make_async_copy(rows_hbm, rows_ref, sems.at[0]),
        pltpu.make_async_copy(gain_hbm, gain_ref, sems.at[1]),
    ]
    for copy in copies:
        copy.start()
    for copy in copies:
        copy.wait()
    values = rows_ref[...].astype(jnp.float32)
    inverse = lax.rsqrt(jnp.mean(values * values, axis=-1, keepdims=True) + 1e-05)
    out_ref[...] = (values * inverse * gain_ref[...]).astype(jnp.bfloat16)


def in_hbm(value):
    return pltpu.with_memory_space_constraint(value, pltpu.HBM)


def normalize(rows_in, norm_gain):
    hbm = pl.BlockSpec(memory_space=pltpu.HBM)
    gain = norm_gain.reshape(1, -1)
    return pl.pallas_call(
        normalize_kernel,
        out_shape=jax.ShapeDtypeStruct(rows_in.shape, jnp.bfloat16),
        in_specs=[hbm, hbm],
        out_specs=pl.BlockSpec(memory_space=pltpu.VMEM),
        scratch_shapes=[
            pltpu.VMEM(rows_in.shape, rows_in.dtype),
            pltpu.VMEM(gain.shape, gain.dtype),
            pltpu.SemaphoreType.DMA((2,)),
        ],
        compiler_params=pltpu.CompilerParams(vmem_limit_bytes=4 * MIB),
        cost_estimate=pl.CostEstimate(flops=COST, bytes_accessed=4 * rows_in.size, transcendentals=0),
        name="normalize",
    )(in_hbm(rows_in), in_hbm(gain))


def ring_of(chips):
    return list(range(0, chips, 2)) + list(range(chips - 1, 0, -2))


def ring_place(chip, shift, chips):
    spot = jnp.where(chip % 2 == 0, chip // 2, chips - 1 - (chip - 1) // 2)
    spot = (spot + shift) % chips
    return jnp.where(spot < (chips + 1) // 2, 2 * spot, 2 * (chips - spot) - 1)


def once(value, *others):
    return lax.optimization_barrier((value, *others))[0]


def join_rows(parts, out_ref):
    own = parts[0].shape[0]
    for pair in range(len(parts) // 2):
        both = [parts[2 * pair + k][...].astype(jnp.float32) for k in range(2)]
        out_ref[2 * own * pair : 2 * own * (pair + 1), :] = jnp.concatenate(both, axis=0).astype(jnp.bfloat16)


def up_kernel(shifts, first, lanes_of, *refs):
    count = 2 * len(shifts)
    if first:
        gate_ref, up_ref, out_ref, rows_ref, hidden_ref = refs[count:]
        join_rows(refs[:count], rows_ref)
    else:
        rows_ref, gate_ref, up_ref, out_ref, hidden_ref = refs
    me = lax.axis_index("hid")
    chip, core = me // 2, me % 2
    own = rows_ref.shape[0] // count
    turn = hadamard(BLOCK)
    values = rows_ref[...]
    gate = jnp.dot(values, gate_ref[:, lanes_of], preferred_element_type=jnp.float32)
    up = jnp.dot(values, up_ref[:, lanes_of], preferred_element_type=jnp.float32)
    hidden = gate / (1.0 + jnp.exp(-gate)) * up
    high = hidden.astype(jnp.bfloat16)
    low = (hidden - high.astype(jnp.float32)).astype(jnp.bfloat16)
    for block in range(gate.shape[1] // BLOCK):
        lanes = slice(block * BLOCK, (block + 1) * BLOCK)
        turned = jnp.dot(high[:, lanes], turn, preferred_element_type=jnp.float32) + jnp.dot(
            low[:, lanes], turn, preferred_element_type=jnp.float32
        )
        for part in range(count):
            there = 2 * ring_place(chip, shifts[part // 2], count // 2)
            there = there + core if part % 2 == 0 else there + 1 - core
            spot = pl.multiple_of(there * own, own)
            hidden_ref[pl.ds(spot, own), lanes] = turned[part * own : (part + 1) * own]
    out_ref[...] = hidden_ref[...].astype(jnp.bfloat16)


def up_project(shifts, parts, gate_weight, up_weight, at, pieces):
    first = len(parts) > 1
    depth, width = gate_weight.shape
    width = width // pieces
    rows = sum(part.shape[0] for part in parts)
    vmem = pl.BlockSpec(memory_space=pltpu.VMEM)
    outs = [jax.ShapeDtypeStruct((rows, width), jnp.bfloat16)]
    if first:
        outs.append(jax.ShapeDtypeStruct((rows, depth), jnp.bfloat16))
    return pl.pallas_call(
        functools.partial(up_kernel, shifts, first, slice(at * width, (at + 1) * width)),
        out_shape=outs,
        in_specs=[vmem] * (len(parts) + 2),
        out_specs=[vmem] * len(outs),
        scratch_shapes=[pltpu.VMEM((rows, width), jnp.float32)],
        compiler_params=pltpu.CompilerParams(vmem_limit_bytes=4 * MIB + 2 * rows * depth),
        cost_estimate=pl.CostEstimate(flops=4 * rows * depth * width, bytes_accessed=0, transcendentals=rows * width),
        name="up_project",
    )(*parts, gate_weight, up_weight)


def ring_order(chips):
    steps = chips // 2
    early = [steps - 1, chips + 1 - steps, steps]
    return early + [away for away in range(chips) if away not in early]


EARLY = 3


def down_kernel(blocks, chips, scale, flip, a_ref, b_ref, clip_ref, weight_ref, *refs):
    outs, (rows_ref, mixed_ref) = refs[:-2], refs[-2:]
    half = a_ref.shape[1]
    rows_ref[:, :half] = a_ref[...].astype(jnp.float32)
    rows_ref[:, half:] = b_ref[...].astype(jnp.float32)
    parts = [rows_ref[:, b * BLOCK : (b + 1) * BLOCK] for b in range(blocks)]
    span = 1
    while span < blocks:
        parts = [
            parts[b] + parts[b ^ span] if b & span == 0 else parts[b ^ span] - parts[b] for b in range(blocks)
        ]
        span *= 2
    for b in range(blocks):
        lanes = slice(b * BLOCK, (b + 1) * BLOCK)
        limit = 127.0 * clip_ref[:, lanes]
        rows_ref[:, lanes] = jnp.clip(parts[b] * scale, -limit, limit)
    rows = rows_ref.shape[0]
    each = rows // chips
    me = lax.axis_index("hid")
    for chip in range(chips):
        spot = pl.multiple_of(ring_place(me // 2, ring_order(chips)[chip], chips) * each, each)
        mixed_ref[chip * each : (chip + 1) * each, :] = rows_ref[pl.ds(spot, each), :].astype(jnp.bfloat16)
    wide = weight_ref.shape[1] // 2
    side = 1 - me % 2 if flip else me % 2
    lanes = pl.ds(pl.multiple_of(side * wide, wide), wide)
    product = jnp.dot(mixed_ref[...], weight_ref[:, lanes], preferred_element_type=jnp.float32)
    first = 0
    for out_ref in outs:
        out_ref[...] = product[first : first + out_ref.shape[0]].astype(jnp.bfloat16)
        first += out_ref.shape[0]


def down_project(a, b, clip_scale, weight, flip, chips, total):
    rows = a.shape[0]
    width, depth = weight.shape[0], weight.shape[1] // 2
    vmem = pl.BlockSpec(memory_space=pltpu.VMEM)
    outs = [
        jax.ShapeDtypeStruct((count, depth), jnp.bfloat16) for count in (EARLY * (rows // chips), rows - EARLY * (rows // chips))
    ]
    return pl.pallas_call(
        functools.partial(down_kernel, width // BLOCK, chips, total**-0.5, flip),
        out_shape=outs,
        in_specs=[vmem] * 4,
        out_specs=[vmem] * 2,
        scratch_shapes=[pltpu.VMEM((rows, width), jnp.float32), pltpu.VMEM((rows, width), jnp.bfloat16)],
        compiler_params=pltpu.CompilerParams(vmem_limit_bytes=8 * MIB),
        cost_estimate=pl.CostEstimate(flops=2 * rows * depth * width, bytes_accessed=0, transcendentals=0),
        name="down_project",
    )(a, b, clip_scale, weight)


def pick_kernel(even_ref, odd_ref, out_ref):
    core = lax.axis_index("hid") % 2

    @pl.when(core == 0)
    def _():
        out_ref[...] = even_ref[...]

    @pl.when(core != 0)
    def _():
        out_ref[...] = odd_ref[...]


def turn_kernel(mask, value_ref, other_ref, out_ref):
    sign = jnp.where(lax.axis_index("hid") & mask == 0, 1.0, -1.0).astype(jnp.float32)
    out_ref[...] = (other_ref[...].astype(jnp.float32) + sign * value_ref[...].astype(jnp.float32)).astype(jnp.bfloat16)


def both(body, first, second, name):
    vmem = pl.BlockSpec(memory_space=pltpu.VMEM)
    return pl.pallas_call(
        body,
        out_shape=jax.ShapeDtypeStruct(first.shape, first.dtype),
        in_specs=[vmem, vmem],
        out_specs=vmem,
        compiler_params=pltpu.CompilerParams(vmem_limit_bytes=2 * MIB),
        cost_estimate=pl.CostEstimate(flops=TURN, bytes_accessed=0, transcendentals=0),
        name=name,
    )(first, second)


def chunk(away, chips, own_ref, arrived_ref):
    spot = ring_order(chips).index(away % chips)
    if spot < EARLY:
        rows = own_ref.shape[0] // EARLY
    else:
        rows, spot = own_ref.shape[0] // (chips - EARLY), spot - EARLY
    at = slice(spot * rows, (spot + 1) * rows)
    return own_ref[at, :].astype(jnp.float32) + arrived_ref[at, :].astype(jnp.float32)


def sum_kernel(away, chips, own_ref, arrived_ref, out_ref):
    out_ref[...] = chunk(away, chips, own_ref, arrived_ref).astype(jnp.bfloat16)


def relay_kernel(away, chips, core, own_ref, arrived_ref, *refs):
    out_ref = refs[-1]
    value = chunk(away, chips, own_ref, arrived_ref) + refs[0][...].astype(jnp.float32)
    if len(refs) == 3:
        value = value + jnp.where(lax.axis_index("hid") % 2 == core, refs[1][...].astype(jnp.float32), 0.0)
    out_ref[...] = value.astype(jnp.bfloat16)


def last_kernel(chips, ahead_in, behind_in, own_ref, arrived_ref, keep_ref, give_ref, sum_ref):
    part = keep_ref.shape[0]
    core = lax.axis_index("hid") % 2
    sum_ref[...] = (
        chunk(0, chips, own_ref, arrived_ref) + ahead_in[...].astype(jnp.float32) + behind_in[...].astype(jnp.float32)
    )
    keep_ref[...] = sum_ref[pl.ds(pl.multiple_of(core * part, part), part), :]
    give_ref[...] = sum_ref[pl.ds(pl.multiple_of((1 - core) * part, part), part), :].astype(jnp.bfloat16)


def mix_kernel(tokens_ref, keep_ref, take_ref, out_ref):
    wide = keep_ref.shape[1]
    keep, take = keep_ref[...], take_ref[...].astype(jnp.float32)
    first = lax.axis_index("hid") % 2 == 0
    low, high = jnp.where(first, keep, take), jnp.where(first, take, keep)
    out_ref[:, :wide] = (tokens_ref[:, :wide].astype(jnp.float32) + low).astype(jnp.bfloat16)
    out_ref[:, wide:] = (tokens_ref[:, wide:].astype(jnp.float32) + high).astype(jnp.bfloat16)


def small(body, outs, operands, name, scratch=()):
    vmem = pl.BlockSpec(memory_space=pltpu.VMEM)
    return pl.pallas_call(
        body,
        out_shape=outs,
        in_specs=[vmem] * len(operands),
        out_specs=jax.tree.map(lambda _: vmem, outs),
        scratch_shapes=scratch,
        compiler_params=pltpu.CompilerParams(vmem_limit_bytes=4 * MIB),
        cost_estimate=pl.CostEstimate(flops=2 * operands[0].size, bytes_accessed=0, transcendentals=0),
        name=name,
    )(*operands)


def shards(count, tokens, norm_gain, gate_weight, up_weight, down_weight, clip_scale):
    chips = count // 2
    order = ring_of(chips)
    steps = chips // 2

    def hop(value, shift_even, shift_odd):
        pairs = []
        for at, c in enumerate(order):
            pairs.append((2 * c, 2 * order[(at + shift_even) % chips]))
            pairs.append((2 * c + 1, 2 * order[(at + shift_odd) % chips] + 1))
        return lax.ppermute(value, "hid", pairs)

    def right(value):
        return hop(value, 1, 1)

    def left(value):
        return hop(value, -1, -1)

    def cross(value, mask=1):
        return lax.ppermute(value, "hid", [(d, d ^ mask) for d in range(count)])

    normed = normalize(tokens, norm_gain)
    width = gate_weight.shape[1]
    pieces = width // max(BLOCK, width // 2)
    mine, shifts = [normed], [0]
    ahead = behind = normed
    for step in range(1, steps):
        if step == steps - 1:
            far = hop(both(pick_kernel, ahead, behind, "pick"), 2, -2)
        ahead, behind = right(ahead), left(behind)
        mine += [ahead, behind]
        shifts += [-step, step]
    mine.append(far)
    shifts.append(steps)
    parts = [block for own in mine for block in (own, cross(own))]

    half_b, joined = up_project(shifts, parts, gate_weight, up_weight, pieces - 1, pieces)
    if pieces == 1:
        half_a, half_b = jnp.split(half_b, 2, axis=1)
    else:
        (half_a,) = up_project(shifts, [joined], gate_weight, up_weight, 0, pieces)

    def turn(value, mask, *others):
        return both(functools.partial(turn_kernel, mask), value, once(cross(value, mask), *others), "turn")

    masks = [1 << bit for bit in range(count.bit_length() - 1)]
    for stage in range(len(masks)):
        first, second = masks[stage - 1], masks[stage]
        if stage == 0:
            half_b = turn(half_b, second)
            early = turn(half_b, masks[1])
            half_a = turn(half_a, first, half_b)
        elif stage == 1:
            half_b = early
            half_a = turn(half_a, first, early)
        elif stage < len(masks) - 1:
            half_b = turn(half_b, second, half_a)
            half_a = turn(half_a, first, half_b)
        else:
            half_a = turn(half_a, first, half_b)
            half_b = turn(half_b, second, half_a)

    total = count * width
    limits = clip_scale.reshape(1, -1)
    theirs_early, theirs = down_project(half_a, half_b, limits, down_weight, True, chips, total)
    arrived_early = cross(theirs_early)
    own_early, own = down_project(half_a, half_b, limits, down_weight, False, chips, total)
    arrived = cross(once(theirs, own, arrived_early))
    rows, wide = own_early.shape[0] // EARLY, own_early.shape[1]
    part = jax.ShapeDtypeStruct((rows, wide), jnp.bfloat16)

    first = [
        small(functools.partial(sum_kernel, away, chips), part, (own_early, arrived_early), "sum")
        for away in (steps - 1, 1 - steps, steps)
    ]
    ahead, behind, far = right(first[0]), left(first[1]), hop(first[2], 2, -2)
    for away in range(steps - 2, 0, -1):
        more = (far,) if away == steps - 2 else ()
        ahead = small(
            functools.partial(relay_kernel, away, chips, 0), part, (own, arrived, ahead, *more), "relay"
        )
        behind = small(
            functools.partial(relay_kernel, -away, chips, 1), part, (own, arrived, behind, *more), "relay"
        )
        ahead, behind = right(ahead), left(behind)
    half = jax.ShapeDtypeStruct((rows // 2, wide), jnp.bfloat16)
    kept = jax.ShapeDtypeStruct((rows // 2, wide), jnp.float32)
    keep, give = small(
        functools.partial(last_kernel, chips),
        (kept, half),
        (ahead, behind, own, arrived),
        "last",
        [pltpu.VMEM((rows, wide), jnp.float32)],
    )
    mixed = jax.ShapeDtypeStruct(tokens.shape, tokens.dtype)
    return small(mix_kernel, mixed, (tokens, keep, cross(give)), "mix")


def solution(mesh):
    in_specs = (
        P(("groups", "hid"), None),
        P(),
        P(None, "hid"),
        P(None, "hid"),
        P("hid", None),
        P("hid"),
    )
    out_specs = P(("groups", "hid"), None)
    body = functools.partial(shards, mesh.shape["hid"])
    return jax.shard_map(body, mesh=mesh, in_specs=in_specs, out_specs=out_specs, check_vma=False)
```

```python
import functools

import jax
import jax.numpy as jnp
from jax import lax
from jax.experimental import pallas as pl
from jax.experimental.pallas import tpu as pltpu
from jax.sharding import PartitionSpec as P

BLOCK = 256
MIB = 1 << 20
TURN = 2_000_000_000
COST = 20_000_000_000


def hadamard(count):
    rows = lax.broadcasted_iota(jnp.int32, (count, count), 0)
    cols = lax.broadcasted_iota(jnp.int32, (count, count), 1)
    both = rows & cols
    parity = jnp.zeros((count, count), jnp.int32)
    for place in range(max(count.bit_length(), 1)):
        parity = parity + (both >> place & 1)
    return jnp.where(parity % 2 == 0, 1.0, -1.0).astype(jnp.bfloat16)


def normalize_kernel(rows_hbm, gain_hbm, out_ref, rows_ref, gain_ref, sems):
    copies = [
        pltpu.make_async_copy(rows_hbm, rows_ref, sems.at[0]),
        pltpu.make_async_copy(gain_hbm, gain_ref, sems.at[1]),
    ]
    for copy in copies:
        copy.start()
    for copy in copies:
        copy.wait()
    values = rows_ref[...].astype(jnp.float32)
    inverse = lax.rsqrt(jnp.mean(values * values, axis=-1, keepdims=True) + 1e-05)
    out_ref[...] = (values * inverse * gain_ref[...]).astype(jnp.bfloat16)


def in_hbm(value):
    return pltpu.with_memory_space_constraint(value, pltpu.HBM)


def normalize(rows_in, norm_gain):
    hbm = pl.BlockSpec(memory_space=pltpu.HBM)
    gain = norm_gain.reshape(1, -1)
    return pl.pallas_call(
        normalize_kernel,
        out_shape=jax.ShapeDtypeStruct(rows_in.shape, jnp.bfloat16),
        in_specs=[hbm, hbm],
        out_specs=pl.BlockSpec(memory_space=pltpu.VMEM),
        scratch_shapes=[
            pltpu.VMEM(rows_in.shape, rows_in.dtype),
            pltpu.VMEM(gain.shape, gain.dtype),
            pltpu.SemaphoreType.DMA((2,)),
        ],
        compiler_params=pltpu.CompilerParams(vmem_limit_bytes=4 * MIB),
        cost_estimate=pl.CostEstimate(flops=COST, bytes_accessed=4 * rows_in.size, transcendentals=0),
        name="normalize",
    )(in_hbm(rows_in), in_hbm(gain))


def ring_of(chips):
    return list(range(0, chips, 2)) + list(range(chips - 1, 0, -2))


def ring_place(chip, shift, chips):
    spot = jnp.where(chip % 2 == 0, chip // 2, chips - 1 - (chip - 1) // 2)
    spot = (spot + shift) % chips
    return jnp.where(spot < (chips + 1) // 2, 2 * spot, 2 * (chips - spot) - 1)


def once(value, *others):
    return lax.optimization_barrier((value, *others))[0]


def join_rows(parts, out_ref):
    own = parts[0].shape[0]
    for pair in range(len(parts) // 2):
        both = [parts[2 * pair + k][...].astype(jnp.float32) for k in range(2)]
        out_ref[2 * own * pair : 2 * own * (pair + 1), :] = jnp.concatenate(both, axis=0).astype(jnp.bfloat16)


def up_kernel(shifts, first, lanes_of, *refs):
    count = 2 * len(shifts)
    if first:
        gate_ref, up_ref, out_ref, rows_ref, hidden_ref = refs[count:]
        join_rows(refs[:count], rows_ref)
    else:
        rows_ref, gate_ref, up_ref, out_ref, hidden_ref = refs
    me = lax.axis_index("hid")
    chip, core = me // 2, me % 2
    own = rows_ref.shape[0] // count
    turn = hadamard(BLOCK)
    values = rows_ref[...]
    gate = jnp.dot(values, gate_ref[:, lanes_of], preferred_element_type=jnp.float32)
    up = jnp.dot(values, up_ref[:, lanes_of], preferred_element_type=jnp.float32)
    hidden = gate / (1.0 + jnp.exp(-gate)) * up
    high = hidden.astype(jnp.bfloat16)
    low = (hidden - high.astype(jnp.float32)).astype(jnp.bfloat16)
    for block in range(gate.shape[1] // BLOCK):
        lanes = slice(block * BLOCK, (block + 1) * BLOCK)
        turned = jnp.dot(high[:, lanes], turn, preferred_element_type=jnp.float32) + jnp.dot(
            low[:, lanes], turn, preferred_element_type=jnp.float32
        )
        for part in range(count):
            there = 2 * ring_place(chip, shifts[part // 2], count // 2)
            there = there + core if part % 2 == 0 else there + 1 - core
            spot = pl.multiple_of(there * own, own)
            hidden_ref[pl.ds(spot, own), lanes] = turned[part * own : (part + 1) * own]
    out_ref[...] = hidden_ref[...].astype(jnp.bfloat16)


def up_project(shifts, parts, gate_weight, up_weight, at, pieces):
    first = len(parts) > 1
    depth, width = gate_weight.shape
    width = width // pieces
    rows = sum(part.shape[0] for part in parts)
    vmem = pl.BlockSpec(memory_space=pltpu.VMEM)
    outs = [jax.ShapeDtypeStruct((rows, width), jnp.bfloat16)]
    if first:
        outs.append(jax.ShapeDtypeStruct((rows, depth), jnp.bfloat16))
    return pl.pallas_call(
        functools.partial(up_kernel, shifts, first, slice(at * width, (at + 1) * width)),
        out_shape=outs,
        in_specs=[vmem] * (len(parts) + 2),
        out_specs=[vmem] * len(outs),
        scratch_shapes=[pltpu.VMEM((rows, width), jnp.float32)],
        compiler_params=pltpu.CompilerParams(vmem_limit_bytes=4 * MIB + 2 * rows * depth),
        cost_estimate=pl.CostEstimate(flops=4 * rows * depth * width, bytes_accessed=0, transcendentals=rows * width),
        name="up_project",
    )(*parts, gate_weight, up_weight)


def ring_order(chips):
    steps = chips // 2
    early = [steps - 1, chips + 1 - steps, steps]
    return early + [away for away in range(chips) if away not in early]


EARLY = 3


def down_kernel(blocks, chips, scale, flip, a_ref, b_ref, clip_ref, weight_ref, *refs):
    outs, (rows_ref, mixed_ref) = refs[:-2], refs[-2:]
    half = a_ref.shape[1]
    rows_ref[:, :half] = a_ref[...].astype(jnp.float32)
    rows_ref[:, half:] = b_ref[...].astype(jnp.float32)
    parts = [rows_ref[:, b * BLOCK : (b + 1) * BLOCK] for b in range(blocks)]
    span = 1
    while span < blocks:
        parts = [
            parts[b] + parts[b ^ span] if b & span == 0 else parts[b ^ span] - parts[b] for b in range(blocks)
        ]
        span *= 2
    for b in range(blocks):
        lanes = slice(b * BLOCK, (b + 1) * BLOCK)
        limit = 127.0 * clip_ref[:, lanes]
        rows_ref[:, lanes] = jnp.clip(parts[b] * scale, -limit, limit)
    rows = rows_ref.shape[0]
    each = rows // chips
    me = lax.axis_index("hid")
    for chip in range(chips):
        spot = pl.multiple_of(ring_place(me // 2, ring_order(chips)[chip], chips) * each, each)
        mixed_ref[chip * each : (chip + 1) * each, :] = rows_ref[pl.ds(spot, each), :].astype(jnp.bfloat16)
    wide = weight_ref.shape[1] // 2
    side = 1 - me % 2 if flip else me % 2
    lanes = pl.ds(pl.multiple_of(side * wide, wide), wide)
    product = jnp.dot(mixed_ref[...], weight_ref[:, lanes], preferred_element_type=jnp.float32)
    first = 0
    for out_ref in outs:
        out_ref[...] = product[first : first + out_ref.shape[0]].astype(jnp.bfloat16)
        first += out_ref.shape[0]


def down_project(a, b, clip_scale, weight, flip, chips, total):
    rows = a.shape[0]
    width, depth = weight.shape[0], weight.shape[1] // 2
    vmem = pl.BlockSpec(memory_space=pltpu.VMEM)
    outs = [
        jax.ShapeDtypeStruct((count, depth), jnp.bfloat16) for count in (EARLY * (rows // chips), rows - EARLY * (rows // chips))
    ]
    return pl.pallas_call(
        functools.partial(down_kernel, width // BLOCK, chips, total**-0.5, flip),
        out_shape=outs,
        in_specs=[vmem] * 4,
        out_specs=[vmem] * 2,
        scratch_shapes=[pltpu.VMEM((rows, width), jnp.float32), pltpu.VMEM((rows, width), jnp.bfloat16)],
        compiler_params=pltpu.CompilerParams(vmem_limit_bytes=8 * MIB),
        cost_estimate=pl.CostEstimate(flops=2 * rows * depth * width, bytes_accessed=0, transcendentals=0),
        name="down_project",
    )(a, b, clip_scale, weight)


def pick_kernel(even_ref, odd_ref, out_ref):
    core = lax.axis_index("hid") % 2

    @pl.when(core == 0)
    def _():
        out_ref[...] = even_ref[...]

    @pl.when(core != 0)
    def _():
        out_ref[...] = odd_ref[...]


def turn_kernel(mask, value_ref, other_ref, out_ref):
    sign = jnp.where(lax.axis_index("hid") & mask == 0, 1.0, -1.0).astype(jnp.float32)
    out_ref[...] = (other_ref[...].astype(jnp.float32) + sign * value_ref[...].astype(jnp.float32)).astype(jnp.bfloat16)


def both(body, first, second, name, flops=TURN):
    vmem = pl.BlockSpec(memory_space=pltpu.VMEM)
    return pl.pallas_call(
        body,
        out_shape=jax.ShapeDtypeStruct(first.shape, first.dtype),
        in_specs=[vmem, vmem],
        out_specs=vmem,
        compiler_params=pltpu.CompilerParams(vmem_limit_bytes=2 * MIB),
        cost_estimate=pl.CostEstimate(flops=flops, bytes_accessed=0, transcendentals=0),
        name=name,
    )(first, second)


def chunk(away, chips, own_ref, arrived_ref):
    spot = ring_order(chips).index(away % chips)
    if spot < EARLY:
        rows = own_ref.shape[0] // EARLY
    else:
        rows, spot = own_ref.shape[0] // (chips - EARLY), spot - EARLY
    at = slice(spot * rows, (spot + 1) * rows)
    return own_ref[at, :].astype(jnp.float32) + arrived_ref[at, :].astype(jnp.float32)


def sum_kernel(away, chips, own_ref, arrived_ref, out_ref):
    out_ref[...] = chunk(away, chips, own_ref, arrived_ref).astype(jnp.bfloat16)


def relay_kernel(away, chips, core, own_ref, arrived_ref, *refs):
    out_ref = refs[-1]
    value = chunk(away, chips, own_ref, arrived_ref) + refs[0][...].astype(jnp.float32)
    if len(refs) == 3:
        value = value + jnp.where(lax.axis_index("hid") % 2 == core, refs[1][...].astype(jnp.float32), 0.0)
    out_ref[...] = value.astype(jnp.bfloat16)


def last_kernel(chips, ahead_in, behind_in, own_ref, arrived_ref, keep_ref, give_ref, sum_ref):
    part = keep_ref.shape[0]
    core = lax.axis_index("hid") % 2
    sum_ref[...] = (
        chunk(0, chips, own_ref, arrived_ref) + ahead_in[...].astype(jnp.float32) + behind_in[...].astype(jnp.float32)
    )
    keep_ref[...] = sum_ref[pl.ds(pl.multiple_of(core * part, part), part), :]
    give_ref[...] = sum_ref[pl.ds(pl.multiple_of((1 - core) * part, part), part), :].astype(jnp.bfloat16)


def mix_kernel(tokens_ref, keep_ref, take_ref, out_ref):
    wide = keep_ref.shape[1]
    keep, take = keep_ref[...], take_ref[...].astype(jnp.float32)
    first = lax.axis_index("hid") % 2 == 0
    low, high = jnp.where(first, keep, take), jnp.where(first, take, keep)
    out_ref[:, :wide] = (tokens_ref[:, :wide].astype(jnp.float32) + low).astype(jnp.bfloat16)
    out_ref[:, wide:] = (tokens_ref[:, wide:].astype(jnp.float32) + high).astype(jnp.bfloat16)


def small(body, outs, operands, name, scratch=()):
    vmem = pl.BlockSpec(memory_space=pltpu.VMEM)
    return pl.pallas_call(
        body,
        out_shape=outs,
        in_specs=[vmem] * len(operands),
        out_specs=jax.tree.map(lambda _: vmem, outs),
        scratch_shapes=scratch,
        compiler_params=pltpu.CompilerParams(vmem_limit_bytes=4 * MIB),
        cost_estimate=pl.CostEstimate(flops=2 * operands[0].size, bytes_accessed=0, transcendentals=0),
        name=name,
    )(*operands)


def shards(count, tokens, norm_gain, gate_weight, up_weight, down_weight, clip_scale):
    chips = count // 2
    order = ring_of(chips)
    steps = chips // 2

    def hop(value, shift_even, shift_odd):
        pairs = []
        for at, c in enumerate(order):
            pairs.append((2 * c, 2 * order[(at + shift_even) % chips]))
            pairs.append((2 * c + 1, 2 * order[(at + shift_odd) % chips] + 1))
        return lax.ppermute(value, "hid", pairs)

    def right(value):
        return hop(value, 1, 1)

    def left(value):
        return hop(value, -1, -1)

    def cross(value, mask=1):
        return lax.ppermute(value, "hid", [(d, d ^ mask) for d in range(count)])

    normed = normalize(tokens, norm_gain)
    width = gate_weight.shape[1]
    pieces = width // max(BLOCK, width // 2)
    mine, shifts = [normed], [0]
    ahead = behind = normed
    for step in range(1, steps):
        if step == steps - 1:
            far = hop(both(pick_kernel, ahead, behind, "pick"), 2, -2)
        ahead, behind = right(ahead), left(behind)
        mine += [ahead, behind]
        shifts += [-step, step]
    mine.append(far)
    shifts.append(steps)
    parts = [block for own in mine for block in (own, cross(own))]

    half_b, joined = up_project(shifts, parts, gate_weight, up_weight, pieces - 1, pieces)
    if pieces == 1:
        half_a, half_b = jnp.split(half_b, 2, axis=1)
    else:
        (half_a,) = up_project(shifts, [joined], gate_weight, up_weight, 0, pieces)

    def turn(value, mask, *others, flops=TURN):
        arrived = once(cross(value, mask), *others) if others else cross(value, mask)
        return both(functools.partial(turn_kernel, mask), value, arrived, "turn", flops)

    masks = [1 << bit for bit in range(count.bit_length() - 1)]
    top, first, second, *rest = masks[-1], masks[1], masks[0], *masks[2:-1]
    half_b = turn(half_b, first, half_a, flops=0)
    early = turn(half_b, second, flops=0)
    half_a = turn(half_a, top, early, flops=2 * TURN)
    half_b = early
    half_a = turn(half_a, second)
    for place, mask in enumerate(rest):
        half_b = turn(half_b, mask)
        half_a = turn(half_a, first if place == 0 else rest[place - 1], half_b)
    half_a = turn(half_a, rest[-1] if rest else first)
    half_b = turn(half_b, top)

    total = count * width
    limits = clip_scale.reshape(1, -1)
    theirs_early, theirs = down_project(half_a, half_b, limits, down_weight, True, chips, total)
    arrived_early = cross(theirs_early)
    own_early, own = down_project(half_a, half_b, limits, down_weight, False, chips, total)
    arrived = cross(once(theirs, own, arrived_early))
    rows, wide = own_early.shape[0] // EARLY, own_early.shape[1]
    part = jax.ShapeDtypeStruct((rows, wide), jnp.bfloat16)

    first = [
        small(functools.partial(sum_kernel, away, chips), part, (own_early, arrived_early), "sum")
        for away in (steps - 1, 1 - steps, steps)
    ]
    ahead, behind, far = right(first[0]), left(first[1]), hop(first[2], 2, -2)
    for away in range(steps - 2, 0, -1):
        more = (far,) if away == steps - 2 else ()
        ahead = small(
            functools.partial(relay_kernel, away, chips, 0), part, (own, arrived, ahead, *more), "relay"
        )
        behind = small(
            functools.partial(relay_kernel, -away, chips, 1), part, (own, arrived, behind, *more), "relay"
        )
        ahead, behind = right(ahead), left(behind)
    half = jax.ShapeDtypeStruct((rows // 2, wide), jnp.bfloat16)
    kept = jax.ShapeDtypeStruct((rows // 2, wide), jnp.float32)
    keep, give = small(
        functools.partial(last_kernel, chips),
        (kept, half),
        (ahead, behind, own, arrived),
        "last",
        [pltpu.VMEM((rows, wide), jnp.float32)],
    )
    mixed = jax.ShapeDtypeStruct(tokens.shape, tokens.dtype)
    return small(mix_kernel, mixed, (tokens, keep, cross(give)), "mix")


def solution(mesh):
    in_specs = (
        P(("groups", "hid"), None),
        P(),
        P(None, "hid"),
        P(None, "hid"),
        P("hid", None),
        P("hid"),
    )
    out_specs = P(("groups", "hid"), None)
    body = functools.partial(shards, mesh.shape["hid"])
    return jax.shard_map(body, mesh=mesh, in_specs=in_specs, out_specs=out_specs, check_vma=False)
```

```python
import functools

import jax
import jax.numpy as jnp
from jax import lax
from jax.experimental import pallas as pl
from jax.experimental.pallas import tpu as pltpu
from jax.sharding import PartitionSpec as P

BLOCK = 256
MIB = 1 << 20
OFFSETS = (3, 1, 0, 2)
TURN = 1_000_000_000
COST = 20_000_000_000


def hadamard(count):
    rows = lax.broadcasted_iota(jnp.int32, (count, count), 0)
    cols = lax.broadcasted_iota(jnp.int32, (count, count), 1)
    both = rows & cols
    parity = jnp.zeros((count, count), jnp.int32)
    for place in range(max(count.bit_length(), 1)):
        parity = parity + (both >> place & 1)
    return jnp.where(parity % 2 == 0, 1.0, -1.0).astype(jnp.bfloat16)


def normalize_kernel(rows_hbm, gain_hbm, out_ref, rows_ref, gain_ref, sems):
    copies = [
        pltpu.make_async_copy(rows_hbm, rows_ref, sems.at[0]),
        pltpu.make_async_copy(gain_hbm, gain_ref, sems.at[1]),
    ]
    for copy in copies:
        copy.start()
    for copy in copies:
        copy.wait()
    values = rows_ref[...].astype(jnp.float32)
    inverse = lax.rsqrt(jnp.mean(values * values, axis=-1, keepdims=True) + 1e-05)
    out_ref[...] = (values * inverse * gain_ref[...]).astype(jnp.bfloat16)


def in_hbm(value):
    return pltpu.with_memory_space_constraint(value, pltpu.HBM)


def normalize(rows_in, norm_gain):
    hbm = pl.BlockSpec(memory_space=pltpu.HBM)
    gain = norm_gain.reshape(1, -1)
    return pl.pallas_call(
        normalize_kernel,
        out_shape=jax.ShapeDtypeStruct(rows_in.shape, jnp.bfloat16),
        in_specs=[hbm, hbm],
        out_specs=pl.BlockSpec(memory_space=pltpu.VMEM),
        scratch_shapes=[
            pltpu.VMEM(rows_in.shape, rows_in.dtype),
            pltpu.VMEM(gain.shape, gain.dtype),
            pltpu.SemaphoreType.DMA((2,)),
        ],
        compiler_params=pltpu.CompilerParams(vmem_limit_bytes=4 * MIB),
        cost_estimate=pl.CostEstimate(flops=COST, bytes_accessed=4 * rows_in.size, transcendentals=0),
        name="normalize",
    )(in_hbm(rows_in), in_hbm(gain))


def ring_of(chips):
    return list(range(0, chips, 2)) + list(range(chips - 1, 0, -2))


def ring_place(chip, shift, chips):
    spot = jnp.where(chip % 2 == 0, chip // 2, chips - 1 - (chip - 1) // 2)
    spot = (spot + shift) % chips
    return jnp.where(spot < (chips + 1) // 2, 2 * spot, 2 * (chips - spot) - 1)


def once(value, *others):
    return lax.optimization_barrier((value, *others))[0]


def join_rows(parts, out_ref):
    own = parts[0].shape[0]
    for pair in range(len(parts) // 2):
        both = [parts[2 * pair + k][...].astype(jnp.float32) for k in range(2)]
        out_ref[2 * own * pair : 2 * own * (pair + 1), :] = jnp.concatenate(both, axis=0).astype(jnp.bfloat16)


def up_kernel(shifts, first, lanes_of, *refs):
    count = 2 * len(shifts)
    if first:
        gate_ref, up_ref, *outs, rows_ref, hidden_ref = refs[count:]
        join_rows(refs[:count], rows_ref)
    else:
        rows_ref, gate_ref, up_ref, *outs, hidden_ref = refs
    me = lax.axis_index("hid")
    chip, core = me // 2, me % 2
    own = rows_ref.shape[0] // count
    turn = hadamard(BLOCK)
    values = rows_ref[...]
    gate = jnp.dot(values, gate_ref[:, lanes_of], preferred_element_type=jnp.float32)
    up = jnp.dot(values, up_ref[:, lanes_of], preferred_element_type=jnp.float32)
    hidden = gate / (1.0 + jnp.exp(-gate)) * up
    high = hidden.astype(jnp.bfloat16)
    low = (hidden - high.astype(jnp.float32)).astype(jnp.bfloat16)
    for block in range(gate.shape[1] // BLOCK):
        lanes = slice(block * BLOCK, (block + 1) * BLOCK)
        turned = jnp.dot(high[:, lanes], turn, preferred_element_type=jnp.float32) + jnp.dot(
            low[:, lanes], turn, preferred_element_type=jnp.float32
        )
        for part in range(count):
            there = 2 * ring_place(chip, shifts[part // 2], count // 2)
            there = there + core if part % 2 == 0 else there + 1 - core
            spot = pl.multiple_of(there * own, own)
            hidden_ref[pl.ds(spot, own), lanes] = turned[part * own : (part + 1) * own]
    cols = outs[0].shape[1]
    for at, out_ref in enumerate(outs):
        out_ref[...] = hidden_ref[:, at * cols : (at + 1) * cols].astype(jnp.bfloat16)


def up_project(shifts, parts, gate_weight, up_weight, at, pieces):
    first = len(parts) > 1
    depth, width = gate_weight.shape
    width = width // pieces
    rows = sum(part.shape[0] for part in parts)
    vmem = pl.BlockSpec(memory_space=pltpu.VMEM)
    outs = [jax.ShapeDtypeStruct((rows, width // 2), jnp.bfloat16)] * 2
    if first:
        outs.append(jax.ShapeDtypeStruct((rows, depth), jnp.bfloat16))
    return pl.pallas_call(
        functools.partial(up_kernel, shifts, first, slice(at * width, (at + 1) * width)),
        out_shape=outs,
        in_specs=[vmem] * (len(parts) + 2),
        out_specs=[vmem] * len(outs),
        scratch_shapes=[pltpu.VMEM((rows, width), jnp.float32)],
        compiler_params=pltpu.CompilerParams(vmem_limit_bytes=4 * MIB + 2 * rows * depth),
        cost_estimate=pl.CostEstimate(flops=4 * rows * depth * width, bytes_accessed=0, transcendentals=rows * width),
        name="up_project",
    )(*parts, gate_weight, up_weight)


def ring_order(chips):
    steps = chips // 2
    early = [steps - 1, chips + 1 - steps, steps]
    return early + [away for away in range(chips) if away not in early]


EARLY = 3


def down_kernel(blocks, chips, scale, flip, clip_ref, weight_ref, *refs):
    slices, outs, (rows_ref, mixed_ref) = refs[:-4], refs[-4:-2], refs[-2:]
    cols = slices[0].shape[1]
    for at, slice_ref in enumerate(slices):
        rows_ref[:, at * cols : (at + 1) * cols] = slice_ref[...].astype(jnp.float32)
    parts = [rows_ref[:, b * BLOCK : (b + 1) * BLOCK] for b in range(blocks)]
    span = 1
    while span < blocks:
        parts = [
            parts[b] + parts[b ^ span] if b & span == 0 else parts[b ^ span] - parts[b] for b in range(blocks)
        ]
        span *= 2
    for b in range(blocks):
        lanes = slice(b * BLOCK, (b + 1) * BLOCK)
        limit = 127.0 * clip_ref[:, lanes]
        rows_ref[:, lanes] = jnp.clip(parts[b] * scale, -limit, limit)
    rows = rows_ref.shape[0]
    each = rows // chips
    me = lax.axis_index("hid")
    for chip in range(chips):
        spot = pl.multiple_of(ring_place(me // 2, ring_order(chips)[chip], chips) * each, each)
        mixed_ref[chip * each : (chip + 1) * each, :] = rows_ref[pl.ds(spot, each), :].astype(jnp.bfloat16)
    wide = weight_ref.shape[1] // 2
    side = 1 - me % 2 if flip else me % 2
    lanes = pl.ds(pl.multiple_of(side * wide, wide), wide)
    product = jnp.dot(mixed_ref[...], weight_ref[:, lanes], preferred_element_type=jnp.float32)
    first = 0
    for out_ref in outs:
        out_ref[...] = product[first : first + out_ref.shape[0]].astype(jnp.bfloat16)
        first += out_ref.shape[0]


def down_project(slices, clip_scale, weight, flip, chips, total):
    rows = slices[0].shape[0]
    width, depth = weight.shape[0], weight.shape[1] // 2
    vmem = pl.BlockSpec(memory_space=pltpu.VMEM)
    outs = [
        jax.ShapeDtypeStruct((count, depth), jnp.bfloat16) for count in (EARLY * (rows // chips), rows - EARLY * (rows // chips))
    ]
    return pl.pallas_call(
        functools.partial(down_kernel, width // BLOCK, chips, total**-0.5, flip),
        out_shape=outs,
        in_specs=[vmem] * (2 + len(slices)),
        out_specs=[vmem] * 2,
        scratch_shapes=[pltpu.VMEM((rows, width), jnp.float32), pltpu.VMEM((rows, width), jnp.bfloat16)],
        compiler_params=pltpu.CompilerParams(vmem_limit_bytes=8 * MIB),
        cost_estimate=pl.CostEstimate(flops=2 * rows * depth * width, bytes_accessed=0, transcendentals=0),
        name="down_project",
    )(clip_scale, weight, *slices)


def pick_kernel(even_ref, odd_ref, out_ref):
    core = lax.axis_index("hid") % 2

    @pl.when(core == 0)
    def _():
        out_ref[...] = even_ref[...]

    @pl.when(core != 0)
    def _():
        out_ref[...] = odd_ref[...]


def turn_kernel(mask, value_ref, other_ref, out_ref):
    sign = jnp.where(lax.axis_index("hid") & mask == 0, 1.0, -1.0).astype(jnp.float32)
    out_ref[...] = (other_ref[...].astype(jnp.float32) + sign * value_ref[...].astype(jnp.float32)).astype(jnp.bfloat16)


def both(body, first, second, name):
    vmem = pl.BlockSpec(memory_space=pltpu.VMEM)
    return pl.pallas_call(
        body,
        out_shape=jax.ShapeDtypeStruct(first.shape, first.dtype),
        in_specs=[vmem, vmem],
        out_specs=vmem,
        compiler_params=pltpu.CompilerParams(vmem_limit_bytes=2 * MIB),
        cost_estimate=pl.CostEstimate(flops=TURN, bytes_accessed=0, transcendentals=0),
        name=name,
    )(first, second)


def chunk(away, chips, own_ref, arrived_ref):
    spot = ring_order(chips).index(away % chips)
    if spot < EARLY:
        rows = own_ref.shape[0] // EARLY
    else:
        rows, spot = own_ref.shape[0] // (chips - EARLY), spot - EARLY
    at = slice(spot * rows, (spot + 1) * rows)
    return own_ref[at, :].astype(jnp.float32) + arrived_ref[at, :].astype(jnp.float32)


def sum_kernel(away, chips, own_ref, arrived_ref, out_ref):
    out_ref[...] = chunk(away, chips, own_ref, arrived_ref).astype(jnp.bfloat16)


def relay_kernel(away, chips, core, own_ref, arrived_ref, *refs):
    out_ref = refs[-1]
    value = chunk(away, chips, own_ref, arrived_ref) + refs[0][...].astype(jnp.float32)
    if len(refs) == 3:
        value = value + jnp.where(lax.axis_index("hid") % 2 == core, refs[1][...].astype(jnp.float32), 0.0)
    out_ref[...] = value.astype(jnp.bfloat16)


def last_kernel(chips, ahead_in, behind_in, own_ref, arrived_ref, keep_ref, give_ref, sum_ref):
    part = keep_ref.shape[0]
    core = lax.axis_index("hid") % 2
    sum_ref[...] = (
        chunk(0, chips, own_ref, arrived_ref) + ahead_in[...].astype(jnp.float32) + behind_in[...].astype(jnp.float32)
    )
    keep_ref[...] = sum_ref[pl.ds(pl.multiple_of(core * part, part), part), :]
    give_ref[...] = sum_ref[pl.ds(pl.multiple_of((1 - core) * part, part), part), :].astype(jnp.bfloat16)


def mix_kernel(tokens_ref, keep_ref, take_ref, out_ref):
    wide = keep_ref.shape[1]
    keep, take = keep_ref[...], take_ref[...].astype(jnp.float32)
    first = lax.axis_index("hid") % 2 == 0
    low, high = jnp.where(first, keep, take), jnp.where(first, take, keep)
    out_ref[:, :wide] = (tokens_ref[:, :wide].astype(jnp.float32) + low).astype(jnp.bfloat16)
    out_ref[:, wide:] = (tokens_ref[:, wide:].astype(jnp.float32) + high).astype(jnp.bfloat16)


def small(body, outs, operands, name, scratch=()):
    vmem = pl.BlockSpec(memory_space=pltpu.VMEM)
    return pl.pallas_call(
        body,
        out_shape=outs,
        in_specs=[vmem] * len(operands),
        out_specs=jax.tree.map(lambda _: vmem, outs),
        scratch_shapes=scratch,
        compiler_params=pltpu.CompilerParams(vmem_limit_bytes=4 * MIB),
        cost_estimate=pl.CostEstimate(flops=2 * operands[0].size, bytes_accessed=0, transcendentals=0),
        name=name,
    )(*operands)


def shards(count, tokens, norm_gain, gate_weight, up_weight, down_weight, clip_scale):
    chips = count // 2
    order = ring_of(chips)
    steps = chips // 2

    def hop(value, shift_even, shift_odd):
        pairs = []
        for at, c in enumerate(order):
            pairs.append((2 * c, 2 * order[(at + shift_even) % chips]))
            pairs.append((2 * c + 1, 2 * order[(at + shift_odd) % chips] + 1))
        return lax.ppermute(value, "hid", pairs)

    def right(value):
        return hop(value, 1, 1)

    def left(value):
        return hop(value, -1, -1)

    def cross(value, mask=1):
        return lax.ppermute(value, "hid", [(d, d ^ mask) for d in range(count)])

    normed = normalize(tokens, norm_gain)
    width = gate_weight.shape[1]
    pieces = width // max(BLOCK, width // 2)
    mine, shifts = [normed], [0]
    ahead = behind = normed
    for step in range(1, steps):
        if step == steps - 1:
            far = hop(both(pick_kernel, ahead, behind, "pick"), 2, -2)
        ahead, behind = right(ahead), left(behind)
        mine += [ahead, behind]
        shifts += [-step, step]
    mine.append(far)
    shifts.append(steps)
    parts = [block for own in mine for block in (own, cross(own))]

    *slices, joined = up_project(shifts, parts, gate_weight, up_weight, 0, pieces)
    for at in range(1, pieces):
        slices += up_project(shifts, [joined], gate_weight, up_weight, at, pieces)

    def turn(value, mask, *others):
        return both(functools.partial(turn_kernel, mask), value, once(cross(value, mask), *others), "turn")

    masks = [1 << bit for bit in range(count.bit_length() - 1)]
    for stage in range(len(masks)):
        for at in range(len(slices)):
            place = OFFSETS[at % 4] * len(masks) // 4 + stage
            slices[at] = turn(slices[at], masks[place % len(masks)])

    total = count * width
    limits = clip_scale.reshape(1, -1)
    theirs_early, theirs = down_project(slices, limits, down_weight, True, chips, total)
    arrived_early = cross(theirs_early)
    own_early, own = down_project(slices, limits, down_weight, False, chips, total)
    arrived = cross(once(theirs, own, arrived_early))
    rows, wide = own_early.shape[0] // EARLY, own_early.shape[1]
    part = jax.ShapeDtypeStruct((rows, wide), jnp.bfloat16)

    first = [
        small(functools.partial(sum_kernel, away, chips), part, (own_early, arrived_early), "sum")
        for away in (steps - 1, 1 - steps, steps)
    ]
    ahead, behind, far = right(first[0]), left(first[1]), hop(first[2], 2, -2)
    for away in range(steps - 2, 0, -1):
        more = (far,) if away == steps - 2 else ()
        ahead = small(
            functools.partial(relay_kernel, away, chips, 0), part, (own, arrived, ahead, *more), "relay"
        )
        behind = small(
            functools.partial(relay_kernel, -away, chips, 1), part, (own, arrived, behind, *more), "relay"
        )
        ahead, behind = right(ahead), left(behind)
    half = jax.ShapeDtypeStruct((rows // 2, wide), jnp.bfloat16)
    kept = jax.ShapeDtypeStruct((rows // 2, wide), jnp.float32)
    keep, give = small(
        functools.partial(last_kernel, chips),
        (kept, half),
        (ahead, behind, own, arrived),
        "last",
        [pltpu.VMEM((rows, wide), jnp.float32)],
    )
    mixed = jax.ShapeDtypeStruct(tokens.shape, tokens.dtype)
    return small(mix_kernel, mixed, (tokens, keep, cross(give)), "mix")


def solution(mesh):
    in_specs = (
        P(("groups", "hid"), None),
        P(),
        P(None, "hid"),
        P(None, "hid"),
        P("hid", None),
        P("hid"),
    )
    out_specs = P(("groups", "hid"), None)
    body = functools.partial(shards, mesh.shape["hid"])
    return jax.shard_map(body, mesh=mesh, in_specs=in_specs, out_specs=out_specs, check_vma=False)
```

```python
import functools

import jax
import jax.numpy as jnp
from jax import lax
from jax.experimental import pallas as pl
from jax.experimental.pallas import tpu as pltpu
from jax.sharding import PartitionSpec as P

BLOCK = 256
MIB = 1 << 20
OFFSETS = (3, 1, 0, 2)
TURN = 700_000_000
COST = 20_000_000_000


def hadamard(count):
    rows = lax.broadcasted_iota(jnp.int32, (count, count), 0)
    cols = lax.broadcasted_iota(jnp.int32, (count, count), 1)
    both = rows & cols
    parity = jnp.zeros((count, count), jnp.int32)
    for place in range(max(count.bit_length(), 1)):
        parity = parity + (both >> place & 1)
    return jnp.where(parity % 2 == 0, 1.0, -1.0).astype(jnp.bfloat16)


def normalize_kernel(rows_hbm, gain_hbm, out_ref, rows_ref, gain_ref, sems):
    copies = [
        pltpu.make_async_copy(rows_hbm, rows_ref, sems.at[0]),
        pltpu.make_async_copy(gain_hbm, gain_ref, sems.at[1]),
    ]
    for copy in copies:
        copy.start()
    for copy in copies:
        copy.wait()
    values = rows_ref[...].astype(jnp.float32)
    inverse = lax.rsqrt(jnp.mean(values * values, axis=-1, keepdims=True) + 1e-05)
    out_ref[...] = (values * inverse * gain_ref[...]).astype(jnp.bfloat16)


def in_hbm(value):
    return pltpu.with_memory_space_constraint(value, pltpu.HBM)


def normalize(rows_in, norm_gain):
    hbm = pl.BlockSpec(memory_space=pltpu.HBM)
    gain = norm_gain.reshape(1, -1)
    return pl.pallas_call(
        normalize_kernel,
        out_shape=jax.ShapeDtypeStruct(rows_in.shape, jnp.bfloat16),
        in_specs=[hbm, hbm],
        out_specs=pl.BlockSpec(memory_space=pltpu.VMEM),
        scratch_shapes=[
            pltpu.VMEM(rows_in.shape, rows_in.dtype),
            pltpu.VMEM(gain.shape, gain.dtype),
            pltpu.SemaphoreType.DMA((2,)),
        ],
        compiler_params=pltpu.CompilerParams(vmem_limit_bytes=4 * MIB),
        cost_estimate=pl.CostEstimate(flops=COST, bytes_accessed=4 * rows_in.size, transcendentals=0),
        name="normalize",
    )(in_hbm(rows_in), in_hbm(gain))


def ring_of(chips):
    return list(range(0, chips, 2)) + list(range(chips - 1, 0, -2))


def ring_place(chip, shift, chips):
    spot = jnp.where(chip % 2 == 0, chip // 2, chips - 1 - (chip - 1) // 2)
    spot = (spot + shift) % chips
    return jnp.where(spot < (chips + 1) // 2, 2 * spot, 2 * (chips - spot) - 1)


def once(value, *others):
    return lax.optimization_barrier((value, *others))[0]


def join_rows(parts, out_ref):
    own = parts[0].shape[0]
    for pair in range(len(parts) // 2):
        both = [parts[2 * pair + k][...].astype(jnp.float32) for k in range(2)]
        out_ref[2 * own * pair : 2 * own * (pair + 1), :] = jnp.concatenate(both, axis=0).astype(jnp.bfloat16)


def up_kernel(shifts, first, lanes_of, *refs):
    count = 2 * len(shifts)
    if first:
        gate_ref, up_ref, *outs, rows_ref, hidden_ref = refs[count:]
        join_rows(refs[:count], rows_ref)
    else:
        rows_ref, gate_ref, up_ref, *outs, hidden_ref = refs
    me = lax.axis_index("hid")
    chip, core = me // 2, me % 2
    own = rows_ref.shape[0] // count
    turn = hadamard(BLOCK)
    values = rows_ref[...]
    gate = jnp.dot(values, gate_ref[:, lanes_of], preferred_element_type=jnp.float32)
    up = jnp.dot(values, up_ref[:, lanes_of], preferred_element_type=jnp.float32)
    hidden = gate / (1.0 + jnp.exp(-gate)) * up
    high = hidden.astype(jnp.bfloat16)
    low = (hidden - high.astype(jnp.float32)).astype(jnp.bfloat16)
    for block in range(gate.shape[1] // BLOCK):
        lanes = slice(block * BLOCK, (block + 1) * BLOCK)
        turned = jnp.dot(high[:, lanes], turn, preferred_element_type=jnp.float32) + jnp.dot(
            low[:, lanes], turn, preferred_element_type=jnp.float32
        )
        for part in range(count):
            there = 2 * ring_place(chip, shifts[part // 2], count // 2)
            there = there + core if part % 2 == 0 else there + 1 - core
            spot = pl.multiple_of(there * own, own)
            hidden_ref[pl.ds(spot, own), lanes] = turned[part * own : (part + 1) * own]
    cols = outs[0].shape[1]
    for at, out_ref in enumerate(outs):
        out_ref[...] = hidden_ref[:, at * cols : (at + 1) * cols].astype(jnp.bfloat16)


def up_project(shifts, parts, gate_weight, up_weight, at, pieces):
    first = len(parts) > 1
    depth, width = gate_weight.shape
    width = width // pieces
    rows = sum(part.shape[0] for part in parts)
    vmem = pl.BlockSpec(memory_space=pltpu.VMEM)
    outs = [jax.ShapeDtypeStruct((rows, width // 2), jnp.bfloat16)] * 2
    if first:
        outs.append(jax.ShapeDtypeStruct((rows, depth), jnp.bfloat16))
    return pl.pallas_call(
        functools.partial(up_kernel, shifts, first, slice(at * width, (at + 1) * width)),
        out_shape=outs,
        in_specs=[vmem] * (len(parts) + 2),
        out_specs=[vmem] * len(outs),
        scratch_shapes=[pltpu.VMEM((rows, width), jnp.float32)],
        compiler_params=pltpu.CompilerParams(vmem_limit_bytes=4 * MIB + 2 * rows * depth),
        cost_estimate=pl.CostEstimate(flops=4 * rows * depth * width, bytes_accessed=0, transcendentals=rows * width),
        name="up_project",
    )(*parts, gate_weight, up_weight)


def ring_order(chips):
    steps = chips // 2
    early = [steps - 1, chips + 1 - steps, steps]
    return early + [away for away in range(chips) if away not in early]


EARLY = 3


def down_kernel(blocks, chips, scale, flip, clip_ref, weight_ref, *refs):
    slices, outs, (rows_ref, mixed_ref) = refs[:-4], refs[-4:-2], refs[-2:]
    cols = slices[0].shape[1]
    for at, slice_ref in enumerate(slices):
        rows_ref[:, at * cols : (at + 1) * cols] = slice_ref[...].astype(jnp.float32)
    parts = [rows_ref[:, b * BLOCK : (b + 1) * BLOCK] for b in range(blocks)]
    span = 1
    while span < blocks:
        parts = [
            parts[b] + parts[b ^ span] if b & span == 0 else parts[b ^ span] - parts[b] for b in range(blocks)
        ]
        span *= 2
    for b in range(blocks):
        lanes = slice(b * BLOCK, (b + 1) * BLOCK)
        limit = 127.0 * clip_ref[:, lanes]
        rows_ref[:, lanes] = jnp.clip(parts[b] * scale, -limit, limit)
    rows = rows_ref.shape[0]
    each = rows // chips
    me = lax.axis_index("hid")
    for chip in range(chips):
        spot = pl.multiple_of(ring_place(me // 2, ring_order(chips)[chip], chips) * each, each)
        mixed_ref[chip * each : (chip + 1) * each, :] = rows_ref[pl.ds(spot, each), :].astype(jnp.bfloat16)
    wide = weight_ref.shape[1] // 2
    side = 1 - me % 2 if flip else me % 2
    lanes = pl.ds(pl.multiple_of(side * wide, wide), wide)
    product = jnp.dot(mixed_ref[...], weight_ref[:, lanes], preferred_element_type=jnp.float32)
    first = 0
    for out_ref in outs:
        out_ref[...] = product[first : first + out_ref.shape[0]].astype(jnp.bfloat16)
        first += out_ref.shape[0]


def down_project(slices, clip_scale, weight, flip, chips, total):
    rows = slices[0].shape[0]
    width, depth = weight.shape[0], weight.shape[1] // 2
    vmem = pl.BlockSpec(memory_space=pltpu.VMEM)
    outs = [
        jax.ShapeDtypeStruct((count, depth), jnp.bfloat16) for count in (EARLY * (rows // chips), rows - EARLY * (rows // chips))
    ]
    return pl.pallas_call(
        functools.partial(down_kernel, width // BLOCK, chips, total**-0.5, flip),
        out_shape=outs,
        in_specs=[vmem] * (2 + len(slices)),
        out_specs=[vmem] * 2,
        scratch_shapes=[pltpu.VMEM((rows, width), jnp.float32), pltpu.VMEM((rows, width), jnp.bfloat16)],
        compiler_params=pltpu.CompilerParams(vmem_limit_bytes=8 * MIB),
        cost_estimate=pl.CostEstimate(flops=2 * rows * depth * width, bytes_accessed=0, transcendentals=0),
        name="down_project",
    )(clip_scale, weight, *slices)


def pick_kernel(even_ref, odd_ref, out_ref):
    core = lax.axis_index("hid") % 2

    @pl.when(core == 0)
    def _():
        out_ref[...] = even_ref[...]

    @pl.when(core != 0)
    def _():
        out_ref[...] = odd_ref[...]


def turn_kernel(mask, value_ref, other_ref, out_ref):
    sign = jnp.where(lax.axis_index("hid") & mask == 0, 1.0, -1.0).astype(jnp.float32)
    out_ref[...] = (other_ref[...].astype(jnp.float32) + sign * value_ref[...].astype(jnp.float32)).astype(jnp.bfloat16)


def both(body, first, second, name):
    vmem = pl.BlockSpec(memory_space=pltpu.VMEM)
    return pl.pallas_call(
        body,
        out_shape=jax.ShapeDtypeStruct(first.shape, first.dtype),
        in_specs=[vmem, vmem],
        out_specs=vmem,
        compiler_params=pltpu.CompilerParams(vmem_limit_bytes=2 * MIB),
        cost_estimate=pl.CostEstimate(flops=TURN, bytes_accessed=0, transcendentals=0),
        name=name,
    )(first, second)


def chunk(away, chips, own_ref, arrived_ref, lanes):
    spot = ring_order(chips).index(away % chips)
    if spot < EARLY:
        rows = own_ref.shape[0] // EARLY
    else:
        rows, spot = own_ref.shape[0] // (chips - EARLY), spot - EARLY
    at = slice(spot * rows, (spot + 1) * rows)
    return own_ref[at, lanes].astype(jnp.float32) + arrived_ref[at, lanes].astype(jnp.float32)


def sum_kernel(away, chips, lanes, own_ref, arrived_ref, out_ref):
    out_ref[...] = chunk(away, chips, own_ref, arrived_ref, lanes).astype(jnp.bfloat16)


def relay_kernel(away, chips, lanes, core, own_ref, arrived_ref, *refs):
    out_ref = refs[-1]
    value = chunk(away, chips, own_ref, arrived_ref, lanes) + refs[0][...].astype(jnp.float32)
    if len(refs) == 3:
        value = value + jnp.where(lax.axis_index("hid") % 2 == core, refs[1][...].astype(jnp.float32), 0.0)
    out_ref[...] = value.astype(jnp.bfloat16)


def last_kernel(chips, parts, own_ref, arrived_ref, *refs):
    sums, (keep_ref, give_ref, sum_ref) = refs[:-3], refs[-3:]
    part = keep_ref.shape[0]
    core = lax.axis_index("hid") % 2
    for at, lanes in enumerate(parts):
        sum_ref[:, lanes] = (
            chunk(0, chips, own_ref, arrived_ref, lanes)
            + sums[2 * at][...].astype(jnp.float32)
            + sums[2 * at + 1][...].astype(jnp.float32)
        )
    keep_ref[...] = sum_ref[pl.ds(pl.multiple_of(core * part, part), part), :]
    give_ref[...] = sum_ref[pl.ds(pl.multiple_of((1 - core) * part, part), part), :].astype(jnp.bfloat16)


def mix_kernel(tokens_ref, keep_ref, take_ref, out_ref):
    wide = keep_ref.shape[1]
    keep, take = keep_ref[...], take_ref[...].astype(jnp.float32)
    first = lax.axis_index("hid") % 2 == 0
    low, high = jnp.where(first, keep, take), jnp.where(first, take, keep)
    out_ref[:, :wide] = (tokens_ref[:, :wide].astype(jnp.float32) + low).astype(jnp.bfloat16)
    out_ref[:, wide:] = (tokens_ref[:, wide:].astype(jnp.float32) + high).astype(jnp.bfloat16)


def small(body, outs, operands, name, scratch=()):
    vmem = pl.BlockSpec(memory_space=pltpu.VMEM)
    return pl.pallas_call(
        body,
        out_shape=outs,
        in_specs=[vmem] * len(operands),
        out_specs=jax.tree.map(lambda _: vmem, outs),
        scratch_shapes=scratch,
        compiler_params=pltpu.CompilerParams(vmem_limit_bytes=4 * MIB),
        cost_estimate=pl.CostEstimate(flops=2 * operands[0].size, bytes_accessed=0, transcendentals=0),
        name=name,
    )(*operands)


def shards(count, tokens, norm_gain, gate_weight, up_weight, down_weight, clip_scale):
    chips = count // 2
    order = ring_of(chips)
    steps = chips // 2

    def hop(value, shift_even, shift_odd):
        pairs = []
        for at, c in enumerate(order):
            pairs.append((2 * c, 2 * order[(at + shift_even) % chips]))
            pairs.append((2 * c + 1, 2 * order[(at + shift_odd) % chips] + 1))
        return lax.ppermute(value, "hid", pairs)

    def right(value):
        return hop(value, 1, 1)

    def left(value):
        return hop(value, -1, -1)

    def cross(value, mask=1):
        return lax.ppermute(value, "hid", [(d, d ^ mask) for d in range(count)])

    normed = normalize(tokens, norm_gain)
    width = gate_weight.shape[1]
    pieces = width // max(BLOCK, width // 2)
    mine, shifts = [normed], [0]
    ahead = behind = normed
    for step in range(1, steps):
        if step == steps - 1:
            far = hop(both(pick_kernel, ahead, behind, "pick"), 2, -2)
        ahead, behind = right(ahead), left(behind)
        mine += [ahead, behind]
        shifts += [-step, step]
    mine.append(far)
    shifts.append(steps)
    parts = [block for own in mine for block in (own, cross(own))]

    *slices, joined = up_project(shifts, parts, gate_weight, up_weight, 0, pieces)
    for at in range(1, pieces):
        slices += up_project(shifts, [joined], gate_weight, up_weight, at, pieces)

    def turn(value, mask, *others):
        return both(functools.partial(turn_kernel, mask), value, once(cross(value, mask), *others), "turn")

    masks = [1 << bit for bit in range(count.bit_length() - 1)]
    for stage in range(len(masks)):
        for at in range(len(slices)):
            place = OFFSETS[at % 4] * len(masks) // 4 + stage
            slices[at] = turn(slices[at], masks[place % len(masks)])

    total = count * width
    limits = clip_scale.reshape(1, -1)
    theirs_early, theirs = down_project(slices, limits, down_weight, True, chips, total)
    arrived_early = cross(theirs_early)
    own_early, own = down_project(slices, limits, down_weight, False, chips, total)
    arrived = cross(once(theirs, own, arrived_early))
    rows, wide = own_early.shape[0] // EARLY, own_early.shape[1]
    part = jax.ShapeDtypeStruct((rows, wide // 2), jnp.bfloat16)
    parts = [slice(at * wide // 2, (at + 1) * wide // 2) for at in range(2)]

    sums = []
    for lanes in parts:
        first = [
            small(functools.partial(sum_kernel, away, chips, lanes), part, (own_early, arrived_early), "sum")
            for away in (steps - 1, 1 - steps, steps)
        ]
        sums.append([right(first[0]), left(first[1]), hop(first[2], 2, -2)])
    for away in range(steps - 2, 0, -1):
        for at, lanes in enumerate(parts):
            ahead, behind, *more = sums[at]
            ahead = small(
                functools.partial(relay_kernel, away, chips, lanes, 0), part, (own, arrived, ahead, *more), "relay"
            )
            behind = small(
                functools.partial(relay_kernel, -away, chips, lanes, 1), part, (own, arrived, behind, *more), "relay"
            )
            sums[at] = [right(ahead), left(behind)]
    half = jax.ShapeDtypeStruct((rows // 2, wide), jnp.bfloat16)
    kept = jax.ShapeDtypeStruct((rows // 2, wide), jnp.float32)
    keep, give = small(
        functools.partial(last_kernel, chips, parts),
        (kept, half),
        (own, arrived, *sums[0], *sums[1]),
        "last",
        [pltpu.VMEM((rows, wide), jnp.float32)],
    )
    mixed = jax.ShapeDtypeStruct(tokens.shape, tokens.dtype)
    return small(mix_kernel, mixed, (tokens, keep, cross(give)), "mix")


def solution(mesh):
    in_specs = (
        P(("groups", "hid"), None),
        P(),
        P(None, "hid"),
        P(None, "hid"),
        P("hid", None),
        P("hid"),
    )
    out_specs = P(("groups", "hid"), None)
    body = functools.partial(shards, mesh.shape["hid"])
    return jax.shard_map(body, mesh=mesh, in_specs=in_specs, out_specs=out_specs, check_vma=False)
```

```python
import functools

import jax
import jax.numpy as jnp
from jax import lax
from jax.experimental import pallas as pl
from jax.experimental.pallas import tpu as pltpu
from jax.sharding import PartitionSpec as P

BLOCK = 256
MIB = 1 << 20
OFFSETS = (3, 1, 0, 2)
TURN = 700_000_000
COST = 20_000_000_000


def hadamard(count):
    rows = lax.broadcasted_iota(jnp.int32, (count, count), 0)
    cols = lax.broadcasted_iota(jnp.int32, (count, count), 1)
    both = rows & cols
    parity = jnp.zeros((count, count), jnp.int32)
    for place in range(max(count.bit_length(), 1)):
        parity = parity + (both >> place & 1)
    return jnp.where(parity % 2 == 0, 1.0, -1.0).astype(jnp.bfloat16)


def normalize_kernel(rows_hbm, gain_hbm, out_ref, rows_ref, gain_ref, sems):
    copies = [
        pltpu.make_async_copy(rows_hbm, rows_ref, sems.at[0]),
        pltpu.make_async_copy(gain_hbm, gain_ref, sems.at[1]),
    ]
    for copy in copies:
        copy.start()
    for copy in copies:
        copy.wait()
    values = rows_ref[...].astype(jnp.float32)
    inverse = lax.rsqrt(jnp.mean(values * values, axis=-1, keepdims=True) + 1e-05)
    out_ref[...] = (values * inverse * gain_ref[...]).astype(jnp.bfloat16)


def in_hbm(value):
    return pltpu.with_memory_space_constraint(value, pltpu.HBM)


def normalize(rows_in, norm_gain):
    hbm = pl.BlockSpec(memory_space=pltpu.HBM)
    gain = norm_gain.reshape(1, -1)
    return pl.pallas_call(
        normalize_kernel,
        out_shape=jax.ShapeDtypeStruct(rows_in.shape, jnp.bfloat16),
        in_specs=[hbm, hbm],
        out_specs=pl.BlockSpec(memory_space=pltpu.VMEM),
        scratch_shapes=[
            pltpu.VMEM(rows_in.shape, rows_in.dtype),
            pltpu.VMEM(gain.shape, gain.dtype),
            pltpu.SemaphoreType.DMA((2,)),
        ],
        compiler_params=pltpu.CompilerParams(vmem_limit_bytes=4 * MIB),
        cost_estimate=pl.CostEstimate(flops=COST, bytes_accessed=4 * rows_in.size, transcendentals=0),
        name="normalize",
    )(in_hbm(rows_in), in_hbm(gain))


def ring_of(chips):
    return list(range(0, chips, 2)) + list(range(chips - 1, 0, -2))


def ring_place(chip, shift, chips):
    spot = jnp.where(chip % 2 == 0, chip // 2, chips - 1 - (chip - 1) // 2)
    spot = (spot + shift) % chips
    return jnp.where(spot < (chips + 1) // 2, 2 * spot, 2 * (chips - spot) - 1)


def once(value, *others):
    return lax.optimization_barrier((value, *others))[0]


def join_rows(parts, out_ref):
    own = parts[0].shape[0]
    for pair in range(len(parts) // 2):
        both = [parts[2 * pair + k][...].astype(jnp.float32) for k in range(2)]
        out_ref[2 * own * pair : 2 * own * (pair + 1), :] = jnp.concatenate(both, axis=0).astype(jnp.bfloat16)


def up_kernel(shifts, first, lanes_of, *refs):
    count = 2 * len(shifts)
    if first:
        gate_ref, up_ref, *outs, rows_ref, hidden_ref = refs[count:]
        join_rows(refs[:count], rows_ref)
    else:
        rows_ref, gate_ref, up_ref, *outs, hidden_ref = refs
    me = lax.axis_index("hid")
    chip, core = me // 2, me % 2
    own = rows_ref.shape[0] // count
    turn = hadamard(BLOCK)
    values = rows_ref[...]
    gate = jnp.dot(values, gate_ref[:, lanes_of], preferred_element_type=jnp.float32)
    up = jnp.dot(values, up_ref[:, lanes_of], preferred_element_type=jnp.float32)
    hidden = gate / (1.0 + jnp.exp(-gate)) * up
    high = hidden.astype(jnp.bfloat16)
    low = (hidden - high.astype(jnp.float32)).astype(jnp.bfloat16)
    for block in range(gate.shape[1] // BLOCK):
        lanes = slice(block * BLOCK, (block + 1) * BLOCK)
        turned = jnp.dot(high[:, lanes], turn, preferred_element_type=jnp.float32) + jnp.dot(
            low[:, lanes], turn, preferred_element_type=jnp.float32
        )
        for part in range(count):
            there = 2 * ring_place(chip, shifts[part // 2], count // 2)
            there = there + core if part % 2 == 0 else there + 1 - core
            spot = pl.multiple_of(there * own, own)
            hidden_ref[pl.ds(spot, own), lanes] = turned[part * own : (part + 1) * own]
    cols = outs[0].shape[1]
    for at, out_ref in enumerate(outs):
        out_ref[...] = hidden_ref[:, at * cols : (at + 1) * cols].astype(jnp.bfloat16)


def up_project(shifts, parts, gate_weight, up_weight, at, pieces):
    first = len(parts) > 1
    depth, width = gate_weight.shape
    width = width // pieces
    rows = sum(part.shape[0] for part in parts)
    vmem = pl.BlockSpec(memory_space=pltpu.VMEM)
    outs = [jax.ShapeDtypeStruct((rows, width // 2), jnp.bfloat16)] * 2
    if first:
        outs.append(jax.ShapeDtypeStruct((rows, depth), jnp.bfloat16))
    return pl.pallas_call(
        functools.partial(up_kernel, shifts, first, slice(at * width, (at + 1) * width)),
        out_shape=outs,
        in_specs=[vmem] * (len(parts) + 2),
        out_specs=[vmem] * len(outs),
        scratch_shapes=[pltpu.VMEM((rows, width), jnp.float32)],
        compiler_params=pltpu.CompilerParams(vmem_limit_bytes=4 * MIB + 2 * rows * depth),
        cost_estimate=pl.CostEstimate(flops=4 * rows * depth * width, bytes_accessed=0, transcendentals=rows * width),
        name="up_project",
    )(*parts, gate_weight, up_weight)


def ring_order(chips):
    steps = chips // 2
    early = [steps - 1, chips + 1 - steps, steps]
    return early + [away for away in range(chips) if away not in early]


EARLY = 3


def down_kernel(blocks, chips, scale, flip, clip_ref, weight_ref, *refs):
    slices, outs, (rows_ref, mixed_ref) = refs[:-4], refs[-4:-2], refs[-2:]
    cols = slices[0].shape[1]
    for at, slice_ref in enumerate(slices):
        rows_ref[:, at * cols : (at + 1) * cols] = slice_ref[...].astype(jnp.float32)
    parts = [rows_ref[:, b * BLOCK : (b + 1) * BLOCK] for b in range(blocks)]
    span = 1
    while span < blocks:
        parts = [
            parts[b] + parts[b ^ span] if b & span == 0 else parts[b ^ span] - parts[b] for b in range(blocks)
        ]
        span *= 2
    for b in range(blocks):
        lanes = slice(b * BLOCK, (b + 1) * BLOCK)
        limit = 127.0 * clip_ref[:, lanes]
        rows_ref[:, lanes] = jnp.clip(parts[b] * scale, -limit, limit)
    rows = rows_ref.shape[0]
    each = rows // chips
    me = lax.axis_index("hid")
    for chip in range(chips):
        spot = pl.multiple_of(ring_place(me // 2, ring_order(chips)[chip], chips) * each, each)
        mixed_ref[chip * each : (chip + 1) * each, :] = rows_ref[pl.ds(spot, each), :].astype(jnp.bfloat16)
    wide = weight_ref.shape[1] // 2
    side = 1 - me % 2 if flip else me % 2
    lanes = pl.ds(pl.multiple_of(side * wide, wide), wide)
    product = jnp.dot(mixed_ref[...], weight_ref[:, lanes], preferred_element_type=jnp.float32)
    first = 0
    for out_ref in outs:
        out_ref[...] = product[first : first + out_ref.shape[0]].astype(jnp.bfloat16)
        first += out_ref.shape[0]


def down_project(slices, clip_scale, weight, flip, chips, total):
    rows = slices[0].shape[0]
    width, depth = weight.shape[0], weight.shape[1] // 2
    vmem = pl.BlockSpec(memory_space=pltpu.VMEM)
    outs = [
        jax.ShapeDtypeStruct((count, depth), jnp.bfloat16) for count in (EARLY * (rows // chips), rows - EARLY * (rows // chips))
    ]
    return pl.pallas_call(
        functools.partial(down_kernel, width // BLOCK, chips, total**-0.5, flip),
        out_shape=outs,
        in_specs=[vmem] * (2 + len(slices)),
        out_specs=[vmem] * 2,
        scratch_shapes=[pltpu.VMEM((rows, width), jnp.float32), pltpu.VMEM((rows, width), jnp.bfloat16)],
        compiler_params=pltpu.CompilerParams(vmem_limit_bytes=8 * MIB),
        cost_estimate=pl.CostEstimate(flops=2 * rows * depth * width, bytes_accessed=0, transcendentals=0),
        name="down_project",
    )(clip_scale, weight, *slices)


def pick_kernel(even_ref, odd_ref, out_ref):
    core = lax.axis_index("hid") % 2

    @pl.when(core == 0)
    def _():
        out_ref[...] = even_ref[...]

    @pl.when(core != 0)
    def _():
        out_ref[...] = odd_ref[...]


def turn_kernel(mask, value_ref, other_ref, out_ref):
    sign = jnp.where(lax.axis_index("hid") & mask == 0, 1.0, -1.0).astype(jnp.float32)
    out_ref[...] = (other_ref[...].astype(jnp.float32) + sign * value_ref[...].astype(jnp.float32)).astype(jnp.bfloat16)


def both(body, first, second, name):
    vmem = pl.BlockSpec(memory_space=pltpu.VMEM)
    return pl.pallas_call(
        body,
        out_shape=jax.ShapeDtypeStruct(first.shape, first.dtype),
        in_specs=[vmem, vmem],
        out_specs=vmem,
        compiler_params=pltpu.CompilerParams(vmem_limit_bytes=2 * MIB),
        cost_estimate=pl.CostEstimate(flops=TURN, bytes_accessed=0, transcendentals=0),
        name=name,
    )(first, second)


def chunk(away, chips, own_ref, arrived_ref):
    spot = ring_order(chips).index(away % chips)
    if spot < EARLY:
        rows = own_ref.shape[0] // EARLY
    else:
        rows, spot = own_ref.shape[0] // (chips - EARLY), spot - EARLY
    at = slice(spot * rows, (spot + 1) * rows)
    return own_ref[at, :].astype(jnp.float32) + arrived_ref[at, :].astype(jnp.float32)


def sum_kernel(away, chips, own_ref, arrived_ref, out_ref):
    out_ref[...] = chunk(away, chips, own_ref, arrived_ref).astype(jnp.bfloat16)


def relay_kernel(away, chips, core, own_ref, arrived_ref, *refs):
    out_ref = refs[-1]
    value = chunk(away, chips, own_ref, arrived_ref) + refs[0][...].astype(jnp.float32)
    if len(refs) == 3:
        value = value + jnp.where(lax.axis_index("hid") % 2 == core, refs[1][...].astype(jnp.float32), 0.0)
    out_ref[...] = value.astype(jnp.bfloat16)


def deal_kernel(away, chips, own_ref, arrived_ref, *refs):
    *more, keep_ref, give_ref, sum_ref = refs
    part = keep_ref.shape[0]
    core = lax.axis_index("hid") % 2
    value = chunk(away, chips, own_ref, arrived_ref)
    for arrived_in in more:
        value = value + arrived_in[...].astype(jnp.float32)
    sum_ref[...] = value
    keep_ref[...] = sum_ref[pl.ds(pl.multiple_of(core * part, part), part), :].astype(jnp.bfloat16)
    give_ref[...] = sum_ref[pl.ds(pl.multiple_of((1 - core) * part, part), part), :].astype(jnp.bfloat16)


def mix_kernel(tokens_ref, *refs):
    *sums, out_ref = refs
    wide = out_ref.shape[1] // 2
    keep, take = [
        sums[3 * at][...].astype(jnp.float32)
        + sums[3 * at + 1][...].astype(jnp.float32)
        + sums[3 * at + 2][...].astype(jnp.float32)
        for at in range(2)
    ]
    first = lax.axis_index("hid") % 2 == 0
    low, high = jnp.where(first, keep, take), jnp.where(first, take, keep)
    out_ref[:, :wide] = (tokens_ref[:, :wide].astype(jnp.float32) + low).astype(jnp.bfloat16)
    out_ref[:, wide:] = (tokens_ref[:, wide:].astype(jnp.float32) + high).astype(jnp.bfloat16)


def small(body, outs, operands, name, scratch=()):
    vmem = pl.BlockSpec(memory_space=pltpu.VMEM)
    return pl.pallas_call(
        body,
        out_shape=outs,
        in_specs=[vmem] * len(operands),
        out_specs=jax.tree.map(lambda _: vmem, outs),
        scratch_shapes=scratch,
        compiler_params=pltpu.CompilerParams(vmem_limit_bytes=4 * MIB),
        cost_estimate=pl.CostEstimate(flops=2 * operands[0].size, bytes_accessed=0, transcendentals=0),
        name=name,
    )(*operands)


def shards(count, tokens, norm_gain, gate_weight, up_weight, down_weight, clip_scale):
    chips = count // 2
    order = ring_of(chips)
    steps = chips // 2

    def hop(value, shift_even, shift_odd):
        pairs = []
        for at, c in enumerate(order):
            pairs.append((2 * c, 2 * order[(at + shift_even) % chips]))
            pairs.append((2 * c + 1, 2 * order[(at + shift_odd) % chips] + 1))
        return lax.ppermute(value, "hid", pairs)

    def right(value):
        return hop(value, 1, 1)

    def left(value):
        return hop(value, -1, -1)

    def cross(value, mask=1):
        return lax.ppermute(value, "hid", [(d, d ^ mask) for d in range(count)])

    normed = normalize(tokens, norm_gain)
    width = gate_weight.shape[1]
    pieces = width // max(BLOCK, width // 2)
    mine, shifts = [normed], [0]
    ahead = behind = normed
    for step in range(1, steps):
        if step == steps - 1:
            far = hop(both(pick_kernel, ahead, behind, "pick"), 2, -2)
        ahead, behind = right(ahead), left(behind)
        mine += [ahead, behind]
        shifts += [-step, step]
    mine.append(far)
    shifts.append(steps)
    parts = [block for own in mine for block in (own, cross(own))]

    *slices, joined = up_project(shifts, parts, gate_weight, up_weight, 0, pieces)
    for at in range(1, pieces):
        slices += up_project(shifts, [joined], gate_weight, up_weight, at, pieces)

    def turn(value, mask, *others):
        return both(functools.partial(turn_kernel, mask), value, once(cross(value, mask), *others), "turn")

    masks = [1 << bit for bit in range(count.bit_length() - 1)]
    for stage in range(len(masks)):
        for at in range(len(slices)):
            place = OFFSETS[at % 4] * len(masks) // 4 + stage
            slices[at] = turn(slices[at], masks[place % len(masks)])

    total = count * width
    limits = clip_scale.reshape(1, -1)
    theirs_early, theirs = down_project(slices, limits, down_weight, True, chips, total)
    arrived_early = cross(theirs_early)
    own_early, own = down_project(slices, limits, down_weight, False, chips, total)
    arrived = cross(once(theirs, own, arrived_early))
    rows, wide = own_early.shape[0] // EARLY, own_early.shape[1]
    part = jax.ShapeDtypeStruct((rows, wide), jnp.bfloat16)

    first = [
        small(functools.partial(sum_kernel, away, chips), part, (own_early, arrived_early), "sum")
        for away in (steps - 1, 1 - steps, steps)
    ]
    ahead, behind, far = right(first[0]), left(first[1]), hop(first[2], 2, -2)
    half = jax.ShapeDtypeStruct((rows // 2, wide), jnp.bfloat16)

    def deal(away, *more):
        body = functools.partial(deal_kernel, away, chips)
        return small(body, (half, half), (own, arrived, *more), "deal", [pltpu.VMEM((rows, wide), jnp.float32)])

    def skip(value, shift):
        pairs = []
        for at, c in enumerate(order):
            there = order[(at + shift) % chips]
            pairs += [(2 * c, 2 * there + 1), (2 * c + 1, 2 * there)]
        return lax.ppermute(value, "hid", pairs)

    keep, give = deal(0)
    keeps, takes = [keep], [cross(give)]
    for away in range(steps - 2, 1, -1):
        more = (far,) if away == steps - 2 else ()
        ahead = small(
            functools.partial(relay_kernel, away, chips, 0), part, (own, arrived, ahead, *more), "relay"
        )
        behind = small(
            functools.partial(relay_kernel, -away, chips, 1), part, (own, arrived, behind, *more), "relay"
        )
        ahead, behind = right(ahead), left(behind)
    for shift, value in ((1, ahead), (-1, behind)):
        keep, give = deal(shift, value)
        keeps.append(hop(keep, shift, shift))
        takes.append(skip(give, shift))
    mixed = jax.ShapeDtypeStruct(tokens.shape, tokens.dtype)
    return small(mix_kernel, mixed, (tokens, *keeps, *takes), "mix")


def solution(mesh):
    in_specs = (
        P(("groups", "hid"), None),
        P(),
        P(None, "hid"),
        P(None, "hid"),
        P("hid", None),
        P("hid"),
    )
    out_specs = P(("groups", "hid"), None)
    body = functools.partial(shards, mesh.shape["hid"])
    return jax.shard_map(body, mesh=mesh, in_specs=in_specs, out_specs=out_specs, check_vma=False)
```

```python
import functools

import jax
import jax.numpy as jnp
from jax import lax
from jax.experimental import pallas as pl
from jax.experimental.pallas import tpu as pltpu
from jax.sharding import PartitionSpec as P

BLOCK = 256
MIB = 1 << 20
OFFSETS = (3, 1, 0, 2)
TURN = 700_000_000
COST = 20_000_000_000


def hadamard(count):
    rows = lax.broadcasted_iota(jnp.int32, (count, count), 0)
    cols = lax.broadcasted_iota(jnp.int32, (count, count), 1)
    both = rows & cols
    parity = jnp.zeros((count, count), jnp.int32)
    for place in range(max(count.bit_length(), 1)):
        parity = parity + (both >> place & 1)
    return jnp.where(parity % 2 == 0, 1.0, -1.0).astype(jnp.bfloat16)


def normalize_kernel(rows_hbm, gain_hbm, out_ref, rows_ref, gain_ref, sems):
    copies = [
        pltpu.make_async_copy(rows_hbm, rows_ref, sems.at[0]),
        pltpu.make_async_copy(gain_hbm, gain_ref, sems.at[1]),
    ]
    for copy in copies:
        copy.start()
    for copy in copies:
        copy.wait()
    values = rows_ref[...].astype(jnp.float32)
    inverse = lax.rsqrt(jnp.mean(values * values, axis=-1, keepdims=True) + 1e-05)
    out_ref[...] = (values * inverse * gain_ref[...]).astype(jnp.bfloat16)


def in_hbm(value):
    return pltpu.with_memory_space_constraint(value, pltpu.HBM)


def normalize(rows_in, norm_gain):
    hbm = pl.BlockSpec(memory_space=pltpu.HBM)
    gain = norm_gain.reshape(1, -1)
    return pl.pallas_call(
        normalize_kernel,
        out_shape=jax.ShapeDtypeStruct(rows_in.shape, jnp.bfloat16),
        in_specs=[hbm, hbm],
        out_specs=pl.BlockSpec(memory_space=pltpu.VMEM),
        scratch_shapes=[
            pltpu.VMEM(rows_in.shape, rows_in.dtype),
            pltpu.VMEM(gain.shape, gain.dtype),
            pltpu.SemaphoreType.DMA((2,)),
        ],
        compiler_params=pltpu.CompilerParams(vmem_limit_bytes=4 * MIB),
        cost_estimate=pl.CostEstimate(flops=COST, bytes_accessed=4 * rows_in.size, transcendentals=0),
        name="normalize",
    )(in_hbm(rows_in), in_hbm(gain))


def ring_of(chips):
    return list(range(0, chips, 2)) + list(range(chips - 1, 0, -2))


def ring_place(chip, shift, chips):
    spot = jnp.where(chip % 2 == 0, chip // 2, chips - 1 - (chip - 1) // 2)
    spot = (spot + shift) % chips
    return jnp.where(spot < (chips + 1) // 2, 2 * spot, 2 * (chips - spot) - 1)


def once(value, *others):
    return lax.optimization_barrier((value, *others))[0]


def join_rows(parts, out_ref):
    own = parts[0].shape[0]
    for pair in range(len(parts) // 2):
        both = [parts[2 * pair + k][...].astype(jnp.float32) for k in range(2)]
        out_ref[2 * own * pair : 2 * own * (pair + 1), :] = jnp.concatenate(both, axis=0).astype(jnp.bfloat16)


def up_kernel(shifts, pieces, *refs):
    count = 2 * len(shifts)
    gate_ref, up_ref, *outs, rows_ref, hidden_ref = refs[count:]
    join_rows(refs[:count], rows_ref)
    me = lax.axis_index("hid")
    chip, core = me // 2, me % 2
    own = rows_ref.shape[0] // count
    turn = hadamard(BLOCK)
    values = rows_ref[...]
    wide = gate_ref.shape[1] // pieces
    for piece in range(pieces):
        gate = jnp.dot(values, gate_ref[:, piece * wide : (piece + 1) * wide], preferred_element_type=jnp.float32)
        up = jnp.dot(values, up_ref[:, piece * wide : (piece + 1) * wide], preferred_element_type=jnp.float32)
        hidden = gate / (1.0 + jnp.exp(-gate)) * up
        high = hidden.astype(jnp.bfloat16)
        low = (hidden - high.astype(jnp.float32)).astype(jnp.bfloat16)
        for block in range(wide // BLOCK):
            lanes = slice(block * BLOCK, (block + 1) * BLOCK)
            outer = slice(piece * wide + block * BLOCK, piece * wide + (block + 1) * BLOCK)
            turned = jnp.dot(high[:, lanes], turn, preferred_element_type=jnp.float32) + jnp.dot(
                low[:, lanes], turn, preferred_element_type=jnp.float32
            )
            for part in range(count):
                there = 2 * ring_place(chip, shifts[part // 2], count // 2)
                there = there + core if part % 2 == 0 else there + 1 - core
                spot = pl.multiple_of(there * own, own)
                hidden_ref[pl.ds(spot, own), outer] = turned[part * own : (part + 1) * own]
    cols = outs[0].shape[1]
    for at, out_ref in enumerate(outs):
        out_ref[...] = hidden_ref[:, at * cols : (at + 1) * cols].astype(jnp.bfloat16)


def up_project(shifts, parts, gate_weight, up_weight, pieces):
    depth, width = gate_weight.shape
    rows = sum(part.shape[0] for part in parts)
    vmem = pl.BlockSpec(memory_space=pltpu.VMEM)
    outs = [jax.ShapeDtypeStruct((rows, width // (2 * pieces)), jnp.bfloat16)] * (2 * pieces)
    return pl.pallas_call(
        functools.partial(up_kernel, shifts, pieces),
        out_shape=outs,
        in_specs=[vmem] * (len(parts) + 2),
        out_specs=[vmem] * len(outs),
        scratch_shapes=[pltpu.VMEM((rows, depth), jnp.bfloat16), pltpu.VMEM((rows, width), jnp.float32)],
        compiler_params=pltpu.CompilerParams(vmem_limit_bytes=4 * MIB + 4 * rows * depth),
        cost_estimate=pl.CostEstimate(flops=4 * rows * depth * width, bytes_accessed=0, transcendentals=rows * width),
        name="up_project",
    )(*parts, gate_weight, up_weight)


def ring_order(chips):
    steps = chips // 2
    early = [steps - 1, chips + 1 - steps, steps]
    return early + [away for away in range(chips) if away not in early]


EARLY = 3


def down_kernel(blocks, chips, scale, flip, clip_ref, weight_ref, *refs):
    slices, outs, (rows_ref, mixed_ref) = refs[:-4], refs[-4:-2], refs[-2:]
    cols = slices[0].shape[1]
    for at, slice_ref in enumerate(slices):
        rows_ref[:, at * cols : (at + 1) * cols] = slice_ref[...].astype(jnp.float32)
    parts = [rows_ref[:, b * BLOCK : (b + 1) * BLOCK] for b in range(blocks)]
    span = 1
    while span < blocks:
        parts = [
            parts[b] + parts[b ^ span] if b & span == 0 else parts[b ^ span] - parts[b] for b in range(blocks)
        ]
        span *= 2
    for b in range(blocks):
        lanes = slice(b * BLOCK, (b + 1) * BLOCK)
        limit = 127.0 * clip_ref[:, lanes]
        rows_ref[:, lanes] = jnp.clip(parts[b] * scale, -limit, limit)
    rows = rows_ref.shape[0]
    each = rows // chips
    me = lax.axis_index("hid")
    for chip in range(chips):
        spot = pl.multiple_of(ring_place(me // 2, ring_order(chips)[chip], chips) * each, each)
        mixed_ref[chip * each : (chip + 1) * each, :] = rows_ref[pl.ds(spot, each), :].astype(jnp.bfloat16)
    wide = weight_ref.shape[1] // 2
    side = 1 - me % 2 if flip else me % 2
    lanes = pl.ds(pl.multiple_of(side * wide, wide), wide)
    product = jnp.dot(mixed_ref[...], weight_ref[:, lanes], preferred_element_type=jnp.float32)
    first = 0
    for out_ref in outs:
        out_ref[...] = product[first : first + out_ref.shape[0]].astype(jnp.bfloat16)
        first += out_ref.shape[0]


def down_project(slices, clip_scale, weight, flip, chips, total):
    rows = slices[0].shape[0]
    width, depth = weight.shape[0], weight.shape[1] // 2
    vmem = pl.BlockSpec(memory_space=pltpu.VMEM)
    outs = [
        jax.ShapeDtypeStruct((count, depth), jnp.bfloat16) for count in (EARLY * (rows // chips), rows - EARLY * (rows // chips))
    ]
    return pl.pallas_call(
        functools.partial(down_kernel, width // BLOCK, chips, total**-0.5, flip),
        out_shape=outs,
        in_specs=[vmem] * (2 + len(slices)),
        out_specs=[vmem] * 2,
        scratch_shapes=[pltpu.VMEM((rows, width), jnp.float32), pltpu.VMEM((rows, width), jnp.bfloat16)],
        compiler_params=pltpu.CompilerParams(vmem_limit_bytes=8 * MIB),
        cost_estimate=pl.CostEstimate(flops=2 * rows * depth * width, bytes_accessed=0, transcendentals=0),
        name="down_project",
    )(clip_scale, weight, *slices)


def pick_kernel(even_ref, odd_ref, out_ref):
    core = lax.axis_index("hid") % 2

    @pl.when(core == 0)
    def _():
        out_ref[...] = even_ref[...]

    @pl.when(core != 0)
    def _():
        out_ref[...] = odd_ref[...]


def turn_kernel(mask, value_ref, other_ref, out_ref):
    sign = jnp.where(lax.axis_index("hid") & mask == 0, 1.0, -1.0).astype(jnp.float32)
    out_ref[...] = (other_ref[...].astype(jnp.float32) + sign * value_ref[...].astype(jnp.float32)).astype(jnp.bfloat16)


def both(body, first, second, name):
    vmem = pl.BlockSpec(memory_space=pltpu.VMEM)
    return pl.pallas_call(
        body,
        out_shape=jax.ShapeDtypeStruct(first.shape, first.dtype),
        in_specs=[vmem, vmem],
        out_specs=vmem,
        compiler_params=pltpu.CompilerParams(vmem_limit_bytes=2 * MIB),
        cost_estimate=pl.CostEstimate(flops=TURN, bytes_accessed=0, transcendentals=0),
        name=name,
    )(first, second)


def chunk(away, chips, own_ref, arrived_ref):
    spot = ring_order(chips).index(away % chips)
    if spot < EARLY:
        rows = own_ref.shape[0] // EARLY
    else:
        rows, spot = own_ref.shape[0] // (chips - EARLY), spot - EARLY
    at = slice(spot * rows, (spot + 1) * rows)
    return own_ref[at, :].astype(jnp.float32) + arrived_ref[at, :].astype(jnp.float32)


def sum_kernel(away, chips, own_ref, arrived_ref, out_ref):
    out_ref[...] = chunk(away, chips, own_ref, arrived_ref).astype(jnp.bfloat16)


def relay_kernel(away, chips, core, own_ref, arrived_ref, *refs):
    out_ref = refs[-1]
    value = chunk(away, chips, own_ref, arrived_ref) + refs[0][...].astype(jnp.float32)
    if len(refs) == 3:
        value = value + jnp.where(lax.axis_index("hid") % 2 == core, refs[1][...].astype(jnp.float32), 0.0)
    out_ref[...] = value.astype(jnp.bfloat16)


def deal_kernel(away, chips, own_ref, arrived_ref, *refs):
    *more, keep_ref, give_ref, sum_ref = refs
    part = keep_ref.shape[0]
    core = lax.axis_index("hid") % 2
    value = chunk(away, chips, own_ref, arrived_ref)
    for arrived_in in more:
        value = value + arrived_in[...].astype(jnp.float32)
    sum_ref[...] = value
    keep_ref[...] = sum_ref[pl.ds(pl.multiple_of(core * part, part), part), :].astype(jnp.bfloat16)
    give_ref[...] = sum_ref[pl.ds(pl.multiple_of((1 - core) * part, part), part), :].astype(jnp.bfloat16)


def mix_kernel(tokens_ref, *refs):
    *sums, out_ref = refs
    wide = out_ref.shape[1] // 2
    keep, take = [
        sums[3 * at][...].astype(jnp.float32)
        + sums[3 * at + 1][...].astype(jnp.float32)
        + sums[3 * at + 2][...].astype(jnp.float32)
        for at in range(2)
    ]
    first = lax.axis_index("hid") % 2 == 0
    low, high = jnp.where(first, keep, take), jnp.where(first, take, keep)
    out_ref[:, :wide] = (tokens_ref[:, :wide].astype(jnp.float32) + low).astype(jnp.bfloat16)
    out_ref[:, wide:] = (tokens_ref[:, wide:].astype(jnp.float32) + high).astype(jnp.bfloat16)


def small(body, outs, operands, name, scratch=()):
    vmem = pl.BlockSpec(memory_space=pltpu.VMEM)
    return pl.pallas_call(
        body,
        out_shape=outs,
        in_specs=[vmem] * len(operands),
        out_specs=jax.tree.map(lambda _: vmem, outs),
        scratch_shapes=scratch,
        compiler_params=pltpu.CompilerParams(vmem_limit_bytes=4 * MIB),
        cost_estimate=pl.CostEstimate(flops=2 * operands[0].size, bytes_accessed=0, transcendentals=0),
        name=name,
    )(*operands)


def shards(count, tokens, norm_gain, gate_weight, up_weight, down_weight, clip_scale):
    chips = count // 2
    order = ring_of(chips)
    steps = chips // 2

    def hop(value, shift_even, shift_odd):
        pairs = []
        for at, c in enumerate(order):
            pairs.append((2 * c, 2 * order[(at + shift_even) % chips]))
            pairs.append((2 * c + 1, 2 * order[(at + shift_odd) % chips] + 1))
        return lax.ppermute(value, "hid", pairs)

    def right(value):
        return hop(value, 1, 1)

    def left(value):
        return hop(value, -1, -1)

    def cross(value, mask=1):
        return lax.ppermute(value, "hid", [(d, d ^ mask) for d in range(count)])

    normed = normalize(tokens, norm_gain)
    width = gate_weight.shape[1]
    pieces = width // max(BLOCK, width // 2)
    mine, shifts = [normed], [0]
    ahead = behind = normed
    for step in range(1, steps):
        if step == steps - 1:
            far = hop(both(pick_kernel, ahead, behind, "pick"), 2, -2)
        ahead, behind = right(ahead), left(behind)
        mine += [ahead, behind]
        shifts += [-step, step]
    mine.append(far)
    shifts.append(steps)
    parts = [block for own in mine for block in (own, cross(own))]

    slices = [*up_project(shifts, parts, gate_weight, up_weight, pieces)]

    def turn(value, mask, *others):
        return both(functools.partial(turn_kernel, mask), value, once(cross(value, mask), *others), "turn")

    masks = [1 << bit for bit in range(count.bit_length() - 1)]
    for stage in range(len(masks)):
        for at in range(len(slices)):
            place = OFFSETS[at % 4] * len(masks) // 4 + stage
            slices[at] = turn(slices[at], masks[place % len(masks)])

    total = count * width
    limits = clip_scale.reshape(1, -1)
    theirs_early, theirs = down_project(slices, limits, down_weight, True, chips, total)
    arrived_early = cross(theirs_early)
    own_early, own = down_project(slices, limits, down_weight, False, chips, total)
    arrived = cross(once(theirs, own, arrived_early))
    rows, wide = own_early.shape[0] // EARLY, own_early.shape[1]
    part = jax.ShapeDtypeStruct((rows, wide), jnp.bfloat16)

    first = [
        small(functools.partial(sum_kernel, away, chips), part, (own_early, arrived_early), "sum")
        for away in (steps - 1, 1 - steps, steps)
    ]
    ahead, behind, far = right(first[0]), left(first[1]), hop(first[2], 2, -2)
    half = jax.ShapeDtypeStruct((rows // 2, wide), jnp.bfloat16)

    def deal(away, *more):
        body = functools.partial(deal_kernel, away, chips)
        return small(body, (half, half), (own, arrived, *more), "deal", [pltpu.VMEM((rows, wide), jnp.float32)])

    def skip(value, shift):
        pairs = []
        for at, c in enumerate(order):
            there = order[(at + shift) % chips]
            pairs += [(2 * c, 2 * there + 1), (2 * c + 1, 2 * there)]
        return lax.ppermute(value, "hid", pairs)

    keep, give = deal(0)
    keeps, takes = [keep], [cross(give)]
    for away in range(steps - 2, 1, -1):
        more = (far,) if away == steps - 2 else ()
        ahead = small(
            functools.partial(relay_kernel, away, chips, 0), part, (own, arrived, ahead, *more), "relay"
        )
        behind = small(
            functools.partial(relay_kernel, -away, chips, 1), part, (own, arrived, behind, *more), "relay"
        )
        ahead, behind = right(ahead), left(behind)
    for shift, value in ((1, ahead), (-1, behind)):
        keep, give = deal(shift, value)
        keeps.append(hop(keep, shift, shift))
        takes.append(skip(give, shift))
    mixed = jax.ShapeDtypeStruct(tokens.shape, tokens.dtype)
    return small(mix_kernel, mixed, (tokens, *keeps, *takes), "mix")


def solution(mesh):
    in_specs = (
        P(("groups", "hid"), None),
        P(),
        P(None, "hid"),
        P(None, "hid"),
        P("hid", None),
        P("hid"),
    )
    out_specs = P(("groups", "hid"), None)
    body = functools.partial(shards, mesh.shape["hid"])
    return jax.shard_map(body, mesh=mesh, in_specs=in_specs, out_specs=out_specs, check_vma=False)
```
